32 devices in a mesh: dp: 4 (over x, core), sp: 8 (over z, y).
Axes of the slice: x: 2, y: 2, z: 4, core: 2. Of those that a mesh axis runs over, the one named last changes fastest.
Arguments:
- ssm_input: bfloat16 [4, 1024, 8192], P('dp', 'sp'), may hold values from -6 to 6
- b_input: bfloat16 [4, 1024, 1024], P('dp', 'sp'), may hold values from -6 to 6
- c_input: bfloat16 [4, 1024, 1024], P('dp', 'sp'), may hold values from -6 to 6
- dt_input: bfloat16 [4, 1024, 128], P('dp', 'sp'), may hold values from -4 to 4
- conv_weight: float32 [4, 10240], replicated, may hold values from -3 to 3
- conv_bias: float32 [10240], replicated, may hold values from -3 to 3
- a_log: float32 [128], replicated, may hold values from -12 to 2
- dt_bias: float32 [128], replicated, may hold values from -5 to -3
- skip_gain: float32 [128], replicated, may hold values from 0.5 to 1.5
- grad_out: bfloat16 [4, 1024, 8192], P('dp', 'sp'), may hold values from -6 to 6
Outputs:
- y_out: bfloat16 [4, 1024, 8192], P('dp', 'sp')
- grad_x: bfloat16 [4, 1024, 8192], P('dp', 'sp')
- grad_b: bfloat16 [4, 1024, 1024], P('dp', 'sp')
- grad_c: bfloat16 [4, 1024, 1024], P('dp', 'sp')
- grad_dt: bfloat16 [4, 1024, 128], P('dp', 'sp')
- grad_conv_w: float32 [4, 10240], replicated
- grad_conv_b: float32 [10240], replicated
- grad_heads: float32 [3, 128], P(None, 'sp')
The draws below stay inside these ranges and needn't reach their ends.
All inputs are finite; a program needn't handle non-finite values.
Results may differ from the reference program's by a relative error of at most 0.015.
Values may be sent and summed in bfloat16 or wider, within the bound.
No kernel may reach another device: no remote copies, remote signals or barrier semaphores. Data moves between devices by JAX's collectives and lax.ppermute only.
A program may use at most 192 MiB of HBM per device.

```python
import jax
import jax.numpy as jnp
from jax import lax

H = 128
P_SIZE = 64
N = 256
G = 4
K = 4
Q = 128
LEN = 1024
SEQS = 4
CH = 10240
N_SP = 8


def draw_a_log(key, part):
    pick_key, fast_key, slow_key = jax.random.split(key, 3)
    fast_share = 0.5
    chosen = jax.random.uniform(pick_key, (H,), jnp.float32) < fast_share
    fast_rate = 1.0 / jax.random.uniform(fast_key, (H,), jnp.float32, minval=30.0, maxval=50.0)
    slow_rate = jax.random.uniform(slow_key, (H,), jnp.float32, minval=0.3, maxval=2.0) / LEN
    chosen_rate = jnp.where(chosen, fast_rate, slow_rate)
    return jnp.log(chosen_rate / 0.02).astype(jnp.float32)


def steps_of(key, extent, cuts, low, top_value):
    def one(axis_at, blocks):
        steps = jax.random.uniform(jax.random.fold_in(jax.random.fold_in(key, 6), axis_at), (blocks,), jnp.float32, low / len(cuts), top_value / len(cuts))
        return jnp.repeat(jnp.exp(steps), extent[axis_at] // blocks).reshape((-1,) + (1,) * (len(extent) - axis_at - 1))

    gain = one(*cuts[0])
    for cut in cuts[1:]:
        gain = gain * one(*cut)
    return gain


def normal_values(own_key, dims, spread, most, cuts=(), kind=jnp.bfloat16):
    gain = steps_of(own_key, dims, cuts, -0.22, 0.18) if cuts else 1.0
    result = jax.random.normal(own_key, dims, jnp.float32) * spread * gain
    return jnp.minimum(jnp.maximum(result, -most), most).astype(kind)


def setup_inputs(seed: int = 0) -> dict:
    keys = jax.random.split(jax.random.key(seed), 11)
    ssm_input = normal_values(keys[0], (SEQS, LEN, H * P_SIZE), 1.0, 6.0, ((0, 4), (1, 8)))
    b_input = normal_values(keys[1], (SEQS, LEN, G * N), 1.0, 6.0, ((0, 4), (1, 8)))
    c_input = normal_values(keys[2], (SEQS, LEN, G * N), 1.0, 6.0, ((0, 4), (1, 8)))
    dt_input = normal_values(keys[3], (SEQS, LEN, H), 1.0, 4.0, ((0, 4), (1, 8)))
    conv_weight = normal_values(keys[4], (K, CH), K ** -0.5, 3.0, (), jnp.float32)
    conv_bias = normal_values(keys[5], (CH,), 0.5, 3.0, (), jnp.float32)
    a_log = draw_a_log(jax.random.fold_in(keys[10], 71), 0)
    dt_bias = jnp.clip(jax.random.uniform(keys[7], (H,), jnp.float32, -5.0, -3.0), -5.0, -3.0)
    skip_gain = jnp.clip(jax.random.uniform(keys[8], (H,), jnp.float32, 0.5, 1.5), 0.5, 1.5)
    grad_out = normal_values(keys[9], (SEQS, LEN, H * P_SIZE), 1.0, 6.0, ((0, 4), (1, 8)))
    return dict(ssm_input=ssm_input, b_input=b_input, c_input=c_input, dt_input=dt_input, conv_weight=conv_weight, conv_bias=conv_bias, a_log=a_log, dt_bias=dt_bias, skip_gain=skip_gain, grad_out=grad_out)


def conv_silu(padded, kernel_cols, offset_cols):
    span = kernel_cols.shape[0]
    count_rows = padded.shape[0] - span + 1
    summed = offset_cols[None, :] + jnp.zeros((count_rows, offset_cols.shape[0]), jnp.float32)
    for tap_index in range(span):
        summed = summed + kernel_cols[tap_index][None, :] * padded[tap_index:tap_index + count_rows]
    return jax.nn.silu(summed)

def conv_all(x_full, b_full, c_full, kernel, offset):
    x_width = x_full.shape[1]
    b_width = b_full.shape[1]
    x_out = conv_silu(x_full, kernel[:, :x_width], offset[:x_width])
    b_out = conv_silu(b_full, kernel[:, x_width:x_width + b_width], offset[x_width:x_width + b_width])
    c_out = conv_silu(c_full, kernel[:, x_width + b_width:], offset[x_width + b_width:])
    return (x_out, b_out, c_out)

def product(form, left, right):
    return jnp.einsum(form, left.astype(jnp.float32), right.astype(jnp.float32), precision=lax.Precision.HIGHEST)

def ssd_block(x_heads, dt_heads, b_group, c_group, alog_heads, dtbias_heads, skip_heads):
    length = x_heads.shape[0]
    nheads = dt_heads.shape[1]
    states = b_group.shape[1]
    hwidth = x_heads.shape[1] // nheads
    blocks = length // Q
    step_size = jax.nn.softplus(dt_heads.astype(jnp.float32) + dtbias_heads[None, :])
    steps_t = jnp.transpose(step_size).reshape(nheads, blocks, Q)
    log_t = steps_t * (-jnp.exp(alog_heads))[:, None, None]
    running = jnp.cumsum(log_t, axis=2)
    x_blocks = x_heads.reshape(blocks, Q, nheads * hwidth)
    b_blocks = b_group.reshape(blocks, Q, states)
    c_blocks = c_group.reshape(blocks, Q, states)
    scores = product('cqn,ckn->cqk', c_blocks, b_blocks)
    causal = (jnp.arange(Q)[:, None] >= jnp.arange(Q)[None, :])[None, None, :, :]
    spread_log = jnp.where(causal, running[:, :, :, None] - running[:, :, None, :], -1e+30)
    mixing = (scores[None] * jnp.exp(spread_log) * steps_t[:, :, None, :]).astype(jnp.bfloat16)
    within = product('hcqk,ckhp->cqhp', mixing, x_blocks.reshape(blocks, Q, nheads, hwidth))
    to_end = jnp.exp(running[:, :, -1:] - running)
    factor = jnp.transpose(steps_t * to_end, (1, 2, 0))
    x_wide = x_blocks.astype(jnp.float32).reshape(blocks, Q, nheads, hwidth)
    weighted = (x_wide * factor[:, :, :, None]).astype(jnp.bfloat16).reshape(blocks, Q, nheads * hwidth)
    block_states = product('ckn,ckm->cnm', b_blocks, weighted)
    totals = running[:, :, -1]
    before = jnp.cumsum(totals, axis=1) - totals
    earlier = (jnp.arange(blocks)[:, None] > jnp.arange(blocks)[None, :])[None, :, :]
    gap_log = jnp.where(earlier, before[:, :, None] - before[:, None, :] - totals[:, None, :], -1e+30)
    carried = jnp.exp(gap_log)
    entering = jnp.einsum('hcd,dnhp->cnhp', carried, block_states.reshape(blocks, states, nheads, hwidth), precision=lax.Precision.HIGHEST)
    entering_low = entering.reshape(blocks, states, nheads * hwidth).astype(jnp.bfloat16)
    across = product('cqn,cnm->cqm', c_blocks, entering_low).reshape(blocks, Q, nheads, hwidth)
    across = across * jnp.transpose(jnp.exp(running), (1, 2, 0))[:, :, :, None]
    skipped = skip_heads[None, None, :, None] * x_wide
    return (within + across + skipped).reshape(length, nheads * hwidth)

def reference(ssm_input, b_input, c_input, dt_input, conv_weight, conv_bias, a_log, dt_bias, skip_gain, grad_out):
    per_dev = H // N_SP
    group_devs = N_SP // G
    length = ssm_input.shape[1]
    outputs = []
    kernel_total = jnp.zeros(conv_weight.shape, jnp.float32)
    offset_total = jnp.zeros(conv_bias.shape, jnp.float32)
    head_total = jnp.zeros((3, H), jnp.float32)
    for seq_index in range(SEQS):
        x_full = jnp.concatenate([jnp.zeros((K - 1, H * P_SIZE), jnp.float32), ssm_input[seq_index].astype(jnp.float32)], 0)
        b_full = jnp.concatenate([jnp.zeros((K - 1, G * N), jnp.float32), b_input[seq_index].astype(jnp.float32)], 0)
        c_full = jnp.concatenate([jnp.zeros((K - 1, G * N), jnp.float32), c_input[seq_index].astype(jnp.float32)], 0)
        conv_outs, conv_back = jax.vjp(conv_all, x_full, b_full, c_full, conv_weight, conv_bias)
        x_conv = conv_outs[0].astype(jnp.bfloat16)
        b_conv = conv_outs[1].astype(jnp.bfloat16)
        c_conv = conv_outs[2].astype(jnp.bfloat16)
        dt_rows = dt_input[seq_index]
        dy_rows = grad_out[seq_index]

        def one_set(set_index):
            first_col = (set_index * per_dev * P_SIZE).astype(jnp.int32)
            first_head = (set_index * per_dev).astype(jnp.int32)
            group_col = (set_index // group_devs * N).astype(jnp.int32)
            x_heads = lax.dynamic_slice_in_dim(x_conv, first_col, per_dev * P_SIZE, 1)
            dy_heads = lax.dynamic_slice_in_dim(dy_rows, first_col, per_dev * P_SIZE, 1)
            dt_heads = lax.dynamic_slice_in_dim(dt_rows, first_head, per_dev, 1)
            b_group = lax.dynamic_slice_in_dim(b_conv, group_col, N, 1)
            c_group = lax.dynamic_slice_in_dim(c_conv, group_col, N, 1)
            alog_heads = lax.dynamic_slice_in_dim(a_log, first_head, per_dev)
            dtbias_heads = lax.dynamic_slice_in_dim(dt_bias, first_head, per_dev)
            skip_heads = lax.dynamic_slice_in_dim(skip_gain, first_head, per_dev)
            y_heads, ssd_back = jax.vjp(ssd_block, x_heads, dt_heads, b_group, c_group, alog_heads, dtbias_heads, skip_heads)
            grads = ssd_back(dy_heads.astype(jnp.float32))
            return (y_heads.astype(jnp.bfloat16),) + tuple(grads)
        results = lax.map(one_set, jnp.arange(N_SP, dtype=jnp.int32))
        y_rows = jnp.transpose(results[0], (1, 0, 2)).reshape(length, H * P_SIZE)
        gx_rows = jnp.transpose(results[1], (1, 0, 2)).reshape(length, H * P_SIZE)
        gdt_rows = jnp.transpose(results[2], (1, 0, 2)).reshape(length, H)
        gb_sum = results[3].astype(jnp.float32).reshape(G, group_devs, length, N).sum(axis=1)
        gc_sum = results[4].astype(jnp.float32).reshape(G, group_devs, length, N).sum(axis=1)
        gb_sum = jnp.transpose(gb_sum, (1, 0, 2)).reshape(length, G * N)
        gc_sum = jnp.transpose(gc_sum, (1, 0, 2)).reshape(length, G * N)
        head_terms = jnp.stack([results[5].reshape(H), results[6].reshape(H), results[7].reshape(H)])
        d_xfull, d_bfull, d_cfull, d_kernel, d_offset = conv_back((gx_rows.astype(jnp.float32), gb_sum, gc_sum))
        kernel_total = kernel_total + d_kernel
        offset_total = offset_total + d_offset
        head_total = head_total + head_terms
        outputs.append((y_rows, d_xfull[K - 1:].astype(jnp.bfloat16), d_bfull[K - 1:].astype(jnp.bfloat16), d_cfull[K - 1:].astype(jnp.bfloat16), gdt_rows))
    y_out = jnp.stack([entry[0] for entry in outputs])
    grad_x = jnp.stack([entry[1] for entry in outputs])
    grad_b = jnp.stack([entry[2] for entry in outputs])
    grad_c = jnp.stack([entry[3] for entry in outputs])
    grad_dt = jnp.stack([entry[4] for entry in outputs])
    return (y_out, grad_x, grad_b, grad_c, grad_dt, kernel_total, offset_total, head_total)
```

```python
import functools

import jax
import jax.numpy as jnp
from jax import lax
from jax.experimental import pallas as pl
from jax.experimental.pallas import tpu as pltpu
from jax.sharding import PartitionSpec as P

N = 256
Q = 128
HEAD = 64
SUB = 256
LOG2E = 1.4426950408889634
F32 = jnp.float32
BF16 = jnp.bfloat16
NEG = -1e30


def params():
    return pltpu.CompilerParams(vmem_limit_bytes=40 * 1024 * 1024)


def cost(micros, nbytes):
    return pl.CostEstimate(flops=int(micros * 1e9), bytes_accessed=nbytes, transcendentals=0)


def dot(a, b):
    return jnp.dot(a, b, preferred_element_type=F32)


def dot_tb(a, b):
    return lax.dot_general(a, b, (((1,), (1,)), ((), ())), preferred_element_type=F32)


def dot_ta(a, b):
    return lax.dot_general(a, b, (((0,), (0,)), ((), ())), preferred_element_type=F32)


def halves(v):
    hi = v.astype(BF16)
    return hi, (v - hi.astype(F32)).astype(BF16)


def split_dot(v, m):
    hi, lo = halves(v)
    return dot(hi, m) + dot(lo, m)


def exact_dot(m, v):
    hi = v.astype(BF16)
    rest = v - hi.astype(F32)
    mid = rest.astype(BF16)
    low = (rest - mid.astype(F32)).astype(BF16)
    return dot(m, hi) + dot(m, mid) + dot(m, low)


def triangle(lower):
    row = lax.broadcasted_iota(jnp.int32, (Q, Q), 0)
    col = lax.broadcasted_iota(jnp.int32, (Q, Q), 1)
    return row >= col if lower else row <= col


def in_order(y, own, rec, dst, first=0):
    rows = own.shape[0]

    @pl.when(y == 0)
    def _():
        dst[first : first + rows] = own.astype(dst.dtype)
        dst[first + rows : first + 2 * rows] = rec.astype(dst.dtype)

    @pl.when(y != 0)
    def _():
        dst[first : first + rows] = rec.astype(dst.dtype)
        dst[first + rows : first + 2 * rows] = own.astype(dst.dtype)


def conv_sum(xs, w, rows):
    total = w[4:5]
    for k in range(4):
        total = total + w[k : k + 1] * xs[5 + k : 5 + k + rows]
    return total


def conv_back(g, s, xs, gs, w, rows):
    sig = 1.0 / (1.0 + jnp.exp(-s))
    ds = g * (sig * (1.0 + s * (1.0 - sig)))
    gs[0:rows] = ds
    gs[rows : rows + 8] = jnp.zeros((8, ds.shape[1]), F32)
    dx = w[3:4] * ds
    for k in range(3):
        dx = dx + w[k : k + 1] * gs[3 - k : 3 - k + rows]
    dw = [jnp.sum(ds * xs[5 + k : 5 + k + rows], axis=0, keepdims=True) for k in range(4)]
    dw.append(jnp.sum(ds, axis=0, keepdims=True))
    dw.append(jnp.zeros((3, ds.shape[1]), F32))
    return dx, jnp.concatenate(dw, axis=0), ds[0:8]


def setup_kernel(
    yv, b_own, c_own, dt_own, rec, halo, w, par, exp2,
    bc_ref, cc_ref, fe_ref, rows_ref, cols_ref, rowt_ref, st_ref, xs, dts, xs2,
):
    y = yv[0]
    width = b_own.shape[1]
    heads = par.shape[1]
    for own, at, out in ((b_own, 0, bc_ref), (c_own, width, cc_ref)):
        xs[0:8] = halo[:, at : at + width]
        in_order(y, own[...], rec[:, at : at + width], xs, 8)
        s = conv_sum(xs, w[:, at : at + width], 2 * Q)
        out[...] = (s / (1.0 + jnp.exp(-s))).astype(BF16)

    @pl.when(y == 0)
    def _():
        dts[0:Q] = dt_own[:, 0:heads].astype(F32)
        dts[Q : 2 * Q] = rec[:, 2 * width : 2 * width + heads].astype(F32)

    @pl.when(y != 0)
    def _():
        dts[0:Q] = rec[:, 2 * width + heads : 2 * width + 2 * heads].astype(F32)
        dts[Q : 2 * Q] = dt_own[:, heads : 2 * heads].astype(F32)

    step = jnp.log1p(jnp.exp(dts[...] + par[1:2]))
    logs = -step * jnp.exp(par[0:1])
    tri = jnp.where(triangle(True), 1.0, 0.0).astype(BF16)
    run0 = exact_dot(tri, logs[0:Q])
    run1 = exact_dot(tri, logs[Q:])
    tot0, tot1 = run0[Q - 1 : Q], run1[Q - 1 : Q]
    run = jnp.concatenate([run0, run1], axis=0)
    to_end = jnp.concatenate([jnp.exp(tot0 - run0), jnp.exp(tot1 - run1)], axis=0)
    hi, lo = halves(step * to_end)
    fe_ref[0] = jnp.concatenate([hi, lo], axis=1)
    hi, lo = halves(jnp.exp(run))
    fe_ref[1] = jnp.concatenate([hi, lo], axis=1)
    st_ref[...] = step
    small = jnp.concatenate(
        [jnp.exp(tot0), jnp.exp(tot1), jnp.exp(tot0 + tot1), par[2:3], jnp.zeros((4, heads), F32)],
        axis=0,
    )
    hi, lo = halves(small)
    rows_ref[...] = dot(jnp.concatenate([hi, lo], axis=1), exp2[...])
    r2 = run * LOG2E
    q2 = (run - jnp.log(step)) * LOG2E
    both = jnp.concatenate([r2, q2], axis=1)
    xs2[...] = jnp.transpose(both)
    for j in range(heads // 4):
        cols_ref[j] = jnp.concatenate([r2[:, 4 * j : 4 * j + 4], q2[:, 4 * j : 4 * j + 4]], axis=1)
        rowt_ref[j] = jnp.concatenate(
            [xs2[4 * j : 4 * j + 4], xs2[heads + 4 * j : heads + 4 * j + 4]], axis=0
        )


def state_kernel(
    yv, x_own, dy_own, rec, halo, w, bc, cc, fe, exp2, rows, xc_ref, dyo_ref, t_ref, u_ref, xs
):
    y = yv[0]
    xs[0:8] = halo[...]
    in_order(y, x_own[...], rec[0], xs, 8)
    in_order(y, dy_own[...], rec[1], dyo_ref)
    s = conv_sum(xs, w, 2 * Q)
    xc = (s / (1.0 + jnp.exp(-s))).astype(BF16)
    xc_ref[...] = xc
    wt = (xc.astype(F32) * dot(fe[0], exp2[...])).astype(BF16)
    dyr = (dyo_ref[...].astype(F32) * dot(fe[1], exp2[...])).astype(BF16)
    t_ref[...] = (rows[1:2] * dot_ta(bc[0:Q], wt[0:Q]) + dot_ta(bc[Q:], wt[Q:])).astype(BF16)
    u_ref[...] = (dot_ta(cc[0:Q], dyr[0:Q]) + rows[0:1] * dot_ta(cc[Q:], dyr[Q:])).astype(BF16)


def within_kernel(xc, dyo, cols, rowt, bc, cc, yi_ref, dxi_ref, dcb_ref, cb):
    @pl.when(pl.program_id(0) == 0)
    def _():
        dcb_ref[...] = jnp.zeros(dcb_ref.shape, F32)
        for b in range(2):
            at = slice(b * Q, b * Q + Q)
            cb[b] = dot_tb(cc[at], bc[at])
            cb[2 + b] = dot_tb(bc[at], cc[at])

    low = triangle(True)
    high = triangle(False)
    lane = lax.broadcasted_iota(jnp.int32, (1, 2 * HEAD), 1)
    first = jnp.where(lane < HEAD, 1.0, 0.0).astype(BF16)
    second = jnp.where(lane < HEAD, 0.0, 1.0).astype(BF16)
    for b in range(2):
        at = slice(b * Q, b * Q + Q)
        dcb = dcb_ref[b]
        for p in range(2):
            ls = slice(p * 2 * HEAD, (p + 1) * 2 * HEAD)
            xp = xc[at, ls]
            dyp = dyo[at, ls]
            xbd = jnp.concatenate([xp * first, xp * second], axis=0)
            dbd = jnp.concatenate([dyp * first, dyp * second], axis=0)
            decay, mix, mixt = [], [], []
            for i in range(2):
                h = 2 * p + i
                ex = cols[0, at, h : h + 1] - rowt[0, 4 + h : 5 + h, at]
                lt = jnp.exp2(jnp.where(low, ex, NEG))
                ext = rowt[0, h : h + 1, at] - cols[0, at, 4 + h : 5 + h]
                ltt = jnp.exp2(jnp.where(high, ext, NEG))
                decay.append(lt)
                mix.append((cb[b] * lt).astype(BF16))
                mixt.append((cb[2 + b] * ltt).astype(BF16))
            yi_ref[at, ls] = dot(jnp.concatenate(mix, axis=1), xbd)
            dxi_ref[at, ls] = dot(jnp.concatenate(mixt, axis=1), dbd)
            dm = dot_tb(dyp, xbd)
            dcb = dcb + dm[:, 0:Q] * decay[0] + dm[:, Q:] * decay[1]
        dcb_ref[b] = dcb


def across_kernel(
    yv, x_own, rec, halo, w, xc, dyo, yi, dxi, ent, lea, bc, cc, fe, exp2, seg, rows, *rest
):
    (y_ref, gx_ref, send_ref, dc_ref, db_ref, wv_ref, ends_ref, dw_ref, head_ref, xs, gs, gy) = rest[-12:]
    y = yv[0]

    @pl.when(pl.program_id(0) == 0)
    def _():
        dc_ref[...] = jnp.zeros(dc_ref.shape, F32)
        db_ref[...] = jnp.zeros(db_ref.shape, F32)
        wv_ref[...] = jnp.zeros(wv_ref.shape, F32)

    xs[0:8] = halo[...]
    in_order(y, x_own[...], rec[0], xs, 8)
    s = conv_sum(xs, w, 2 * Q)
    x = xc[...].astype(F32)
    dy = dyo[...].astype(F32)
    f = dot(fe[0], exp2[...])
    er = dot(fe[1], exp2[...])
    wt = (x * f).astype(BF16)
    dyr = (dy * er).astype(BF16)
    d0, d1, skip = rows[0:1], rows[1:2], rows[3:4]
    top, end = slice(0, Q), slice(Q, 2 * Q)
    e0 = ent[...]
    r1 = lea[...]
    e1 = (d0 * e0.astype(F32) + dot_ta(bc[top], wt[top])).astype(BF16)
    r0 = (d1 * r1.astype(F32) + dot_ta(cc[end], dyr[end])).astype(BF16)
    over = jnp.concatenate([dot(cc[top], e0), dot(cc[end], e1)], axis=0) * er
    back = jnp.concatenate([dot(bc[top], r0), dot(bc[end], r1)], axis=0) * f
    yn = yi[...] + over
    dxn = dxi[...] + back
    dc_ref[top] += dot_tb(dyr[top], e0)
    dc_ref[end] += dot_tb(dyr[end], e1)
    db_ref[top] += dot_tb(wt[top], r0)
    db_ref[end] += dot_tb(wt[end], r1)
    wv_ref[0] += split_dot(dy * yn, seg[...])
    wv_ref[1] += split_dot(x * dxn, seg[...])
    xb = x * back
    ends_ref[...] = jnp.concatenate(
        [
            jnp.sum(xb[top], axis=0, keepdims=True)
            + d0 * jnp.sum(r0.astype(F32) * e0.astype(F32), axis=0, keepdims=True),
            jnp.sum(xb[end], axis=0, keepdims=True)
            + d1 * jnp.sum(r1.astype(F32) * e1.astype(F32), axis=0, keepdims=True),
            jnp.sum(x * dy, axis=0, keepdims=True),
            jnp.zeros((5, SUB), F32),
        ],
        axis=0,
    )
    gx, dw, head = conv_back(dxn + skip * dy, s, xs, gs, w, 2 * Q)
    dw_ref[...] = dw
    head_ref[...] = head
    gy[0] = (yn + skip * x).astype(BF16)
    gy[1] = gx.astype(BF16)

    @pl.when(y == 0)
    def _():
        y_ref[...] = gy[0, top]
        gx_ref[...] = gy[1, top]
        send_ref[...] = gy[:, end]

    @pl.when(y != 0)
    def _():
        y_ref[...] = gy[0, end]
        gx_ref[...] = gy[1, end]
        send_ref[...] = gy[:, top]


def finish_kernel(
    yv, b_own, c_own, dt_own, rec, halo, w, par, bc, cc, st, seg, dc, db, dcb, wv, ends,
    gb_ref, gc_ref, send_ref, gdt_ref, dw_ref, head_ref, gh_ref, xs, gs, gv, dts, gd,
):
    y = yv[0]
    width = b_own.shape[1]
    heads = par.shape[1]
    groups = width // N
    per = dc.shape[0] // groups
    for g in range(groups):
        cs = slice(g * N, (g + 1) * N)
        dcg = dc[g * per]
        dbg = db[g * per]
        dcbg = dcb[g * per]
        for i in range(1, per):
            dcg = dcg + dc[g * per + i]
            dbg = dbg + db[g * per + i]
            dcbg = dcbg + dcb[g * per + i]
        dcbg = dcbg.astype(BF16)
        for b in range(2):
            at = slice(b * Q, b * Q + Q)
            gv[1, at, cs] = dcg[at] + dot(dcbg[b], bc[at, cs])
            gv[0, at, cs] = dbg[at] + dot_ta(dcbg[b], cc[at, cs])
    for i, (own, out) in enumerate(((b_own, gb_ref), (c_own, gc_ref))):
        at = i * width
        xs[0:8] = halo[:, at : at + width]
        in_order(y, own[...], rec[:, at : at + width], xs, 8)
        wi = w[:, at : at + width]
        s = conv_sum(xs, wi, 2 * Q)
        gx, dw, head = conv_back(gv[i], s, xs, gs, wi, 2 * Q)
        dw_ref[:, at : at + width] = dw
        head_ref[:, at : at + width] = head

        @pl.when(y == 0)
        def _():
            out[...] = gx[0:Q].astype(BF16)
            send_ref[:, at : at + width] = gx[Q:].astype(BF16)

        @pl.when(y != 0)
        def _():
            out[...] = gx[Q:].astype(BF16)
            send_ref[:, at : at + width] = gx[0:Q].astype(BF16)

    @pl.when(y == 0)
    def _():
        dts[0:Q] = dt_own[:, 0:heads].astype(F32)
        dts[Q : 2 * Q] = rec[:, 2 * width : 2 * width + heads].astype(F32)

    @pl.when(y != 0)
    def _():
        dts[0:Q] = rec[:, 2 * width + heads : 2 * width + 2 * heads].astype(F32)
        dts[Q : 2 * Q] = dt_own[:, heads : 2 * heads].astype(F32)

    raw = dts[...] + par[1:2]
    step = st[...]
    rate = jnp.exp(par[0:1])
    chunks = wv.shape[0]
    w_sum, v_sum, e_sum = wv[0, 0], wv[0, 1], split_dot(ends[0], seg[0])
    for i in range(1, chunks):
        w_sum = w_sum + wv[i, 0]
        v_sum = v_sum + wv[i, 1]
        e_sum = e_sum + split_dot(ends[i], seg[i])
    tri = jnp.where(triangle(False), 1.0, 0.0).astype(BF16)
    diff = w_sum - v_sum
    dl = jnp.concatenate(
        [exact_dot(tri, diff[0:Q]) + e_sum[0:1], exact_dot(tri, diff[Q:]) + e_sum[1:2]], axis=0
    )
    ds = v_sum / step - rate * dl
    draw = ds / (1.0 + jnp.exp(-raw))
    gh_ref[...] = jnp.concatenate(
        [
            jnp.sum(dl * (-rate * step), axis=0, keepdims=True),
            jnp.sum(draw, axis=0, keepdims=True),
            e_sum[2:3],
            jnp.zeros((5, heads), F32),
        ],
        axis=0,
    )
    gd[...] = jnp.concatenate([draw, draw], axis=1).astype(BF16)

    @pl.when(y == 0)
    def _():
        gdt_ref[...] = gd[0:Q]
        send_ref[:, 2 * width :] = gd[Q:]

    @pl.when(y != 0)
    def _():
        gdt_ref[...] = gd[Q:]
        send_ref[:, 2 * width :] = gd[0:Q]


def whole(shape):
    return pl.BlockSpec(shape, lambda *_: (0,) * len(shape))


def shape_of(*dims, dtype=F32):
    return jax.ShapeDtypeStruct(dims, dtype)


def call(kernel, grid, in_specs, out_specs, out_shape, scratch, micros, nbytes, aliases=None):
    return pl.pallas_call(
        kernel,
        out_shape=out_shape,
        grid_spec=pltpu.PrefetchScalarGridSpec(
            num_scalar_prefetch=1,
            grid=grid,
            in_specs=in_specs,
            out_specs=out_specs,
            scratch_shapes=scratch,
        ),
        compiler_params=params(),
        cost_estimate=cost(micros, nbytes),
        input_output_aliases=aliases or {},
    )


def per_device(
    ssm_input, b_input, c_input, dt_input, conv_weight, conv_bias, a_log, dt_bias, skip_gain, grad_out
):
    x_rows, b_rows, c_rows = ssm_input[0], b_input[0], c_input[0]
    dt_rows, dy_rows = dt_input[0], grad_out[0]
    devices = lax.axis_size("sp")
    dp_size = lax.axis_size("dp")
    spots = devices // 2
    me = lax.axis_index("sp")
    y = lax.rem(me, 2)
    z = me // 2
    yv = jnp.reshape(y, (1,)).astype(jnp.int32)
    xw = x_rows.shape[1] // 2
    bw = b_rows.shape[1] // 2
    hl = dt_rows.shape[1] // 2
    chunks = 4
    cw = xw // chunks
    subs = cw // SUB
    per_group = chunks // (bw // N)
    edge = 8

    def pairs(fn):
        return [(i, fn(i)) for i in range(devices) if fn(i) is not None and 0 <= fn(i) < devices]

    swap = pairs(lambda i: i ^ 1)

    def half(v, which, width):
        return lax.dynamic_slice_in_dim(v, which * width, width, v.ndim - 1)

    msg = jnp.concatenate([half(b_rows, 1 - y, bw), half(c_rows, 1 - y, bw), dt_rows], axis=1)
    rec_bc = lax.ppermute(msg, "sp", swap)

    def rim(k):
        return jnp.concatenate(
            [
                x_rows[Q - edge :, k * xw : (k + 1) * xw],
                b_rows[Q - edge :, k * bw : (k + 1) * bw],
                c_rows[Q - edge :, k * bw : (k + 1) * bw],
            ],
            axis=1,
        )

    rim0 = lax.ppermute(rim(0), "sp", pairs(lambda i: i + 1 if i % 2 else None))
    rim1 = lax.ppermute(rim(1), "sp", pairs(lambda i: i + 2 if i % 2 else None))
    halo = rim0.astype(F32) + rim1.astype(F32)
    rec = []
    for c in range(chunks):
        at = (1 - y) * xw + c * cw
        out = jnp.stack(
            [lax.dynamic_slice_in_dim(x_rows, at, cw, 1), lax.dynamic_slice_in_dim(dy_rows, at, cw, 1)]
        )
        rec.append(lax.ppermute(out, "sp", swap))

    wb = jnp.concatenate([conv_weight, conv_bias[None], jnp.zeros((3, conv_bias.shape[0]), F32)], 0)
    wbx = half(wb[:, : 2 * xw], y, xw)
    wbc = jnp.concatenate(
        [half(wb[:, 2 * xw : 2 * xw + 2 * bw], y, bw), half(wb[:, 2 * xw + 2 * bw :], y, bw)], axis=1
    )
    halo_x, halo_bc = halo[:, :xw], halo[:, xw:]
    par = half(
        jnp.concatenate([jnp.stack([a_log, dt_bias, skip_gain]), jnp.zeros((5, 2 * hl), F32)], 0), y, hl
    )
    lanes = jnp.arange(xw) // HEAD
    expand = (jnp.arange(hl)[:, None] == lanes[None, :]).astype(BF16)
    exp2 = jnp.concatenate([expand, expand], axis=0)
    seg = (lanes[:, None] == jnp.arange(hl)[None, :]).astype(BF16)

    nq = hl // 4
    two = 2 * Q
    own_b = pl.BlockSpec((Q, bw), lambda j, yr: (0, yr[0]))
    bcc, ccc, fe, rows, cols, rowt, st = call(
        setup_kernel,
        (1,),
        [
            own_b, own_b, whole(dt_rows.shape), whole(rec_bc.shape), whole((edge, 2 * bw)),
            whole((8, 2 * bw)), whole((8, hl)), whole((2 * hl, xw)),
        ],
        [
            whole((two, bw)), whole((two, bw)), whole((2, two, 2 * hl)), whole((8, xw)),
            whole((nq, two, 8)), whole((nq, 8, two)), whole((two, hl)),
        ],
        [
            shape_of(two, bw, dtype=BF16), shape_of(two, bw, dtype=BF16),
            shape_of(2, two, 2 * hl, dtype=BF16), shape_of(8, xw), shape_of(nq, two, 8),
            shape_of(nq, 8, two), shape_of(two, hl),
        ],
        [
            pltpu.VMEM((two + 8, bw), F32), pltpu.VMEM((two, hl), F32),
            pltpu.VMEM((2 * hl, two), F32),
        ],
        4, 4 << 20,
    )(yv, b_rows, c_rows, dt_rows, rec_bc, halo_bc, wbc, par, exp2)

    def own(c):
        return pl.BlockSpec((Q, SUB), lambda j, yr: (0, (yr[0] * chunks + c) * subs + j))

    def band(rows_, c):
        return pl.BlockSpec((rows_, SUB), lambda j, yr: (0, c * subs + j))

    def group(c):
        return pl.BlockSpec((two, N), lambda j, yr: (0, c // per_group))

    local = pl.BlockSpec((two, SUB), lambda j, yr: (0, j))
    local8 = pl.BlockSpec((8, SUB), lambda j, yr: (0, j))
    full_fe = whole(fe.shape)

    xcs, dyos, ts, us = [], [], [], []
    for c in range(chunks):
        xc, dyo, t, u = call(
            state_kernel,
            (subs,),
            [
                own(c), own(c), pl.BlockSpec((2, Q, SUB), lambda j, yr: (0, 0, j)), band(edge, c),
                band(8, c), group(c), group(c), full_fe, band(2 * hl, c), band(8, c),
            ],
            [local] * 4,
            [shape_of(two, cw, dtype=BF16)] * 4,
            [pltpu.VMEM((two + 8, SUB), F32)],
            3, 4 << 20,
        )(yv, x_rows, dy_rows, rec[c], halo_x, wbx, bcc, ccc, fe, exp2, rows)
        xcs.append(xc)
        dyos.append(dyo)
        ts.append(t)
        us.append(u)

    zero = jnp.zeros((N, cw), BF16)
    both = rows[2]
    ent_in, lea_in = zero, zero
    ents = [zero] * chunks
    leas = [zero] * chunks
    back_spot = spots - 1 - z
    for t in range(chunks + spots - 2):
        def pick(items, at):
            out = items[0]
            for c in range(1, min(t, chunks - 1) + 1):
                out = jnp.where(at == c, items[c], out)
            return out

        decays = [both[c * cw : (c + 1) * cw] for c in range(chunks)]
        go = pick(decays, t - z) * ent_in.astype(F32) + pick(ts, t - z).astype(F32)
        ent_in = lax.ppermute(go.astype(BF16), "sp", pairs(lambda i: i + 2))
        go = pick(decays, t - back_spot) * lea_in.astype(F32) + pick(us, t - back_spot).astype(F32)
        lea_in = lax.ppermute(go.astype(BF16), "sp", pairs(lambda i: i - 2))
        for c in range(max(0, t + 2 - spots), min(t, chunks - 1) + 1):
            ents[c] = jnp.where(t + 1 - z == c, ent_in, ents[c])
            leas[c] = jnp.where(t + 1 - back_spot == c, lea_in, leas[c])

    yis, dxis, dcbs = [], [], []
    for c in range(chunks):
        yi, dxi, dcb = call(
            lambda yr, *refs: within_kernel(*refs),
            (subs,),
            [
                local, local,
                pl.BlockSpec((1, two, 8), lambda j, yr: (c * subs + j, 0, 0)),
                pl.BlockSpec((1, 8, two), lambda j, yr: (c * subs + j, 0, 0)),
                group(c), group(c),
            ],
            [local, local, whole((2, Q, Q))],
            [shape_of(two, cw), shape_of(two, cw), shape_of(2, Q, Q)],
            [pltpu.VMEM((4, Q, Q), F32)],
            5, 4 << 20,
        )(yv, xcs[c], dyos[c], cols, rowt, bcc, ccc)
        yis.append(yi)
        dxis.append(dxi)
        dcbs.append(dcb)

    y_all, gx_all = None, None
    parts = []
    for c in range(chunks):
        ins = [
            x_rows, rec[c], halo_x, wbx, xcs[c], dyos[c], yis[c], dxis[c], ents[c], leas[c],
            bcc, ccc, fe, exp2, seg, rows,
        ]
        specs = [
            own(c), pl.BlockSpec((1, Q, SUB), lambda j, yr: (0, 0, j)), band(edge, c), band(8, c),
            local, local, local, local, local, local, group(c), group(c), full_fe,
            band(2 * hl, c), pl.BlockSpec((SUB, hl), lambda j, yr: (c * subs + j, 0)), band(8, c),
        ]
        aliases = {}
        if c:
            aliases = {len(ins) + 1: 0, len(ins) + 2: 1}
            ins += [y_all, gx_all]
            specs += [pl.BlockSpec(memory_space=pl.ANY)] * 2
        full = shape_of(Q, 2 * xw, dtype=BF16)
        y_all, gx_all, send, *part = call(
            across_kernel,
            (subs,),
            specs,
            [
                own(c), own(c), pl.BlockSpec((2, Q, SUB), lambda j, yr: (0, 0, j)),
                whole((two, N)), whole((two, N)), whole((2, two, hl)), local8, local8, local8,
            ],
            [
                full, full, shape_of(2, Q, cw, dtype=BF16), shape_of(two, N), shape_of(two, N),
                shape_of(2, two, hl), shape_of(8, cw), shape_of(8, cw), shape_of(8, cw),
            ],
            [
                pltpu.VMEM((two + 8, SUB), F32), pltpu.VMEM((two + 8, SUB), F32),
                pltpu.VMEM((2, two, SUB), BF16),
            ],
            6, 6 << 20, aliases,
        )(yv, *ins)
        parts.append(part)
        got = lax.ppermute(send, "sp", swap)
        at = (1 - y) * xw + c * cw
        y_all = lax.dynamic_update_slice(y_all, got[0], (0, at))
        gx_all = lax.dynamic_update_slice(gx_all, got[1], (0, at))

    dcs, dbs, wvs, ends, dws, heads_ = [jnp.stack(v) for v in zip(*parts)]
    gb_own, gc_own, send, gdt_own, dw_bc, head_bc, gh = call(
        finish_kernel,
        (1,),
        [
            own_b, own_b, whole(dt_rows.shape), whole(rec_bc.shape), whole((edge, 2 * bw)),
            whole((8, 2 * bw)), whole((8, hl)), whole((two, bw)), whole((two, bw)), whole((two, hl)),
            whole((chunks, cw, hl)), whole(dcs.shape), whole(dbs.shape),
            whole((chunks, 2, Q, Q)), whole(wvs.shape), whole(ends.shape),
        ],
        [
            own_b, own_b, whole((Q, 2 * bw + 2 * hl)), whole((Q, 2 * hl)), whole((8, 2 * bw)),
            whole((8, 2 * bw)), whole((8, hl)),
        ],
        [
            shape_of(Q, 2 * bw, dtype=BF16), shape_of(Q, 2 * bw, dtype=BF16),
            shape_of(Q, 2 * bw + 2 * hl, dtype=BF16), shape_of(Q, 2 * hl, dtype=BF16),
            shape_of(8, 2 * bw), shape_of(8, 2 * bw), shape_of(8, hl),
        ],
        [
            pltpu.VMEM((two + 8, bw), F32), pltpu.VMEM((two + 8, bw), F32),
            pltpu.VMEM((2, two, bw), F32), pltpu.VMEM((two, hl), F32), pltpu.VMEM((two, 2 * hl), BF16),
        ],
        6, 8 << 20,
    )(
        yv, b_rows, c_rows, dt_rows, rec_bc, halo_bc, wbc, par, bcc, ccc, st,
        seg.reshape(chunks, cw, hl), dcs, dbs, jnp.stack(dcbs), wvs, ends,
    )
    got = lax.ppermute(send, "sp", swap)
    gb = lax.dynamic_update_slice(gb_own, got[:, :bw], (0, (1 - y) * bw))
    gc = lax.dynamic_update_slice(gc_own, got[:, bw : 2 * bw], (0, (1 - y) * bw))
    low_lane = jnp.arange(2 * hl)[None, :] < hl
    gdt = jnp.where(low_lane == (y == 0), gdt_own, got[:, 2 * bw :])

    first_rows = jnp.concatenate([jnp.concatenate(list(heads_), axis=1), head_bc], axis=1).astype(BF16)
    next0 = lax.ppermute(first_rows, "sp", pairs(lambda i: i - 1 if i % 2 == 0 else None)).astype(F32)
    next1 = lax.ppermute(first_rows, "sp", pairs(lambda i: i - 2 if i % 2 else None)).astype(F32)

    def rim_add(grad, lo, width, w):
        g = jnp.concatenate([next0[:, lo : lo + width], next1[:, lo : lo + width]], axis=1)
        add = jnp.concatenate(
            [
                jnp.zeros((5, 2 * width), F32),
                w[0:1] * g[0:1],
                w[0:1] * g[1:2] + w[1:2] * g[0:1],
                w[0:1] * g[2:3] + w[1:2] * g[1:2] + w[2:3] * g[0:1],
            ],
            axis=0,
        )
        tail = (grad[Q - 8 :].astype(F32) + add).astype(BF16)
        return lax.dynamic_update_slice(grad, tail, (Q - 8, 0))

    grad_x = rim_add(gx_all, 0, xw, conv_weight[:, : 2 * xw])
    grad_b = rim_add(gb, xw, bw, conv_weight[:, 2 * xw : 2 * xw + 2 * bw])
    grad_c = rim_add(gc, xw + bw, bw, conv_weight[:, 2 * xw + 2 * bw :])

    red = jnp.concatenate(
        [
            jnp.concatenate(list(dws) + [dw_bc], axis=1)[:5].reshape(-1),
            gh[:3].reshape(-1),
            jnp.zeros((5 * 128 - 3 * hl,), F32),
        ]
    ).reshape(-1, 128)
    size = 1
    while size < dp_size:
        red = red + lax.ppermute(red, "dp", [(i, i ^ size) for i in range(dp_size)])
        size *= 2
    size = 2
    while size < devices:
        red = red + lax.ppermute(red, "sp", [(i, i ^ size) for i in range(devices)])
        size *= 2
    other = lax.ppermute(red, "sp", swap)
    first = jnp.where(y == 0, red, other).reshape(-1)
    second = jnp.where(y == 0, other, red).reshape(-1)
    count = 5 * (xw + 2 * bw)
    g0 = first[:count].reshape(5, xw + 2 * bw)
    g1 = second[:count].reshape(5, xw + 2 * bw)
    total = jnp.concatenate(
        [g0[:, :xw], g1[:, :xw], g0[:, xw : xw + bw], g1[:, xw : xw + bw], g0[:, xw + bw :], g1[:, xw + bw :]],
        axis=1,
    )
    gheads = jnp.concatenate(
        [first[count : count + 3 * hl].reshape(3, hl), second[count : count + 3 * hl].reshape(3, hl)], axis=1
    )
    per_dev = 2 * hl // devices
    head_total = lax.dynamic_slice_in_dim(gheads, me * per_dev, per_dev, 1)
    return (
        y_all[None], grad_x[None], grad_b[None], grad_c[None], gdt[None], total[:4], total[4], head_total,
    )


def solution(mesh):
    rows = P("dp", "sp", None)
    in_specs = (rows, rows, rows, rows, P(), P(), P(), P(), P(), rows)
    out_specs = (rows, rows, rows, rows, rows, P(), P(), P(None, "sp"))
    return jax.shard_map(
        per_device, mesh=mesh, in_specs=in_specs, out_specs=out_specs, check_vma=False
    )
```

```python
import jax
import jax.numpy as jnp
import numpy as np
from jax import lax
from jax.experimental import pallas as pl
from jax.experimental.pallas import tpu as pltpu
from jax.sharding import PartitionSpec as P

N = 256
Q = 128
HEAD = 64
SUB = 256
LOG2E = 1.4426950408889634
F32 = jnp.float32
BF16 = jnp.bfloat16
NEG = -1e30


def params():
    return pltpu.CompilerParams(vmem_limit_bytes=14 * 1024 * 1024)


def cost(micros, nbytes):
    return pl.CostEstimate(flops=int(micros * 1e9), bytes_accessed=nbytes, transcendentals=0)


def dot(a, b):
    return jnp.dot(a, b, preferred_element_type=F32)


def dot_tb(a, b):
    return lax.dot_general(a, b, (((1,), (1,)), ((), ())), preferred_element_type=F32)


def dot_ta(a, b):
    return lax.dot_general(a, b, (((0,), (0,)), ((), ())), preferred_element_type=F32)


def halves(v):
    hi = v.astype(BF16)
    return hi, (v - hi.astype(F32)).astype(BF16)


def split_dot(v, m):
    hi, lo = halves(v)
    return dot(hi, m) + dot(lo, m)


def exact_dot(m, v):
    hi = v.astype(BF16)
    rest = v - hi.astype(F32)
    mid = rest.astype(BF16)
    low = (rest - mid.astype(F32)).astype(BF16)
    return dot(m, hi) + dot(m, mid) + dot(m, low)


def triangle(lower):
    row = lax.broadcasted_iota(jnp.int32, (Q, Q), 0)
    col = lax.broadcasted_iota(jnp.int32, (Q, Q), 1)
    return row >= col if lower else row <= col


def in_order(y, own, rec, dst, first=0):
    rows = own.shape[0]

    @pl.when(y == 0)
    def _():
        dst[first : first + rows] = own.astype(dst.dtype)
        dst[first + rows : first + 2 * rows] = rec.astype(dst.dtype)

    @pl.when(y != 0)
    def _():
        dst[first : first + rows] = rec.astype(dst.dtype)
        dst[first + rows : first + 2 * rows] = own.astype(dst.dtype)


def conv_sum(xs, w, bias, rows):
    total = bias[...]
    for k in range(4):
        total = total + w[k : k + 1] * xs[5 + k : 5 + k + rows]
    return total


def gates(s):
    sig = 0.5 + 0.5 * jnp.tanh(0.5 * s)
    out = s * sig
    return out, sig + out * (1.0 - sig)


def conv_back(ds, xs, gs, w, rows):
    gs[0:rows] = ds
    gs[rows : rows + 8] = jnp.zeros((8, ds.shape[1]), F32)
    dx = w[3:4] * ds
    for k in range(3):
        dx = dx + w[k : k + 1] * gs[3 - k : 3 - k + rows]
    dw = [jnp.sum(ds * xs[5 + k : 5 + k + rows], axis=0, keepdims=True) for k in range(4)]
    dw.append(jnp.sum(ds, axis=0, keepdims=True))
    dw.append(jnp.zeros((3, ds.shape[1]), F32))
    return dx, jnp.concatenate(dw, axis=0)


def pack_small_kernel(yv, b, c, dt, xr, br, cr, msg_ref, rim_ref):
    width = b.shape[1]
    msg_ref[:, 0:width] = b[...]
    msg_ref[:, width : 2 * width] = c[...]
    msg_ref[:, 2 * width :] = dt[...]
    half = xr.shape[1] // 2
    for k in range(2):
        rim_ref[k, :, 0:half] = xr[:, k * half : (k + 1) * half]
        rim_ref[k, :, half : half + width] = br[:, k * width : (k + 1) * width]
        rim_ref[k, :, half + width :] = cr[:, k * width : (k + 1) * width]


def pack_kernel(yv, x, dy, out):
    out[0] = x[...]
    out[1] = dy[...]


def unpack_kernel(yv, got, y_ref, gx_ref):
    y_ref[...] = got[0]
    gx_ref[...] = got[1]


def setup_kernel(
    yv, b_own, c_own, dt_own, rec, rim0, rim1, wb, wc, bb, bc_, par, exp2,
    halo_ref, bc_ref, cc_ref, bt_ref, ct_ref, ds_ref, fe_ref, rows_ref, cols_ref, rowt_ref, st_ref,
    xs, dts, xs2,
):
    y = yv[0]
    width = b_own.shape[1]
    heads = par.shape[1]
    half = halo_ref.shape[1] - 2 * width
    halo_ref[...] = (rim0[...].astype(F32) + rim1[...].astype(F32))[8:16]
    for i, (own, w, bias, out, out_t) in enumerate(
        ((b_own, wb, bb, bc_ref, bt_ref), (c_own, wc, bc_, cc_ref, ct_ref))
    ):
        at = i * width
        xs[0:8] = halo_ref[:, half + at : half + at + width]
        in_order(y, own[...], rec[:, at : at + width], xs, 8)
        v, slope = gates(conv_sum(xs, w, bias, 2 * Q))
        out[...] = v.astype(BF16)
        out_t[...] = jnp.transpose(v).astype(BF16)
        ds_ref[i] = slope

    @pl.when(y == 0)
    def _():
        dts[0:Q] = dt_own[:, 0:heads].astype(F32)
        dts[Q : 2 * Q] = rec[:, 2 * width : 2 * width + heads].astype(F32)

    @pl.when(y != 0)
    def _():
        dts[0:Q] = rec[:, 2 * width + heads : 2 * width + 2 * heads].astype(F32)
        dts[Q : 2 * Q] = dt_own[:, heads : 2 * heads].astype(F32)

    raw = dts[...] + par[1:2]
    step = jnp.log1p(jnp.exp(raw))
    logs = -step * jnp.exp(par[0:1])
    tri = jnp.where(triangle(True), 1.0, 0.0).astype(BF16)
    run0 = exact_dot(tri, logs[0:Q])
    run1 = exact_dot(tri, logs[Q:])
    tot0, tot1 = run0[Q - 1 : Q], run1[Q - 1 : Q]
    run = jnp.concatenate([run0, run1], axis=0)
    to_end = jnp.concatenate([jnp.exp(tot0 - run0), jnp.exp(tot1 - run1)], axis=0)
    hi, lo = halves(step * to_end)
    fe_ref[0] = jnp.concatenate([hi, lo], axis=1)
    hi, lo = halves(jnp.exp(run))
    fe_ref[1] = jnp.concatenate([hi, lo], axis=1)
    st_ref[...] = jnp.concatenate([step, raw], axis=1)
    small = jnp.concatenate(
        [jnp.exp(tot0), jnp.exp(tot1), jnp.exp(tot0 + tot1), par[2:3], jnp.zeros((4, heads), F32)],
        axis=0,
    )
    hi, lo = halves(small)
    rows_ref[...] = dot(jnp.concatenate([hi, lo], axis=1), exp2[...])
    r2 = run * LOG2E
    q2 = (run - jnp.log(step)) * LOG2E
    xs2[...] = jnp.transpose(jnp.concatenate([r2, q2], axis=1))
    for j in range(heads // 4):
        cols_ref[j] = jnp.concatenate([r2[:, 4 * j : 4 * j + 4], q2[:, 4 * j : 4 * j + 4]], axis=1)
        rowt_ref[j] = jnp.concatenate(
            [xs2[4 * j : 4 * j + 4], xs2[heads + 4 * j : heads + 4 * j + 4]], axis=0
        )


def state_kernel(
    yv, x_own, dy_own, rec, halo, w, bias, bt, ct, fe, exp2, rows,
    t_ref, u_ref, xc_ref, dyo_ref, sl_ref, xs,
):
    y = yv[0]
    xs[0:8] = halo[...]
    in_order(y, x_own[...], rec[0], xs, 8)
    in_order(y, dy_own[...], rec[1], dyo_ref)
    v, slope = gates(conv_sum(xs, w, bias, 2 * Q))
    xc = v.astype(BF16)
    xc_ref[...] = xc
    sl_ref[...] = slope.astype(BF16)
    wt = (xc.astype(F32) * dot(fe[0], exp2[...])).astype(BF16)
    dyr = (dyo_ref[...].astype(F32) * dot(fe[1], exp2[...])).astype(BF16)
    top, end = slice(0, Q), slice(Q, 2 * Q)
    t_ref[0] = (rows[1:2] * dot(bt[:, top], wt[top]) + dot(bt[:, end], wt[end])).astype(BF16)
    u_ref[0] = (dot(ct[:, top], dyr[top]) + rows[0:1] * dot(ct[:, end], dyr[end])).astype(BF16)


def hop_kernel(yv, in_e, in_o, t, u, row_f, row_b, out_e, out_o):
    @pl.when(yv[2] == 0)
    def _():
        out_e[...] = (row_f[2:3] * in_o[...].astype(F32) + t[0].astype(F32)).astype(BF16)
        out_o[...] = (row_b[2:3] * in_e[...].astype(F32) + u[0].astype(F32)).astype(BF16)

    @pl.when(yv[2] != 0)
    def _():
        out_o[...] = (row_f[2:3] * in_e[...].astype(F32) + t[0].astype(F32)).astype(BF16)
        out_e[...] = (row_b[2:3] * in_o[...].astype(F32) + u[0].astype(F32)).astype(BF16)


def within_kernel(yv, xc, dyo, cols, rowt, bc, cc, yi_ref, dxi_ref, dcb_ref, cb):
    @pl.when(pl.program_id(0) == 0)
    def _():
        dcb_ref[...] = jnp.zeros(dcb_ref.shape, F32)
        for b in range(2):
            at = slice(b * Q, b * Q + Q)
            cb[b] = dot_tb(cc[at], bc[at])
            cb[2 + b] = dot_tb(bc[at], cc[at])

    low = triangle(True)
    high = triangle(False)
    lane = lax.broadcasted_iota(jnp.int32, (1, 2 * HEAD), 1)
    first = jnp.where(lane < HEAD, 1.0, 0.0).astype(BF16)
    second = jnp.where(lane < HEAD, 0.0, 1.0).astype(BF16)
    for b in range(2):
        at = slice(b * Q, b * Q + Q)
        dcb = dcb_ref[b]
        for p in range(2):
            ls = slice(p * 2 * HEAD, (p + 1) * 2 * HEAD)
            xp = xc[at, ls]
            dyp = dyo[at, ls]
            xbd = jnp.concatenate([xp * first, xp * second], axis=0)
            dbd = jnp.concatenate([dyp * first, dyp * second], axis=0)
            decay, mix, mixt = [], [], []
            for i in range(2):
                h = 2 * p + i
                ex = cols[0, at, h : h + 1] - rowt[0, 4 + h : 5 + h, at]
                lt = jnp.exp2(jnp.where(low, ex, NEG))
                ext = rowt[0, h : h + 1, at] - cols[0, at, 4 + h : 5 + h]
                ltt = jnp.exp2(jnp.where(high, ext, NEG))
                decay.append(lt)
                mix.append((cb[b] * lt).astype(BF16))
                mixt.append((cb[2 + b] * ltt).astype(BF16))
            yi_ref[at, ls] = dot(jnp.concatenate(mix, axis=1), xbd)
            dxi_ref[at, ls] = dot(jnp.concatenate(mixt, axis=1), dbd)
            dm = dot_tb(dyp, xbd)
            dcb = dcb + dm[:, 0:Q] * decay[0] + dm[:, Q:] * decay[1]
        dcb_ref[b] = dcb


def fetch(spot, choices, dst, sem):
    @pl.when(spot == 0)
    def _():
        dst[...] = jnp.zeros(dst.shape, dst.dtype)

    for k, src in enumerate(choices, 1):

        @pl.when(spot == k)
        def _():
            copy = pltpu.make_async_copy(src, dst, sem)
            copy.start()
            copy.wait()


def across_kernel(
    yv, x_own, rec, halo, w, xc, dyo, sl, yi, dxi, bc, cc, bt, ct, fe, exp2, seg, rows, *rest
):
    hops = (len(rest) - 16) // 2
    (y_ref, gx_ref, red_ref, head_ref, send_ref, dc_ref, db_ref, wv_ref, ends_ref) = rest[2 * hops : -7]
    xs, gs, gy, ent, lea, sem0, sem1 = rest[-7:]
    y = yv[0]

    @pl.when(pl.program_id(0) == 0)
    def _():
        dc_ref[...] = jnp.zeros(dc_ref.shape, F32)
        db_ref[...] = jnp.zeros(db_ref.shape, F32)
        wv_ref[...] = jnp.zeros(wv_ref.shape, F32)
        fetch(yv[1], rest[:hops], ent, sem0)
        fetch(hops - yv[1], rest[hops : 2 * hops], lea, sem1)

    at = pl.multiple_of(pl.program_id(0) * SUB, SUB)
    xs[0:8] = halo[...]
    in_order(y, x_own[...], rec[0], xs, 8)
    x = xc[...].astype(F32)
    dy = dyo[...].astype(F32)
    f = dot(fe[0], exp2[...])
    er = dot(fe[1], exp2[...])
    wt = (x * f).astype(BF16)
    dyr = (dy * er).astype(BF16)
    d0, d1, skip = rows[0:1], rows[1:2], rows[3:4]
    top, end = slice(0, Q), slice(Q, 2 * Q)
    e0 = ent[:, pl.ds(at, SUB)]
    r1 = lea[:, pl.ds(at, SUB)]
    e1 = (d0 * e0.astype(F32) + dot(bt[:, top], wt[top])).astype(BF16)
    r0 = (d1 * r1.astype(F32) + dot(ct[:, end], dyr[end])).astype(BF16)
    over = jnp.concatenate([dot(cc[top], e0), dot(cc[end], e1)], axis=0) * er
    back = jnp.concatenate([dot(bc[top], r0), dot(bc[end], r1)], axis=0) * f
    yn = yi[...] + over
    dxn = dxi[...] + back
    dc_ref[top] += dot_tb(dyr[top], e0)
    dc_ref[end] += dot_tb(dyr[end], e1)
    db_ref[top] += dot_tb(wt[top], r0)
    db_ref[end] += dot_tb(wt[end], r1)
    wv_ref[0] += split_dot(dy * yn, seg[...])
    wv_ref[1] += split_dot(x * dxn, seg[...])
    xb = x * back
    ends_ref[...] = jnp.concatenate(
        [
            jnp.sum(xb[top], axis=0, keepdims=True)
            + d0 * jnp.sum(r0.astype(F32) * e0.astype(F32), axis=0, keepdims=True),
            jnp.sum(xb[end], axis=0, keepdims=True)
            + d1 * jnp.sum(r1.astype(F32) * e1.astype(F32), axis=0, keepdims=True),
            jnp.sum(x * dy, axis=0, keepdims=True),
            jnp.zeros((5, SUB), F32),
        ],
        axis=0,
    )
    ds = (dxn + skip * dy) * sl[...].astype(F32)
    gx, dw = conv_back(ds, xs, gs, w, 2 * Q)
    red_ref[...] = dw
    head_ref[...] = ds[0:8]
    gy[0] = (yn + skip * x).astype(BF16)
    gy[1] = gx.astype(BF16)

    @pl.when(y == 0)
    def _():
        y_ref[...] = gy[0, top]
        gx_ref[...] = gy[1, top]
        send_ref[...] = gy[:, end]

    @pl.when(y != 0)
    def _():
        y_ref[...] = gy[0, end]
        gx_ref[...] = gy[1, end]
        send_ref[...] = gy[:, top]


def finish_group(
    yv, b_own, c_own, b_rec, c_rec, b_halo, c_halo, wb, wc, slope, bc, cc, parts,
    gb_ref, gc_ref, red_ref, head_ref, send_ref, xs, gs, gv,
):
    y = yv[0]
    dc, db, dcb = [sum(r[...] for r in refs[1:]) + refs[0][...] for refs in zip(*parts)]
    dcb = dcb.astype(BF16)
    for b in range(2):
        at = slice(b * Q, b * Q + Q)
        gv[0, at] = db[at] + dot_ta(dcb[b], cc[at])
        gv[1, at] = dc[at] + dot(dcb[b], bc[at])
    for i, (own, rec, halo, w, out) in enumerate(
        ((b_own, b_rec, b_halo, wb, gb_ref), (c_own, c_rec, c_halo, wc, gc_ref))
    ):
        cs = slice(i * N, (i + 1) * N)
        xs[0:8] = halo[...]
        in_order(y, own[...], rec[...], xs, 8)
        ds = gv[i] * slope[i]
        gx, dw = conv_back(ds, xs, gs, w, 2 * Q)
        red_ref[:, cs] = dw
        head_ref[:, cs] = ds[0:8]

        @pl.when(y == 0)
        def _():
            out[...] = gx[0:Q].astype(BF16)
            send_ref[:, cs] = gx[Q:].astype(BF16)

        @pl.when(y != 0)
        def _():
            out[...] = gx[Q:].astype(BF16)
            send_ref[:, cs] = gx[0:Q].astype(BF16)


def finish_kernel(
    yv, b_own, c_own, b_rec, c_rec, b_halo, c_halo, wb, wc, slope, bc, cc,
    dc0, db0, dcb0, dc1, db1, dcb1,
    gb_ref, gc_ref, red_ref, head_ref, send_ref, xs, gs, gv,
):
    finish_group(
        yv, b_own, c_own, b_rec, c_rec, b_halo, c_halo, wb, wc, slope, bc, cc,
        [(dc0, db0, dcb0), (dc1, db1, dcb1)],
        gb_ref, gc_ref, red_ref, head_ref, send_ref, xs, gs, gv,
    )
    red_ref[:, 2 * N :] = jnp.zeros((8, red_ref.shape[1] - 2 * N), F32)
    head_ref[:, 2 * N :] = jnp.zeros((8, head_ref.shape[1] - 2 * N), F32)


def finish_last_kernel(
    yv, b_own, c_own, b_rec, c_rec, b_halo, c_halo, wb, wc, slope, bc, cc,
    dc0, db0, dcb0, dc1, db1, dcb1, st, par, seg, *rest,
):
    chunks = (len(rest) - 10) // 2
    wvs, ends, rest = rest[:chunks], rest[chunks : 2 * chunks], rest[2 * chunks :]
    gb_ref, gc_ref, red_ref, head_ref, send_ref, gdt_ref, xs, gs, gv, gd = rest
    y = yv[0]
    finish_group(
        yv, b_own, c_own, b_rec, c_rec, b_halo, c_halo, wb, wc, slope, bc, cc,
        [(dc0, db0, dcb0), (dc1, db1, dcb1)],
        gb_ref, gc_ref, red_ref, head_ref, send_ref, xs, gs, gv,
    )
    heads = par.shape[1]
    step, raw = st[:, 0:heads], st[:, heads:]
    rate = jnp.exp(par[0:1])
    cw = ends[0].shape[1]
    w_sum = sum(wv[0] for wv in wvs[1:]) + wvs[0][0]
    v_sum = sum(wv[1] for wv in wvs[1:]) + wvs[0][1]
    e_sum = split_dot(ends[0][...], seg[0:cw])
    for i in range(1, chunks):
        e_sum = e_sum + split_dot(ends[i][...], seg[i * cw : (i + 1) * cw])
    tri = jnp.where(triangle(False), 1.0, 0.0).astype(BF16)
    diff = w_sum - v_sum
    dl = jnp.concatenate(
        [exact_dot(tri, diff[0:Q]) + e_sum[0:1], exact_dot(tri, diff[Q:]) + e_sum[1:2]], axis=0
    )
    draw = (v_sum / step - rate * dl) / (1.0 + jnp.exp(-raw))
    red_ref[:, 2 * N :] = jnp.concatenate(
        [
            jnp.concatenate(
                [
                    jnp.sum(dl * (-rate * step), axis=0, keepdims=True),
                    jnp.sum(draw, axis=0, keepdims=True),
                    e_sum[2:3],
                    jnp.zeros((5, heads), F32),
                ],
                axis=0,
            ),
            jnp.zeros((8, red_ref.shape[1] - 2 * N - heads), F32),
        ],
        axis=1,
    )
    head_ref[:, 2 * N :] = jnp.zeros((8, head_ref.shape[1] - 2 * N), F32)
    gd[...] = jnp.concatenate([draw, draw], axis=1).astype(BF16)

    @pl.when(y == 0)
    def _():
        gdt_ref[...] = gd[0:Q]
        send_ref[:, 2 * N :] = gd[Q:]

    @pl.when(y != 0)
    def _():
        gdt_ref[...] = gd[Q:]
        send_ref[:, 2 * N :] = gd[0:Q]


def add_kernel(yv, *refs):
    total = refs[0][...]
    for r in refs[1:-1]:
        total = total + r[...]
    refs[-1][...] = total


def close_kernel(yv, got0, got1, gdt_own, gb_ref, gc_ref, gdt_ref):
    at = [got0, got1]
    for g in range(2):
        gb_ref[:, g * N : (g + 1) * N] = at[g][:, 0:N]
        gc_ref[:, g * N : (g + 1) * N] = at[g][:, N : 2 * N]
    lane = lax.broadcasted_iota(jnp.int32, gdt_own.shape, 1)
    low = lane < gdt_own.shape[1] // 2
    own, got = gdt_own[...].astype(F32), got1[:, 2 * N :].astype(F32)

    @pl.when(yv[0] == 0)
    def _():
        gdt_ref[...] = jnp.where(low, own, got).astype(BF16)

    @pl.when(yv[0] != 0)
    def _():
        gdt_ref[...] = jnp.where(low, got, own).astype(BF16)


def rim_kernel(yv, next0, next1, w, gx, gb, gc, gx_ref, gb_ref, gc_ref):
    wide = gx.shape[1] // 2
    base = next0.shape[1] - wide
    step = base // 2

    def add(src, dst, pieces):
        at = 0
        for ref, lo, size, wlo in pieces:
            h = ref[:, lo : lo + size]
            k = w[:, wlo : wlo + size]
            more = jnp.concatenate(
                [
                    jnp.zeros((13, size), F32),
                    k[0:1] * h[0:1],
                    k[0:1] * h[1:2] + k[1:2] * h[0:1],
                    k[0:1] * h[2:3] + k[1:2] * h[1:2] + k[2:3] * h[0:1],
                ],
                axis=0,
            )
            dst[:, at : at + size] = (src[:, at : at + size].astype(F32) + more).astype(BF16)
            at += size

    both = (next0, next1)
    add(gx, gx_ref, [(both[k], base, wide, k * wide) for k in range(2)])
    for i, (src, dst) in enumerate(((gb, gb_ref), (gc, gc_ref))):
        first = 2 * wide + i * 4 * N
        add(
            src, dst,
            [(both[k], g * step + i * N, N, first + (2 * k + g) * N) for k in range(2) for g in range(2)],
        )


def sums_kernel(yv, mine, theirs, gw_ref, gb_ref, gh_ref, both, *, wide):
    width = mine.shape[2]

    @pl.when(yv[3] == 0)
    def _():
        both[:, :, 0:width] = mine[...]
        both[:, :, width:] = theirs[...]

    @pl.when(yv[3] != 0)
    def _():
        both[:, :, 0:width] = theirs[...]
        both[:, :, width:] = mine[...]

    base = 2 * width - wide
    step = base // 2
    heads = gh_ref.shape[1] // 2

    def fill(order):
        for k in range(2):
            v = both[order[k]]
            gw_ref[:, k * wide : (k + 1) * wide] = v[0:4, base:]
            gb_ref[:, k * wide : (k + 1) * wide] = v[4:5, base:]
            for i in range(2):
                for g in range(2):
                    to = 2 * wide + i * 4 * N + (2 * k + g) * N
                    gw_ref[:, to : to + N] = v[0:4, g * step + i * N : g * step + (i + 1) * N]
                    gb_ref[:, to : to + N] = v[4:5, g * step + i * N : g * step + (i + 1) * N]
        at = step + 2 * N
        gh_ref[...] = jnp.concatenate(
            [both[order[0]][:, at : at + heads], both[order[1]][:, at : at + heads]], axis=1
        )

    @pl.when(yv[0] == 0)
    def _():
        fill((0, 1))

    @pl.when(yv[0] != 0)
    def _():
        fill((1, 0))


def whole(shape):
    return pl.BlockSpec(shape, lambda *_: (0,) * len(shape))


def shape_of(*dims, dtype=F32):
    return jax.ShapeDtypeStruct(dims, dtype)


def call(kernel, yv, grid, ins, outs, scratch, micros, nbytes, keep=(), after=()):
    count = len(ins)
    extra = len(keep) + len(after)

    def run(yr, *refs):
        kernel(yr, *refs[:count], *refs[count + extra :])

    anywhere = pl.BlockSpec(memory_space=pl.ANY)
    return pl.pallas_call(
        run,
        out_shape=[o[0] for o in outs],
        grid_spec=pltpu.PrefetchScalarGridSpec(
            num_scalar_prefetch=1,
            grid=grid,
            in_specs=[i[1] for i in ins] + [anywhere] * extra,
            out_specs=[o[1] for o in outs],
            scratch_shapes=scratch,
        ),
        compiler_params=params(),
        cost_estimate=cost(micros, nbytes),
        input_output_aliases={1 + count + k: k for k in range(len(keep))},
    )(yv, *[i[0] for i in ins], *keep, *after)


def per_device(
    ssm_input, b_input, c_input, dt_input, conv_weight, conv_bias, a_log, dt_bias, skip_gain, grad_out
):
    x_rows, b_rows, c_rows = ssm_input[0], b_input[0], c_input[0]
    dt_rows, dy_rows = dt_input[0], grad_out[0]
    devices = lax.axis_size("sp")
    dp_size = lax.axis_size("dp")
    spots = devices // 2
    me = lax.axis_index("sp")
    y = lax.rem(me, 2)
    z = me // 2
    core = lax.rem(lax.axis_index("dp"), 2)
    yv = jnp.stack([y, z, lax.rem(z, 2), core]).astype(jnp.int32)
    xw = x_rows.shape[1] // 2
    bw = b_rows.shape[1] // 2
    hl = dt_rows.shape[1] // 2
    chunks = 4
    cw = xw // chunks
    subs = cw // SUB
    groups = bw // N
    per_group = chunks // groups
    two = 2 * Q
    piece = 2 * N + 2 * hl
    base = groups * piece
    bands = base // SUB
    bias = conv_bias[None]

    def pairs(fn, n=devices):
        return [(i, fn(i)) for i in range(n) if fn(i) is not None and 0 <= fn(i) < n]

    swap = pairs(lambda i: i ^ 1)

    def cols(width, other, step=1, plus=0):
        if other:
            return pl.BlockSpec((Q, width), lambda j, yr: (0, (1 - yr[0]) * step + plus))
        return pl.BlockSpec((Q, width), lambda j, yr: (0, yr[0] * step + plus))

    def tail(width):
        return pl.BlockSpec((16, width), lambda j, yr: (Q // 16 - 1, 0))

    msg, rims = call(
        pack_small_kernel, yv, (1,),
        [
            (b_rows, cols(bw, True)), (c_rows, cols(bw, True)), (dt_rows, whole(dt_rows.shape)),
            (x_rows, tail(2 * xw)), (b_rows, tail(2 * bw)), (c_rows, tail(2 * bw)),
        ],
        [
            (shape_of(Q, 2 * bw + 2 * hl, dtype=BF16), whole((Q, 2 * bw + 2 * hl))),
            (shape_of(2, 16, xw + 2 * bw, dtype=BF16), whole((2, 16, xw + 2 * bw))),
        ],
        [], 1, 2 << 20,
    )
    rec_bc = lax.ppermute(msg, "sp", swap)
    rim0 = lax.ppermute(rims[0], "sp", pairs(lambda i: i + 1 if i % 2 else None))
    rim1 = lax.ppermute(rims[1], "sp", pairs(lambda i: i + 2 if i % 2 else None))

    rec = []

    def send_chunk(c, after):
        (out,) = call(
            pack_kernel, yv, (1,),
            [(x_rows, cols(cw, True, chunks, c)), (dy_rows, cols(cw, True, chunks, c))],
            [(shape_of(2, Q, cw, dtype=BF16), whole((2, Q, cw)))],
            [], 1, 1 << 20, after=after,
        )
        rec.append(lax.ppermute(out, "sp", swap))

    send_chunk(0, [msg])

    par = lax.dynamic_slice_in_dim(
        jnp.concatenate([jnp.stack([a_log, dt_bias, skip_gain]), jnp.zeros((5, 2 * hl), F32)], 0),
        y * hl, hl, 1,
    )
    lanes = np.arange(xw) // HEAD
    expand = (np.arange(hl)[:, None] == lanes[None, :]).astype(BF16)
    exp2 = jnp.asarray(np.concatenate([expand, expand], axis=0))
    seg = jnp.asarray(np.ascontiguousarray(expand.T))

    nq = hl // 4
    first_b, first_c = 2 * xw // bw, 2 * xw // bw + 2

    def wide_w(rows_, at):
        return pl.BlockSpec((rows_, bw), lambda j, yr: (0, at + yr[0]))

    halo, bcc, ccc, bct, cct, slopes, fe, rows, qcols, rowt, st = call(
        setup_kernel, yv, (1,),
        [
            (b_rows, cols(bw, False)), (c_rows, cols(bw, False)), (dt_rows, whole(dt_rows.shape)),
            (rec_bc, whole(rec_bc.shape)), (rim0, whole(rim0.shape)), (rim1, whole(rim1.shape)),
            (conv_weight, wide_w(4, first_b)), (conv_weight, wide_w(4, first_c)),
            (bias, wide_w(1, first_b)), (bias, wide_w(1, first_c)),
            (par, whole((8, hl))), (exp2, whole((2 * hl, xw))),
        ],
        [
            (shape_of(8, xw + 2 * bw), whole((8, xw + 2 * bw))),
            (shape_of(two, bw, dtype=BF16), whole((two, bw))),
            (shape_of(two, bw, dtype=BF16), whole((two, bw))),
            (shape_of(bw, two, dtype=BF16), whole((bw, two))),
            (shape_of(bw, two, dtype=BF16), whole((bw, two))),
            (shape_of(2, two, bw), whole((2, two, bw))),
            (shape_of(2, two, 2 * hl, dtype=BF16), whole((2, two, 2 * hl))),
            (shape_of(8, xw), whole((8, xw))),
            (shape_of(nq, two, 8), whole((nq, two, 8))),
            (shape_of(nq, 8, two), whole((nq, 8, two))),
            (shape_of(two, 2 * hl), whole((two, 2 * hl))),
        ],
        [
            pltpu.VMEM((two + 8, bw), F32), pltpu.VMEM((two, hl), F32),
            pltpu.VMEM((2 * hl, two), F32),
        ],
        4, 4 << 20,
    )
    send_chunk(1, [rec_bc])

    def own(c):
        return pl.BlockSpec((Q, SUB), lambda j, yr: (0, (yr[0] * chunks + c) * subs + j))

    def weight(rows_, c):
        return pl.BlockSpec((rows_, SUB), lambda j, yr: (0, (yr[0] * chunks + c) * subs + j))

    def band(rows_, c, first=0):
        return pl.BlockSpec((rows_, SUB), lambda j, yr: (0, first + c * subs + j))

    def group(c):
        return pl.BlockSpec((two, N), lambda j, yr: (0, c // per_group))

    def group_t(c):
        return pl.BlockSpec((N, two), lambda j, yr: (c // per_group, 0))

    local = pl.BlockSpec((two, SUB), lambda j, yr: (0, j))
    local8 = pl.BlockSpec((8, SUB), lambda j, yr: (0, j))
    wave = pl.BlockSpec((N, SUB), lambda j, yr: (0, j))
    arrived = pl.BlockSpec((2, Q, SUB), lambda j, yr: (0, 0, j))

    states = []
    xcs, dyos, sls = [], [], []

    def state(c, after):
        nonlocal states
        slot = pl.BlockSpec((1, N, SUB), lambda j, yr: (c, 0, j))
        big = shape_of(chunks, N, cw, dtype=BF16)
        tall = shape_of(two, cw, dtype=BF16)
        t, u, xc, dyo, sl = call(
            state_kernel, yv, (subs,),
            [
                (x_rows, own(c)), (dy_rows, own(c)), (rec[c], arrived), (halo, band(8, c)),
                (conv_weight, weight(4, c)), (bias, weight(1, c)), (bct, group_t(c)),
                (cct, group_t(c)), (fe, whole(fe.shape)), (exp2, band(2 * hl, c)), (rows, band(8, c)),
            ],
            [(big, slot), (big, slot), (tall, local), (tall, local), (tall, local)],
            [pltpu.VMEM((two + 8, SUB), F32)],
            3, 4 << 20, keep=states, after=after,
        )
        states = [t, u]
        xcs.append(xc)
        dyos.append(dyo)
        sls.append(sl)
        return xc

    yis, dxis, dcbs = [], [], []

    def within(c, after):
        yi, dxi, dcb = call(
            within_kernel, yv, (subs,),
            [
                (xcs[c], local), (dyos[c], local),
                (qcols, pl.BlockSpec((1, two, 8), lambda j, yr: (c * subs + j, 0, 0))),
                (rowt, pl.BlockSpec((1, 8, two), lambda j, yr: (c * subs + j, 0, 0))),
                (bcc, group(c)), (ccc, group(c)),
            ],
            [
                (shape_of(two, cw), local), (shape_of(two, cw), local),
                (shape_of(2, Q, Q), whole((2, Q, Q))),
            ],
            [pltpu.VMEM((4, Q, Q), F32)],
            3, 4 << 20, after=after,
        )
        yis.append(yi)
        dxis.append(dxi)
        dcbs.append(dcb)
        return dcb

    finals = []
    sums = []
    got_x = []

    def across(c, ents, leas, after):
        nonlocal finals
        full = shape_of(Q, 2 * xw, dtype=BF16)
        strip = shape_of(8, base + xw)
        out = call(
            across_kernel, yv, (subs,),
            [
                (x_rows, own(c)), (rec[c], pl.BlockSpec((1, Q, SUB), lambda j, yr: (0, 0, j))),
                (halo, band(8, c)), (conv_weight, weight(4, c)), (xcs[c], local), (dyos[c], local),
                (sls[c], local), (yis[c], local), (dxis[c], local),
                (bcc, group(c)), (ccc, group(c)), (bct, group_t(c)), (cct, group_t(c)),
                (fe, whole(fe.shape)), (exp2, band(2 * hl, c)),
                (seg, pl.BlockSpec((SUB, hl), lambda j, yr: (c * subs + j, 0))), (rows, band(8, c)),
            ] + [(v, pl.BlockSpec(memory_space=pl.ANY)) for v in ents + leas],
            [
                (full, own(c)), (full, own(c)), (strip, band(8, c, bands)), (strip, band(8, c, bands)),
                (shape_of(2, Q, cw, dtype=BF16), arrived), (shape_of(two, N), whole((two, N))),
                (shape_of(two, N), whole((two, N))), (shape_of(2, two, hl), whole((2, two, hl))),
                (shape_of(8, cw), local8),
            ],
            [
                pltpu.VMEM((two + 8, SUB), F32), pltpu.VMEM((two + 8, SUB), F32),
                pltpu.VMEM((2, two, SUB), BF16), pltpu.VMEM((N, cw), BF16), pltpu.VMEM((N, cw), BF16),
                pltpu.SemaphoreType.DMA, pltpu.SemaphoreType.DMA,
            ],
            6, 6 << 20, keep=finals, after=after,
        )
        finals = list(out[:4])
        sums.append(out[5:])
        got_x.append(lax.ppermute(out[4], "sp", swap))
        return out[8]

    def unpack(c, after):
        full = shape_of(Q, 2 * xw, dtype=BF16)
        finals[:2] = call(
            unpack_kernel, yv, (1,),
            [(got_x[c], whole((2, Q, cw)))],
            [(full, cols(cw, True, chunks, c)), (full, cols(cw, True, chunks, c))],
            [], 1, 1 << 20, keep=finals[:2], after=after,
        )

    grads_bc = []

    def finish(g, last, after):
        nonlocal grads_bc
        full = shape_of(Q, 2 * bw, dtype=BF16)
        strip = shape_of(8, base + xw)

        def wg(at):
            return pl.BlockSpec((4, N), lambda j, yr: (0, (2 * xw + at) // N + yr[0] * groups + g))

        def rec_at(at):
            return pl.BlockSpec((Q, N), lambda j, yr: (0, at // N + g))

        def halo_at(at):
            return pl.BlockSpec((8, N), lambda j, yr: (0, (xw + at) // N + g))

        tok_own = cols(N, False, groups, g)
        ins = [
            (b_rows, tok_own), (c_rows, tok_own), (rec_bc, rec_at(0)), (rec_bc, rec_at(bw)),
            (halo, halo_at(0)), (halo, halo_at(bw)), (conv_weight, wg(0)), (conv_weight, wg(2 * bw)),
            (slopes, pl.BlockSpec((2, two, N), lambda j, yr: (0, 0, g))),
            (bcc, pl.BlockSpec((two, N), lambda j, yr: (0, g))),
            (ccc, pl.BlockSpec((two, N), lambda j, yr: (0, g))),
        ]
        for c in range(g * per_group, (g + 1) * per_group):
            ins += [
                (sums[c][0], whole((two, N))), (sums[c][1], whole((two, N))),
                (dcbs[c], whole((2, Q, Q))),
            ]
        place = pl.BlockSpec((8, piece), lambda j, yr: (0, g))
        send_w = piece if last else 2 * N
        outs = [
            (strip, place), (strip, place), (full, tok_own), (full, tok_own),
            (shape_of(Q, send_w, dtype=BF16), whole((Q, send_w))),
        ]
        scratch = [
            pltpu.VMEM((two + 8, N), F32), pltpu.VMEM((two + 8, N), F32), pltpu.VMEM((2, two, N), F32),
        ]
        if last:
            ins += [(st, whole(st.shape)), (par, whole(par.shape)), (seg, whole(seg.shape))]
            ins += [(s[2], whole(s[2].shape)) for s in sums]
            ins += [(s[3], whole(s[3].shape)) for s in sums]
            outs.append((shape_of(Q, 2 * hl, dtype=BF16), whole((Q, 2 * hl))))
            scratch.append(pltpu.VMEM((two, 2 * hl), BF16))
        kernel = finish_last_kernel if last else finish_kernel
        count = len(ins)

        def reordered(yr, *refs):
            red, head, gb, gc = refs[count : count + 4]
            kernel(yr, *refs[:count], gb, gc, red, head, *refs[count + 4 :])

        out = call(
            reordered, yv, (1,), ins, outs, scratch, 3, 4 << 20,
            keep=finals[2:4] + grads_bc, after=after,
        )
        finals[2:4] = out[:2]
        grads_bc = list(out[2:4])
        return lax.ppermute(out[4], "sp", swap), (out[5] if last else out[4])

    evens = pairs(lambda i: i ^ 2)
    odds = pairs(lambda i: ((i + 2) ^ 2) - 2 if 2 <= i < devices - 2 else None)
    zero = jnp.zeros((N, cw), BF16)
    in_e, in_o = zero, zero
    ins_e, ins_o = [], []
    steps = chunks + spots - 2
    state(0, [])
    send_chunk(2, [rec[0]])
    got_bc = []
    waits = []
    for t in range(steps + 1):
        if t:
            ins_e.append(in_e)
            ins_o.append(in_o)
        token = []
        if t < steps:

            def slot(back):
                def at(j, yr):
                    c = t - (spots - 1 - yr[1] if back else yr[1])
                    return (jnp.clip(c, 0, chunks - 1), 0, j)

                return pl.BlockSpec((1, N, SUB), at)

            def slot_row(back):
                def at(j, yr):
                    c = t - (spots - 1 - yr[1] if back else yr[1])
                    return (0, jnp.clip(c, 0, chunks - 1) * subs + j)

                return pl.BlockSpec((8, SUB), at)

            moving = shape_of(N, cw, dtype=BF16)
            out_e, out_o = call(
                hop_kernel, yv, (subs,),
                [
                    (in_e, wave), (in_o, wave), (states[0], slot(False)), (states[1], slot(True)),
                    (rows, slot_row(False)), (rows, slot_row(True)),
                ],
                [(moving, wave), (moving, wave)],
                [], 1, 3 << 20, after=waits,
            )
            token = [out_e]
            in_e = lax.ppermute(out_e, "sp", evens)
            in_o = lax.ppermute(out_o, "sp", odds)
        waits = []
        if t + 1 < chunks:
            waits.append(state(t + 1, token))
            if t + 3 < chunks:
                send_chunk(t + 3, [rec[t + 1]])
        if t < chunks:
            waits.append(within(t, token))
        c = t + 1 - spots
        if 0 <= c < chunks:
            ents = [(ins_o if k % 2 == 0 else ins_e)[c + k - 1] for k in range(1, spots)]
            leas = [(ins_o if (spots - 1 - k) % 2 else ins_e)[c + k - 1] for k in range(1, spots)]
            waits.append(across(c, ents, leas, token))
            if c == chunks - 2:
                unpack(0, token)
                got, tok = finish(0, False, token)
                got_bc.append(got)
                waits += [tok, finals[0]]
            if c == chunks - 1:
                unpack(1, [])
                unpack(2, [])
    got, gdt_own = finish(1, True, [finals[0]])
    got_bc.append(got)
    unpack(3, [gdt_own])
    y_all, gx_all, red, heads_ = finals

    hw = (base + xw) // 2
    slab = shape_of(8, hw)

    def side(other):
        if other:
            return pl.BlockSpec((8, hw), lambda j, yr: (0, 1 - yr[3]))
        return pl.BlockSpec((8, hw), lambda j, yr: (0, yr[3]))

    def add(items, after=()):
        (out,) = call(
            add_kernel, yv, (1,), items, [(slab, whole((8, hw)))], [], 1, 1 << 20, after=after
        )
        return out

    theirs = add([(red, side(True))])
    mine = add([(red, side(False)), (lax.ppermute(theirs, "dp", pairs(lambda i: i ^ 1, dp_size)), whole((8, hw)))])
    size = 2
    while size < dp_size:
        mine = mine + lax.ppermute(mine, "dp", pairs(lambda i: i ^ size, dp_size))
        size *= 2
    size = 2
    while size < devices:
        ways = 4 if size * 4 <= devices else 2
        got = [lax.ppermute(mine, "sp", pairs(lambda i: i ^ (size * k))) for k in range(1, ways)]
        size *= ways
        mine = add([(v, whole((8, hw))) for v in [mine] + got], [y_all] if size >= devices else [])
    mine = jnp.stack([mine, lax.ppermute(mine, "sp", swap)])
    theirs = lax.ppermute(mine, "dp", pairs(lambda i: i ^ 1, dp_size))

    next0 = lax.ppermute(heads_, "sp", pairs(lambda i: i - 1 if i % 2 == 0 else None))
    next1 = lax.ppermute(heads_, "sp", pairs(lambda i: i - 2 if i % 2 else None))
    full = shape_of(Q, 2 * bw, dtype=BF16)
    gb, gc, gdt = call(
        close_kernel, yv, (1,),
        [
            (got_bc[0], whole(got_bc[0].shape)), (got_bc[1], whole(got_bc[1].shape)),
            (gdt_own, whole(gdt_own.shape)),
        ],
        [
            (full, cols(bw, True)), (full, cols(bw, True)),
            (shape_of(Q, 2 * hl, dtype=BF16), whole((Q, 2 * hl))),
        ],
        [], 1, 1 << 20, keep=grads_bc,
    )
    last = [pl.BlockSpec((16, v.shape[1]), lambda j, yr: (Q // 16 - 1, 0)) for v in (gx_all, gb, gc)]
    kept = [gx_all, gb, gc]
    grad_x, grad_b, grad_c = pl.pallas_call(
        rim_kernel,
        out_shape=[shape_of(*v.shape, dtype=BF16) for v in kept],
        grid_spec=pltpu.PrefetchScalarGridSpec(
            num_scalar_prefetch=1,
            grid=(1,),
            in_specs=[whole(next0.shape), whole(next1.shape), whole(conv_weight.shape)] + last,
            out_specs=last,
        ),
        compiler_params=params(),
        cost_estimate=cost(1, 1 << 20),
        input_output_aliases={4: 0, 5: 1, 6: 2},
    )(yv, next0, next1, conv_weight, *kept)

    def summed(*refs):
        sums_kernel(*refs, wide=xw)

    gw, gbias, gheads = call(
        summed, yv, (1,),
        [(mine, whole(mine.shape)), (theirs, whole(theirs.shape))],
        [
            (shape_of(4, bias.shape[1]), whole((4, bias.shape[1]))),
            (shape_of(1, bias.shape[1]), whole((1, bias.shape[1]))),
            (shape_of(8, 2 * hl), whole((8, 2 * hl))),
        ],
        [pltpu.VMEM((2, 8, base + xw), F32)], 1, 1 << 20, after=[grad_x, gdt],
    )

    per_dev = 2 * hl // devices
    head_total = lax.dynamic_slice(gheads, (0, me * per_dev), (3, per_dev))
    return (
        y_all[None], grad_x[None], grad_b[None], grad_c[None], gdt[None], gw, gbias[0], head_total,
    )


def solution(mesh):
    rows = P("dp", "sp", None)
    in_specs = (rows, rows, rows, rows, P(), P(), P(), P(), P(), rows)
    out_specs = (rows, rows, rows, rows, rows, P(), P(), P(None, "sp"))
    return jax.shard_map(
        per_device, mesh=mesh, in_specs=in_specs, out_specs=out_specs, check_vma=False
    )
```

```python
import jax
import jax.numpy as jnp
import numpy as np
from jax import lax
from jax.experimental import pallas as pl
from jax.experimental.pallas import tpu as pltpu
from jax.sharding import PartitionSpec as P

N = 256
Q = 128
HEAD = 64
SUB = 256
LOG2E = 1.4426950408889634
F32 = jnp.float32
BF16 = jnp.bfloat16
NEG = -1e30


def params():
    return pltpu.CompilerParams(vmem_limit_bytes=14 * 1024 * 1024)


def cost(micros, nbytes):
    return pl.CostEstimate(flops=int(micros * 1e9), bytes_accessed=nbytes, transcendentals=0)


def dot(a, b):
    return jnp.dot(a, b, preferred_element_type=F32)


def dot_tb(a, b):
    return lax.dot_general(a, b, (((1,), (1,)), ((), ())), preferred_element_type=F32)


def dot_ta(a, b):
    return lax.dot_general(a, b, (((0,), (0,)), ((), ())), preferred_element_type=F32)


def halves(v):
    hi = v.astype(BF16)
    return hi, (v - hi.astype(F32)).astype(BF16)


def split_dot(v, m):
    hi, lo = halves(v)
    return dot(hi, m) + dot(lo, m)


def exact_dot(m, v):
    hi = v.astype(BF16)
    rest = v - hi.astype(F32)
    mid = rest.astype(BF16)
    low = (rest - mid.astype(F32)).astype(BF16)
    return dot(m, hi) + dot(m, mid) + dot(m, low)


def triangle(lower):
    row = lax.broadcasted_iota(jnp.int32, (Q, Q), 0)
    col = lax.broadcasted_iota(jnp.int32, (Q, Q), 1)
    return row >= col if lower else row <= col


def in_order(y, own, rec, dst, first=0):
    rows = own.shape[0]

    @pl.when(y == 0)
    def _():
        dst[first : first + rows] = own.astype(dst.dtype)
        dst[first + rows : first + 2 * rows] = rec.astype(dst.dtype)

    @pl.when(y != 0)
    def _():
        dst[first : first + rows] = rec.astype(dst.dtype)
        dst[first + rows : first + 2 * rows] = own.astype(dst.dtype)


def conv_sum(xs, w, bias, rows):
    total = bias[...]
    for k in range(4):
        total = total + w[k : k + 1] * xs[5 + k : 5 + k + rows]
    return total


def gates(s):
    sig = 0.5 + 0.5 * jnp.tanh(0.5 * s)
    out = s * sig
    return out, sig + out * (1.0 - sig)


def conv_back(ds, xs, gs, w, rows):
    gs[0:rows] = ds
    gs[rows : rows + 8] = jnp.zeros((8, ds.shape[1]), F32)
    dx = w[3:4] * ds
    for k in range(3):
        dx = dx + w[k : k + 1] * gs[3 - k : 3 - k + rows]
    dw = [jnp.sum(ds * xs[5 + k : 5 + k + rows], axis=0, keepdims=True) for k in range(4)]
    dw.append(jnp.sum(ds, axis=0, keepdims=True))
    dw.append(jnp.zeros((3, ds.shape[1]), F32))
    return dx, jnp.concatenate(dw, axis=0)


def copies(pairs, sems):
    moves = [pltpu.make_async_copy(src, dst, sems.at[i]) for i, (src, dst) in enumerate(pairs)]
    for m in moves:
        m.start()
    for m in moves:
        m.wait()


def pack_rim_kernel(yv, x, b, c, out, xt, bt, ct, sems):
    half = x.shape[1] // 2
    width = b.shape[1] // 2
    step = 2 * width
    copies([(src.at[pl.ds(Q - 16, 16)], dst) for src, dst in ((x, xt), (b, bt), (c, ct))], sems)
    x3, b3, c3 = [r[...].astype(F32)[13:16] for r in (xt, bt, ct)]
    blocks = half // step + 1
    for k in range(2):
        items = []
        for r in range(3):
            for i in range(blocks - 1):
                at = k * half + i * step
                items.append(x3[r : r + 1, at : at + step])
            mine = slice(k * width, (k + 1) * width)
            items.append(jnp.concatenate([b3[r : r + 1, mine], c3[r : r + 1, mine]], axis=1))
        items.append(jnp.zeros((16 - 3 * blocks, step), F32))
        out[16 * k : 16 * (k + 1)] = jnp.concatenate(items, axis=0).astype(BF16)


def pack_small_kernel(yv, b, c, dt, out, sems):
    width = b.shape[1] // 2
    at = pl.multiple_of((1 - yv[0]) * width, 128)
    copies(
        [
            (b.at[:, pl.ds(at, width)], out.at[pl.ds(0, Q), pl.ds(0, width)]),
            (c.at[:, pl.ds(at, width)], out.at[pl.ds(0, Q), pl.ds(width, width)]),
            (dt, out.at[pl.ds(0, Q), pl.ds(2 * width, dt.shape[1])]),
        ],
        sems,
    )


def pack_kernel(yv, x, dy, out, sems, *, chunk, chunks):
    width = out.shape[2]
    at = pl.multiple_of(((1 - yv[0]) * chunks + chunk) * width, 128)
    copies([(x.at[:, pl.ds(at, width)], out.at[0]), (dy.at[:, pl.ds(at, width)], out.at[1])], sems)


def unpack_kernel(yv, got, y_ref, gx_ref, mark):
    y_ref[...] = got[0]
    gx_ref[...] = got[1]
    mark[...] = jnp.zeros(mark.shape, F32)


def setup_kernel(
    yv, b_own, c_own, dt_own, rec, rim, rim_e, rim_o, wb, wc, bb, bc_, par, exp2,
    halo_ref, bc_ref, cc_ref, bt_ref, ct_ref, ds_ref, fe_ref, rows_ref, cols_ref, rowt_ref, st_ref,
    xs, dts, xs2, rims,
):
    y = yv[0]
    width = b_own.shape[1]
    heads = par.shape[1]
    half = halo_ref.shape[1] - 2 * width

    @pl.when(y == 0)
    def _():
        rims[...] = rim[0:16].astype(F32)

    @pl.when((y != 0) & (yv[2] == 0))
    def _():
        rims[...] = rim_o[16:32].astype(F32)

    @pl.when((y != 0) & (yv[2] != 0))
    def _():
        rims[...] = rim_e[16:32].astype(F32)

    blocks = halo_ref.shape[1] // rim.shape[1]
    keep = jnp.where(yv[1] == 0, 0.0, 1.0)
    halo_ref[...] = keep * jnp.concatenate(
        [jnp.zeros((5, halo_ref.shape[1]), F32)]
        + [
            jnp.concatenate([rims[r * blocks + i : r * blocks + i + 1] for i in range(blocks)], axis=1)
            for r in range(3)
        ],
        axis=0,
    )
    for i, (own, w, bias, out, out_t) in enumerate(
        ((b_own, wb, bb, bc_ref, bt_ref), (c_own, wc, bc_, cc_ref, ct_ref))
    ):
        at = i * width
        xs[0:8] = halo_ref[:, half + at : half + at + width]
        in_order(y, own[...], rec[0:Q, at : at + width], xs, 8)
        v, slope = gates(conv_sum(xs, w, bias, 2 * Q))
        out[...] = v.astype(BF16)
        out_t[...] = jnp.transpose(v).astype(BF16)
        ds_ref[i] = slope

    @pl.when(y == 0)
    def _():
        dts[0:Q] = dt_own[:, 0:heads].astype(F32)
        dts[Q : 2 * Q] = rec[0:Q, 2 * width : 2 * width + heads].astype(F32)

    @pl.when(y != 0)
    def _():
        dts[0:Q] = rec[0:Q, 2 * width + heads : 2 * width + 2 * heads].astype(F32)
        dts[Q : 2 * Q] = dt_own[:, heads : 2 * heads].astype(F32)

    raw = dts[...] + par[1:2]
    step = jnp.log1p(jnp.exp(raw))
    logs = -step * jnp.exp(par[0:1])
    tri = jnp.where(triangle(True), 1.0, 0.0).astype(BF16)
    run0 = exact_dot(tri, logs[0:Q])
    run1 = exact_dot(tri, logs[Q:])
    tot0, tot1 = run0[Q - 1 : Q], run1[Q - 1 : Q]
    run = jnp.concatenate([run0, run1], axis=0)
    to_end = jnp.concatenate([jnp.exp(tot0 - run0), jnp.exp(tot1 - run1)], axis=0)
    hi, lo = halves(step * to_end)
    fe_ref[0] = jnp.concatenate([hi, lo], axis=1)
    hi, lo = halves(jnp.exp(run))
    fe_ref[1] = jnp.concatenate([hi, lo], axis=1)
    st_ref[...] = jnp.concatenate([step, raw], axis=1)
    small = jnp.concatenate(
        [jnp.exp(tot0), jnp.exp(tot1), jnp.exp(tot0 + tot1), par[2:3], jnp.zeros((4, heads), F32)],
        axis=0,
    )
    hi, lo = halves(small)
    rows_ref[...] = dot(jnp.concatenate([hi, lo], axis=1), exp2[...])
    r2 = run * LOG2E
    q2 = (run - jnp.log(step)) * LOG2E
    xs2[...] = jnp.transpose(jnp.concatenate([r2, q2], axis=1))
    for j in range(heads // 4):
        cols_ref[j] = jnp.concatenate([r2[:, 4 * j : 4 * j + 4], q2[:, 4 * j : 4 * j + 4]], axis=1)
        rowt_ref[j] = jnp.concatenate(
            [xs2[4 * j : 4 * j + 4], xs2[heads + 4 * j : heads + 4 * j + 4]], axis=0
        )


def state_kernel(
    yv, x_own, dy_own, rec, halo, w, bias, bt, ct, fe, exp2, rows,
    t_ref, u_ref, xc_ref, dyo_ref, sl_ref, xs,
):
    y = yv[0]
    xs[0:8] = halo[...]
    in_order(y, x_own[...], rec[0], xs, 8)
    in_order(y, dy_own[...], rec[1], dyo_ref)
    v, slope = gates(conv_sum(xs, w, bias, 2 * Q))
    xc = v.astype(BF16)
    xc_ref[...] = xc
    sl_ref[...] = slope.astype(BF16)
    wt = (xc.astype(F32) * dot(fe[0], exp2[...])).astype(BF16)
    dyr = (dyo_ref[...].astype(F32) * dot(fe[1], exp2[...])).astype(BF16)
    top, end = slice(0, Q), slice(Q, 2 * Q)
    t_ref[0] = (rows[1:2] * dot(bt[:, top], wt[top]) + dot(bt[:, end], wt[end])).astype(BF16)
    u_ref[0] = (dot(ct[:, top], dyr[top]) + rows[0:1] * dot(ct[:, end], dyr[end])).astype(BF16)


def hop_kernel(yv, in_e, in_o, t, u, row_f, row_b, out_e, out_o):
    row_f = row_f[2:3] * jnp.where(yv[1] == 0, 0.0, 1.0)
    row_b = row_b[2:3] * jnp.where(yv[4] == 0, 0.0, 1.0)

    @pl.when(yv[2] == 0)
    def _():
        out_e[...] = (row_f * in_o[...].astype(F32) + t[0].astype(F32)).astype(BF16)
        out_o[...] = (row_b * in_e[...].astype(F32) + u[0].astype(F32)).astype(BF16)

    @pl.when(yv[2] != 0)
    def _():
        out_o[...] = (row_f * in_e[...].astype(F32) + t[0].astype(F32)).astype(BF16)
        out_e[...] = (row_b * in_o[...].astype(F32) + u[0].astype(F32)).astype(BF16)


def within_kernel(yv, xc, dyo, cols, rowt, bc, cc, yi_ref, dxi_ref, dcb_ref, cb):
    @pl.when(pl.program_id(0) == 0)
    def _():
        dcb_ref[...] = jnp.zeros(dcb_ref.shape, F32)
        for b in range(2):
            at = slice(b * Q, b * Q + Q)
            cb[b] = dot_tb(cc[at], bc[at])
            cb[2 + b] = dot_tb(bc[at], cc[at])

    low = triangle(True)
    high = triangle(False)
    lane = lax.broadcasted_iota(jnp.int32, (1, 2 * HEAD), 1)
    first = jnp.where(lane < HEAD, 1.0, 0.0).astype(BF16)
    second = jnp.where(lane < HEAD, 0.0, 1.0).astype(BF16)
    for b in range(2):
        at = slice(b * Q, b * Q + Q)
        dcb = dcb_ref[b]
        for p in range(2):
            ls = slice(p * 2 * HEAD, (p + 1) * 2 * HEAD)
            xp = xc[at, ls]
            dyp = dyo[at, ls]
            xbd = jnp.concatenate([xp * first, xp * second], axis=0)
            dbd = jnp.concatenate([dyp * first, dyp * second], axis=0)
            decay, mix, mixt = [], [], []
            for i in range(2):
                h = 2 * p + i
                ex = cols[0, at, h : h + 1] - rowt[0, 4 + h : 5 + h, at]
                lt = jnp.exp2(jnp.where(low, ex, NEG))
                ext = rowt[0, h : h + 1, at] - cols[0, at, 4 + h : 5 + h]
                ltt = jnp.exp2(jnp.where(high, ext, NEG))
                decay.append(lt)
                mix.append((cb[b] * lt).astype(BF16))
                mixt.append((cb[2 + b] * ltt).astype(BF16))
            yi_ref[at, ls] = dot(jnp.concatenate(mix, axis=1), xbd)
            dxi_ref[at, ls] = dot(jnp.concatenate(mixt, axis=1), dbd)
            dm = dot_tb(dyp, xbd)
            dcb = dcb + dm[:, 0:Q] * decay[0] + dm[:, Q:] * decay[1]
        dcb_ref[b] = dcb


def fetch(spot, choices, dst, sem):
    @pl.when(spot == 0)
    def _():
        dst[...] = jnp.zeros(dst.shape, dst.dtype)

    for k, src in enumerate(choices, 1):

        @pl.when(spot == k)
        def _():
            copy = pltpu.make_async_copy(src, dst, sem)
            copy.start()
            copy.wait()


def across_kernel(
    yv, x_own, rec, halo, w, xc, dyo, sl, yi, dxi, bc, cc, bt, ct, fe, exp2, seg, rows, *rest
):
    hops = (len(rest) - 16) // 2
    (y_ref, gx_ref, red_ref, head_ref, send_ref, dc_ref, db_ref, wv_ref, ends_ref) = rest[2 * hops : -7]
    xs, gs, gy, ent, lea, sem0, sem1 = rest[-7:]
    y = yv[0]

    @pl.when(pl.program_id(0) == 0)
    def _():
        dc_ref[...] = jnp.zeros(dc_ref.shape, F32)
        db_ref[...] = jnp.zeros(db_ref.shape, F32)
        wv_ref[...] = jnp.zeros(wv_ref.shape, F32)
        fetch(yv[1], rest[:hops], ent, sem0)
        fetch(hops - yv[1], rest[hops : 2 * hops], lea, sem1)

    at = pl.multiple_of(pl.program_id(0) * SUB, SUB)
    xs[0:8] = halo[...]
    in_order(y, x_own[...], rec[0], xs, 8)
    x = xc[...].astype(F32)
    dy = dyo[...].astype(F32)
    f = dot(fe[0], exp2[...])
    er = dot(fe[1], exp2[...])
    wt = (x * f).astype(BF16)
    dyr = (dy * er).astype(BF16)
    d0, d1, skip = rows[0:1], rows[1:2], rows[3:4]
    top, end = slice(0, Q), slice(Q, 2 * Q)
    e0 = ent[:, pl.ds(at, SUB)]
    r1 = lea[:, pl.ds(at, SUB)]
    e1 = (d0 * e0.astype(F32) + dot(bt[:, top], wt[top])).astype(BF16)
    r0 = (d1 * r1.astype(F32) + dot(ct[:, end], dyr[end])).astype(BF16)
    over = jnp.concatenate([dot(cc[top], e0), dot(cc[end], e1)], axis=0) * er
    back = jnp.concatenate([dot(bc[top], r0), dot(bc[end], r1)], axis=0) * f
    yn = yi[...] + over
    dxn = dxi[...] + back
    dc_ref[top] += dot_tb(dyr[top], e0)
    dc_ref[end] += dot_tb(dyr[end], e1)
    db_ref[top] += dot_tb(wt[top], r0)
    db_ref[end] += dot_tb(wt[end], r1)
    wv_ref[0] += split_dot(dy * yn, seg[...])
    wv_ref[1] += split_dot(x * dxn, seg[...])
    xb = x * back
    ends_ref[...] = jnp.concatenate(
        [
            jnp.sum(xb[top], axis=0, keepdims=True)
            + d0 * jnp.sum(r0.astype(F32) * e0.astype(F32), axis=0, keepdims=True),
            jnp.sum(xb[end], axis=0, keepdims=True)
            + d1 * jnp.sum(r1.astype(F32) * e1.astype(F32), axis=0, keepdims=True),
            jnp.sum(x * dy, axis=0, keepdims=True),
            jnp.zeros((5, SUB), F32),
        ],
        axis=0,
    )
    ds = (dxn + skip * dy) * sl[...].astype(F32)
    gx, dw = conv_back(ds, xs, gs, w, 2 * Q)
    red_ref[...] = dw
    head_ref[...] = ds[0:8]
    gy[0] = (yn + skip * x).astype(BF16)
    gy[1] = gx.astype(BF16)

    @pl.when(y == 0)
    def _():
        y_ref[...] = gy[0, top]
        gx_ref[...] = gy[1, top]
        send_ref[...] = gy[:, end]

    @pl.when(y != 0)
    def _():
        y_ref[...] = gy[0, end]
        gx_ref[...] = gy[1, end]
        send_ref[...] = gy[:, top]


def finish_group(
    yv, b_own, c_own, b_rec, c_rec, b_halo, c_halo, wb, wc, slope, bc, cc, parts,
    gb_ref, gc_ref, red_ref, head_ref, send_ref, xs, gs, gv,
):
    y = yv[0]
    dc, db, dcb = [sum(r[...] for r in refs[1:]) + refs[0][...] for refs in zip(*parts)]
    dcb = dcb.astype(BF16)
    for b in range(2):
        at = slice(b * Q, b * Q + Q)
        gv[0, at] = db[at] + dot_ta(dcb[b], cc[at])
        gv[1, at] = dc[at] + dot(dcb[b], bc[at])
    for i, (own, rec, halo, w, out) in enumerate(
        ((b_own, b_rec, b_halo, wb, gb_ref), (c_own, c_rec, c_halo, wc, gc_ref))
    ):
        cs = slice(i * N, (i + 1) * N)
        xs[0:8] = halo[...]
        in_order(y, own[...], rec[...], xs, 8)
        ds = gv[i] * slope[i]
        gx, dw = conv_back(ds, xs, gs, w, 2 * Q)
        red_ref[:, cs] = dw
        head_ref[:, cs] = ds[0:8]

        @pl.when(y == 0)
        def _():
            out[...] = gx[0:Q].astype(BF16)
            send_ref[:, cs] = gx[Q:].astype(BF16)

        @pl.when(y != 0)
        def _():
            out[...] = gx[Q:].astype(BF16)
            send_ref[:, cs] = gx[0:Q].astype(BF16)


def finish_kernel(
    yv, b_own, c_own, b_rec, c_rec, b_halo, c_halo, wb, wc, slope, bc, cc,
    dc0, db0, dcb0, dc1, db1, dcb1,
    gb_ref, gc_ref, red_ref, head_ref, send_ref, xs, gs, gv,
):
    finish_group(
        yv, b_own, c_own, b_rec, c_rec, b_halo, c_halo, wb, wc, slope, bc, cc,
        [(dc0, db0, dcb0), (dc1, db1, dcb1)],
        gb_ref, gc_ref, red_ref, head_ref, send_ref, xs, gs, gv,
    )
    red_ref[:, 2 * N :] = jnp.zeros((8, red_ref.shape[1] - 2 * N), F32)
    head_ref[:, 2 * N :] = jnp.zeros((8, head_ref.shape[1] - 2 * N), F32)


def finish_last_kernel(
    yv, b_own, c_own, b_rec, c_rec, b_halo, c_halo, wb, wc, slope, bc, cc,
    dc0, db0, dcb0, dc1, db1, dcb1, st, par, seg, heads_before, *rest,
):
    chunks = (len(rest) - 11) // 2
    wvs, ends, rest = rest[:chunks], rest[chunks : 2 * chunks], rest[2 * chunks :]
    gb_ref, gc_ref, red_ref, head_ref, send_ref, gdt_ref, next_ref, xs, gs, gv, gd = rest
    y = yv[0]
    finish_group(
        yv, b_own, c_own, b_rec, c_rec, b_halo, c_halo, wb, wc, slope, bc, cc,
        [(dc0, db0, dcb0), (dc1, db1, dcb1)],
        gb_ref, gc_ref, red_ref, head_ref, send_ref, xs, gs, gv,
    )
    heads = par.shape[1]
    step, raw = st[:, 0:heads], st[:, heads:]
    rate = jnp.exp(par[0:1])
    cw = ends[0].shape[1]
    w_sum = sum(wv[0] for wv in wvs[1:]) + wvs[0][0]
    v_sum = sum(wv[1] for wv in wvs[1:]) + wvs[0][1]
    e_sum = split_dot(ends[0][...], seg[0:cw])
    for i in range(1, chunks):
        e_sum = e_sum + split_dot(ends[i][...], seg[i * cw : (i + 1) * cw])
    tri = jnp.where(triangle(False), 1.0, 0.0).astype(BF16)
    diff = w_sum - v_sum
    dl = jnp.concatenate(
        [exact_dot(tri, diff[0:Q]) + e_sum[0:1], exact_dot(tri, diff[Q:]) + e_sum[1:2]], axis=0
    )
    draw = (v_sum / step - rate * dl) / (1.0 + jnp.exp(-raw))
    red_ref[:, 2 * N :] = jnp.concatenate(
        [
            jnp.concatenate(
                [
                    jnp.sum(dl * (-rate * step), axis=0, keepdims=True),
                    jnp.sum(draw, axis=0, keepdims=True),
                    e_sum[2:3],
                    jnp.zeros((5, heads), F32),
                ],
                axis=0,
            ),
            jnp.zeros((8, red_ref.shape[1] - 2 * N - heads), F32),
        ],
        axis=1,
    )
    head_ref[:, 2 * N :] = jnp.zeros((8, head_ref.shape[1] - 2 * N), F32)
    piece = head_ref.shape[1]
    items = []
    for r in range(3):
        row = slice(r, r + 1)
        items += [heads_before[row, 2 * piece + i * cw : 2 * piece + (i + 1) * cw] for i in range(chunks)]
        items.append(
            jnp.concatenate(
                [
                    heads_before[row, 0:N], head_ref[row, 0:N],
                    heads_before[row, N : 2 * N], head_ref[row, N : 2 * N],
                ],
                axis=1,
            )
        )
    items.append(jnp.zeros((16 - 3 * (chunks + 1), cw), F32))
    next_ref[...] = jnp.concatenate(items, axis=0)
    gd[...] = jnp.concatenate([draw, draw], axis=1).astype(BF16)

    @pl.when(y == 0)
    def _():
        gdt_ref[...] = gd[0:Q]
        send_ref[:, 2 * N :] = gd[Q:]

    @pl.when(y != 0)
    def _():
        gdt_ref[...] = gd[Q:]
        send_ref[:, 2 * N :] = gd[0:Q]


def add_kernel(yv, *refs):
    total = refs[0][...]
    for r in refs[1:-1]:
        total = total + r[...]
    refs[-1][...] = total


def join_kernel(yv, first, second, out):
    out[0] = first[...]
    out[1] = second[...]


def close_kernel(yv, got0, got1, gdt_own, gb_ref, gc_ref, gdt_ref):
    at = [got0, got1]
    for g in range(2):
        gb_ref[:, g * N : (g + 1) * N] = at[g][:, 0:N]
        gc_ref[:, g * N : (g + 1) * N] = at[g][:, N : 2 * N]
    lane = lax.broadcasted_iota(jnp.int32, gdt_own.shape, 1)
    low = lane < gdt_own.shape[1] // 2
    own, got = gdt_own[...].astype(F32), got1[:, 2 * N :].astype(F32)

    @pl.when(yv[0] == 0)
    def _():
        gdt_ref[...] = jnp.where(low, own, got).astype(BF16)

    @pl.when(yv[0] != 0)
    def _():
        gdt_ref[...] = jnp.where(low, got, own).astype(BF16)


def rim_kernel(yv, next0, next_e, next_o, w, gx, gb, gc, gx_ref, gb_ref, gc_ref, mark, both):
    mark[...] = jnp.zeros(mark.shape, F32)
    both[0] = next0[...]

    @pl.when(yv[2] == 0)
    def _():
        both[1] = next_e[...]

    @pl.when(yv[2] != 0)
    def _():
        both[1] = next_o[...]

    step = next0.shape[1]
    blocks = gx.shape[1] // 2 // step
    keep = jnp.where((yv[0] == 0) | (yv[4] == 0), 0.0, 1.0)

    def add(src, dst, lo, half, block, at, width, to):
        h = [keep * both[half, r * (blocks + 1) + block : r * (blocks + 1) + block + 1, at : at + width] for r in range(3)]
        k = w[:, lo : lo + width]
        more = jnp.concatenate(
            [
                jnp.zeros((13, width), F32),
                k[0:1] * h[0],
                k[0:1] * h[1] + k[1:2] * h[0],
                k[0:1] * h[2] + k[1:2] * h[1] + k[2:3] * h[0],
            ],
            axis=0,
        )
        dst[:, to : to + width] = (src[:, to : to + width].astype(F32) + more).astype(BF16)

    for half in range(2):
        for i in range(blocks):
            at = (half * blocks + i) * step
            add(gx, gx_ref, at, half, i, 0, step, at)
        for i, (src, dst) in enumerate(((gb, gb_ref), (gc, gc_ref))):
            to = half * step // 2
            add(src, dst, (2 * blocks + i) * step + to, half, blocks, i * step // 2, step // 2, to)


def sums_kernel(yv, mine, theirs, gw_ref, gb_ref, gh_ref, both, *, wide, heads):
    width = mine.shape[2]

    @pl.when(yv[3] == 0)
    def _():
        both[:, :, 0:width] = mine[...]
        both[:, :, width:] = theirs[...]

    @pl.when(yv[3] != 0)
    def _():
        both[:, :, 0:width] = theirs[...]
        both[:, :, width:] = mine[...]

    base = 2 * width - wide
    step = base // 2

    def fill(order):
        for k in range(2):
            v = both[order[k]]
            gw_ref[:, k * wide : (k + 1) * wide] = v[0:4, base:]
            gb_ref[:, k * wide : (k + 1) * wide] = v[4:5, base:]
            for i in range(2):
                for g in range(2):
                    to = 2 * wide + i * 4 * N + (2 * k + g) * N
                    gw_ref[:, to : to + N] = v[0:4, g * step + i * N : g * step + (i + 1) * N]
                    gb_ref[:, to : to + N] = v[4:5, g * step + i * N : g * step + (i + 1) * N]
        at = step + 2 * N
        values = jnp.concatenate(
            [both[order[0]][:, at : at + heads], both[order[1]][:, at : at + heads]], axis=1
        )
        per_dev = gh_ref.shape[1]
        row = lax.broadcasted_iota(jnp.int32, (2 * heads, per_dev), 0)
        col = lax.broadcasted_iota(jnp.int32, (2 * heads, per_dev), 1)
        pick = jnp.where(row == col + yv[5] * per_dev, 1.0, 0.0).astype(BF16)
        hi = values.astype(BF16)
        rest = values - hi.astype(F32)
        mid = rest.astype(BF16)
        low = (rest - mid.astype(F32)).astype(BF16)
        gh_ref[...] = (dot(hi, pick) + dot(mid, pick) + dot(low, pick))[0:3]

    @pl.when(yv[0] == 0)
    def _():
        fill((0, 1))

    @pl.when(yv[0] != 0)
    def _():
        fill((1, 0))


def whole(shape):
    return pl.BlockSpec(shape, lambda *_: (0,) * len(shape))


def shape_of(*dims, dtype=F32):
    return jax.ShapeDtypeStruct(dims, dtype)


def call(kernel, yv, grid, ins, outs, scratch, micros, nbytes, keep=(), after=()):
    count = len(ins)
    extra = len(keep) + len(after)

    def run(yr, *refs):
        kernel(yr, *refs[:count], *refs[count + extra :])

    anywhere = pl.BlockSpec(memory_space=pl.ANY)
    return pl.pallas_call(
        run,
        out_shape=[o[0] for o in outs],
        grid_spec=pltpu.PrefetchScalarGridSpec(
            num_scalar_prefetch=1,
            grid=grid,
            in_specs=[i[1] for i in ins] + [anywhere] * extra,
            out_specs=[o[1] for o in outs],
            scratch_shapes=scratch,
        ),
        compiler_params=params(),
        cost_estimate=cost(micros, nbytes),
        input_output_aliases={1 + count + k: k for k in range(len(keep))},
    )(yv, *[i[0] for i in ins], *keep, *after)


def per_device(
    ssm_input, b_input, c_input, dt_input, conv_weight, conv_bias, a_log, dt_bias, skip_gain, grad_out
):
    x_rows, b_rows, c_rows = ssm_input[0], b_input[0], c_input[0]
    dt_rows, dy_rows = dt_input[0], grad_out[0]
    devices = lax.axis_size("sp")
    dp_size = lax.axis_size("dp")
    spots = devices // 2
    me = lax.axis_index("sp")
    y = lax.rem(me, 2)
    z = me // 2
    core = lax.rem(lax.axis_index("dp"), 2)
    yv = jnp.stack([y, z, lax.rem(z, 2), core, spots - 1 - z, me]).astype(jnp.int32)
    xw = x_rows.shape[1] // 2
    bw = b_rows.shape[1] // 2
    hl = dt_rows.shape[1] // 2
    chunks = 4
    cw = xw // chunks
    subs = cw // SUB
    groups = bw // N
    per_group = chunks // groups
    two = 2 * Q
    piece = 2 * N + 2 * hl
    base = groups * piece
    bands = base // SUB
    bias = conv_bias[None]

    def pairs(fn, n=devices):
        return [(i, fn(i)) for i in range(n) if fn(i) is not None and 0 <= fn(i) < n]

    swap = pairs(lambda i: i ^ 1)

    def cols(width, other, step=1, plus=0):
        if other:
            return pl.BlockSpec((Q, width), lambda j, yr: (0, (1 - yr[0]) * step + plus))
        return pl.BlockSpec((Q, width), lambda j, yr: (0, yr[0] * step + plus))

    def joint(v, fn):
        moves = []
        for d in range(dp_size):
            for i in range(devices):
                to = fn(i)
                if to is None or not 0 <= to < devices:
                    moves.append((d * devices + i, (d ^ 1) * devices + i))
                else:
                    moves.append((d * devices + i, d * devices + to))
        return lax.ppermute(v, ("dp", "sp"), moves)

    def slant(i):
        return i + 1 if i % 2 else i - 1

    def evens(i):
        return i ^ 2

    def odds(i):
        return ((i + 2) ^ 2) - 2 if 2 <= i < devices - 2 else None

    in_hbm = pl.BlockSpec(memory_space=pltpu.MemorySpace.HBM)
    anywhere = pl.BlockSpec(memory_space=pl.ANY)
    (msg,) = call(
        pack_small_kernel, yv, (1,), [(b_rows, in_hbm), (c_rows, in_hbm), (dt_rows, in_hbm)],
        [(shape_of(Q, 2 * bw + 2 * hl, dtype=BF16), anywhere)],
        [pltpu.SemaphoreType.DMA((3,))], 1, 1 << 20,
    )
    rec_bc = lax.ppermute(msg, "sp", swap)
    (rim_out,) = call(
        pack_rim_kernel, yv, (1,), [(x_rows, in_hbm), (b_rows, in_hbm), (c_rows, in_hbm)],
        [(shape_of(32, 2 * bw, dtype=BF16), whole((32, 2 * bw)))],
        [
            pltpu.VMEM((16, 2 * xw), BF16), pltpu.VMEM((16, 2 * bw), BF16),
            pltpu.VMEM((16, 2 * bw), BF16), pltpu.SemaphoreType.DMA((3,)),
        ],
        1, 1 << 20, after=[msg],
    )
    rim = joint(rim_out, slant)
    rim_e = joint(rim_out, evens)
    rim_o = joint(rim_out, odds)
    rec = []

    def send_chunk(c, after):
        def kernel(*refs):
            pack_kernel(*refs, chunk=c, chunks=chunks)

        (out,) = call(
            kernel, yv, (1,), [(x_rows, in_hbm), (dy_rows, in_hbm)],
            [(shape_of(2, Q, cw, dtype=BF16), anywhere)],
            [pltpu.SemaphoreType.DMA((2,))], 1, 1 << 20, after=after,
        )
        rec.append(lax.ppermute(out, "sp", swap))
        return out

    send_chunk(0, [rim_out])

    par = lax.dynamic_slice_in_dim(
        jnp.concatenate([jnp.stack([a_log, dt_bias, skip_gain]), jnp.zeros((5, 2 * hl), F32)], 0),
        y * hl, hl, 1,
    )
    lanes = np.arange(xw) // HEAD
    expand = (np.arange(hl)[:, None] == lanes[None, :]).astype(BF16)
    exp2 = jnp.asarray(np.concatenate([expand, expand], axis=0))
    seg = jnp.asarray(np.ascontiguousarray(expand.T))

    nq = hl // 4
    first_b, first_c = 2 * xw // bw, 2 * xw // bw + 2

    def wide_w(rows_, at):
        return pl.BlockSpec((rows_, bw), lambda j, yr: (0, at + yr[0]))

    halo, bcc, ccc, bct, cct, slopes, fe, rows, qcols, rowt, st = call(
        setup_kernel, yv, (1,),
        [
            (b_rows, cols(bw, False)), (c_rows, cols(bw, False)), (dt_rows, whole(dt_rows.shape)),
            (rec_bc, whole(rec_bc.shape)), (rim, whole(rim.shape)), (rim_e, whole(rim.shape)), (rim_o, whole(rim.shape)),
            (conv_weight, wide_w(4, first_b)), (conv_weight, wide_w(4, first_c)),
            (bias, wide_w(1, first_b)), (bias, wide_w(1, first_c)),
            (par, whole((8, hl))), (exp2, whole((2 * hl, xw))),
        ],
        [
            (shape_of(8, xw + 2 * bw), whole((8, xw + 2 * bw))),
            (shape_of(two, bw, dtype=BF16), whole((two, bw))),
            (shape_of(two, bw, dtype=BF16), whole((two, bw))),
            (shape_of(bw, two, dtype=BF16), whole((bw, two))),
            (shape_of(bw, two, dtype=BF16), whole((bw, two))),
            (shape_of(2, two, bw), whole((2, two, bw))),
            (shape_of(2, two, 2 * hl, dtype=BF16), whole((2, two, 2 * hl))),
            (shape_of(8, xw), whole((8, xw))),
            (shape_of(nq, two, 8), whole((nq, two, 8))),
            (shape_of(nq, 8, two), whole((nq, 8, two))),
            (shape_of(two, 2 * hl), whole((two, 2 * hl))),
        ],
        [
            pltpu.VMEM((two + 8, bw), F32), pltpu.VMEM((two, hl), F32),
            pltpu.VMEM((2 * hl, two), F32), pltpu.VMEM((16, rim.shape[1]), F32),
        ],
        4, 4 << 20,
    )
    send_chunk(1, [rec_bc])

    def own(c):
        return pl.BlockSpec((Q, SUB), lambda j, yr: (0, (yr[0] * chunks + c) * subs + j))

    def weight(rows_, c):
        return pl.BlockSpec((rows_, SUB), lambda j, yr: (0, (yr[0] * chunks + c) * subs + j))

    def band(rows_, c, first=0):
        return pl.BlockSpec((rows_, SUB), lambda j, yr: (0, first + c * subs + j))

    def group(c):
        return pl.BlockSpec((two, N), lambda j, yr: (0, c // per_group))

    def group_t(c):
        return pl.BlockSpec((N, two), lambda j, yr: (c // per_group, 0))

    local = pl.BlockSpec((two, SUB), lambda j, yr: (0, j))
    local8 = pl.BlockSpec((8, SUB), lambda j, yr: (0, j))
    wave = pl.BlockSpec((N, SUB), lambda j, yr: (0, j))
    arrived = pl.BlockSpec((2, Q, SUB), lambda j, yr: (0, 0, j))

    states = []
    xcs, dyos, sls = [], [], []

    def state(c, after):
        nonlocal states
        slot = pl.BlockSpec((1, N, SUB), lambda j, yr: (c, 0, j))
        big = shape_of(chunks, N, cw, dtype=BF16)
        tall = shape_of(two, cw, dtype=BF16)
        t, u, xc, dyo, sl = call(
            state_kernel, yv, (subs,),
            [
                (x_rows, own(c)), (dy_rows, own(c)), (rec[c], arrived), (halo, band(8, c)),
                (conv_weight, weight(4, c)), (bias, weight(1, c)), (bct, group_t(c)),
                (cct, group_t(c)), (fe, whole(fe.shape)), (exp2, band(2 * hl, c)), (rows, band(8, c)),
            ],
            [(big, slot), (big, slot), (tall, local), (tall, local), (tall, local)],
            [pltpu.VMEM((two + 8, SUB), F32)],
            3, 4 << 20, keep=states, after=after,
        )
        states = [t, u]
        xcs.append(xc)
        dyos.append(dyo)
        sls.append(sl)
        return xc

    yis, dxis, dcbs = [], [], []

    def within(c, after):
        yi, dxi, dcb = call(
            within_kernel, yv, (subs,),
            [
                (xcs[c], local), (dyos[c], local),
                (qcols, pl.BlockSpec((1, two, 8), lambda j, yr: (c * subs + j, 0, 0))),
                (rowt, pl.BlockSpec((1, 8, two), lambda j, yr: (c * subs + j, 0, 0))),
                (bcc, group(c)), (ccc, group(c)),
            ],
            [
                (shape_of(two, cw), local), (shape_of(two, cw), local),
                (shape_of(2, Q, Q), whole((2, Q, Q))),
            ],
            [pltpu.VMEM((4, Q, Q), F32)],
            3, 4 << 20, after=after,
        )
        yis.append(yi)
        dxis.append(dxi)
        dcbs.append(dcb)
        return dcb

    finals = []
    sums = []
    got_x = []

    def across(c, ents, leas, after):
        nonlocal finals
        full = shape_of(Q, 2 * xw, dtype=BF16)
        strip = shape_of(8, base + xw)
        out = call(
            across_kernel, yv, (subs,),
            [
                (x_rows, own(c)), (rec[c], pl.BlockSpec((1, Q, SUB), lambda j, yr: (0, 0, j))),
                (halo, band(8, c)), (conv_weight, weight(4, c)), (xcs[c], local), (dyos[c], local),
                (sls[c], local), (yis[c], local), (dxis[c], local),
                (bcc, group(c)), (ccc, group(c)), (bct, group_t(c)), (cct, group_t(c)),
                (fe, whole(fe.shape)), (exp2, band(2 * hl, c)),
                (seg, pl.BlockSpec((SUB, hl), lambda j, yr: (c * subs + j, 0))), (rows, band(8, c)),
            ] + [(v, pl.BlockSpec(memory_space=pl.ANY)) for v in ents + leas],
            [
                (full, own(c)), (full, own(c)), (strip, band(8, c, bands)), (strip, band(8, c, bands)),
                (shape_of(2, Q, cw, dtype=BF16), arrived), (shape_of(two, N), whole((two, N))),
                (shape_of(two, N), whole((two, N))), (shape_of(2, two, hl), whole((2, two, hl))),
                (shape_of(8, cw), local8),
            ],
            [
                pltpu.VMEM((two + 8, SUB), F32), pltpu.VMEM((two + 8, SUB), F32),
                pltpu.VMEM((2, two, SUB), BF16), pltpu.VMEM((N, cw), BF16), pltpu.VMEM((N, cw), BF16),
                pltpu.SemaphoreType.DMA, pltpu.SemaphoreType.DMA,
            ],
            6, 6 << 20, keep=finals, after=after,
        )
        finals = list(out[:4])
        sums.append(out[5:])
        got_x.append(lax.ppermute(out[4], "sp", swap))
        return out[8]

    def unpack(c, after):
        full = shape_of(Q, 2 * xw, dtype=BF16)
        *finals[:2], mark = call(
            unpack_kernel, yv, (1,),
            [(got_x[c], whole((2, Q, cw)))],
            [
                (full, cols(cw, True, chunks, c)), (full, cols(cw, True, chunks, c)),
                (shape_of(8, 128), whole((8, 128))),
            ],
            [], 1, 1 << 20, keep=finals[:2], after=after,
        )
        return mark

    grads_bc = []

    def finish(g, last, after):
        nonlocal grads_bc
        full = shape_of(Q, 2 * bw, dtype=BF16)
        strip = shape_of(8, base + xw)

        def wg(at):
            return pl.BlockSpec((4, N), lambda j, yr: (0, (2 * xw + at) // N + yr[0] * groups + g))

        def rec_at(at):
            return pl.BlockSpec((Q, N), lambda j, yr: (0, at // N + g))

        def halo_at(at):
            return pl.BlockSpec((8, N), lambda j, yr: (0, (xw + at) // N + g))

        tok_own = cols(N, False, groups, g)
        ins = [
            (b_rows, tok_own), (c_rows, tok_own), (rec_bc, rec_at(0)), (rec_bc, rec_at(bw)),
            (halo, halo_at(0)), (halo, halo_at(bw)), (conv_weight, wg(0)), (conv_weight, wg(2 * bw)),
            (slopes, pl.BlockSpec((2, two, N), lambda j, yr: (0, 0, g))),
            (bcc, pl.BlockSpec((two, N), lambda j, yr: (0, g))),
            (ccc, pl.BlockSpec((two, N), lambda j, yr: (0, g))),
        ]
        for c in range(g * per_group, (g + 1) * per_group):
            ins += [
                (sums[c][0], whole((two, N))), (sums[c][1], whole((two, N))),
                (dcbs[c], whole((2, Q, Q))),
            ]
        place = pl.BlockSpec((8, piece), lambda j, yr: (0, g))
        send_w = piece if last else 2 * N
        outs = [
            (strip, place), (strip, place), (full, tok_own), (full, tok_own),
            (shape_of(Q, send_w, dtype=BF16), whole((Q, send_w))),
        ]
        scratch = [
            pltpu.VMEM((two + 8, N), F32), pltpu.VMEM((two + 8, N), F32), pltpu.VMEM((2, two, N), F32),
        ]
        if last:
            ins += [(st, whole(st.shape)), (par, whole(par.shape)), (seg, whole(seg.shape))]
            ins.append((finals[3], whole(finals[3].shape)))
            ins += [(s[2], whole(s[2].shape)) for s in sums]
            ins += [(s[3], whole(s[3].shape)) for s in sums]
            outs.append((shape_of(Q, 2 * hl, dtype=BF16), whole((Q, 2 * hl))))
            outs.append((shape_of(16, cw), whole((16, cw))))
            scratch.append(pltpu.VMEM((two, 2 * hl), BF16))
        kernel = finish_last_kernel if last else finish_kernel
        count = len(ins)

        def reordered(yr, *refs):
            red, head, gb, gc = refs[count : count + 4]
            kernel(yr, *refs[:count], gb, gc, red, head, *refs[count + 4 :])

        out = call(
            reordered, yv, (1,), ins, outs, scratch, 3, 4 << 20,
            keep=finals[2:4] + grads_bc, after=after,
        )
        finals[2:4] = out[:2]
        grads_bc = list(out[2:4])
        return lax.ppermute(out[4], "sp", swap), out[4:]

    zero = jnp.zeros((N, cw), BF16)
    in_e, in_o = zero, zero
    ins_e, ins_o = [], []
    steps = chunks + spots - 2
    state(0, [])
    send_chunk(2, [rec[0]])
    got_bc = []
    waits = []
    for t in range(steps + 1):
        if t:
            ins_e.append(in_e)
            ins_o.append(in_o)
        token = []
        if t < steps:

            def slot(back):
                def at(j, yr):
                    c = t - (spots - 1 - yr[1] if back else yr[1])
                    return (jnp.clip(c, 0, chunks - 1), 0, j)

                return pl.BlockSpec((1, N, SUB), at)

            def slot_row(back):
                def at(j, yr):
                    c = t - (spots - 1 - yr[1] if back else yr[1])
                    return (0, jnp.clip(c, 0, chunks - 1) * subs + j)

                return pl.BlockSpec((8, SUB), at)

            moving = shape_of(N, cw, dtype=BF16)
            out_e, out_o = call(
                hop_kernel, yv, (subs,),
                [
                    (in_e, wave), (in_o, wave), (states[0], slot(False)), (states[1], slot(True)),
                    (rows, slot_row(False)), (rows, slot_row(True)),
                ],
                [(moving, wave), (moving, wave)],
                [], 1, 3 << 20, after=waits,
            )
            token = [out_e]
            in_e = joint(out_e, evens)
            in_o = joint(out_o, odds)
        waits = []
        if t + 1 < chunks:
            waits.append(state(t + 1, token))
            if t + 3 < chunks:
                send_chunk(t + 3, [rec[t + 1]])
        if t < chunks:
            waits.append(within(t, token))
        c = t + 1 - spots
        if 0 <= c < chunks:
            ents = [(ins_o if k % 2 == 0 else ins_e)[c + k - 1] for k in range(1, spots)]
            leas = [(ins_o if (spots - 1 - k) % 2 else ins_e)[c + k - 1] for k in range(1, spots)]
            waits.append(across(c, ents, leas, token))
            if c == chunks - 2:
                mark = unpack(0, token)
                got, tok = finish(0, False, token)
                got_bc.append(got)
                waits += [tok[0], mark]
    got, (_, gdt_own, next_rows) = finish(1, True, [])
    got_bc.append(got)
    red = finals[2]

    hw = (base + xw) // 2
    slab = shape_of(8, hw)

    def side(other):
        if other:
            return pl.BlockSpec((8, hw), lambda j, yr: (0, 1 - yr[3]))
        return pl.BlockSpec((8, hw), lambda j, yr: (0, yr[3]))

    def add(items, after=()):
        (out,) = call(
            add_kernel, yv, (1,), items, [(slab, whole((8, hw)))], [], 1, 1 << 20, after=after
        )
        return out

    theirs = add([(red, side(True))])
    mine = add([(red, side(False)), (lax.ppermute(theirs, "dp", pairs(lambda i: i ^ 1, dp_size)), whole((8, hw)))])
    size = 2
    while size < dp_size:
        got = lax.ppermute(mine, "dp", pairs(lambda i: i ^ size, dp_size))
        marks = []
        if size == 2:
            marks = [unpack(1, [mine]), unpack(2, [mine])]
        mine = add([(mine, whole((8, hw))), (got, whole((8, hw)))], marks)
        size *= 2
    mark = unpack(3, [mine])
    y_all, gx_all = finals[:2]
    size = 2
    while size < devices:
        ways = 4 if size * 4 <= devices else 2
        got = [lax.ppermute(mine, "sp", pairs(lambda i: i ^ (size * k))) for k in range(1, ways)]
        size *= ways
        mine = add([(v, whole((8, hw))) for v in [mine] + got], [mark] if size >= devices else [])
    got_y = lax.ppermute(mine, "sp", swap)

    next0 = joint(next_rows, slant)
    next_e = joint(next_rows, evens)
    next_o = joint(next_rows, odds)
    full = shape_of(Q, 2 * bw, dtype=BF16)
    gb, gc, gdt = call(
        close_kernel, yv, (1,),
        [
            (got_bc[0], whole(got_bc[0].shape)), (got_bc[1], whole(got_bc[1].shape)),
            (gdt_own, whole(gdt_own.shape)),
        ],
        [
            (full, cols(bw, True)), (full, cols(bw, True)),
            (shape_of(Q, 2 * hl, dtype=BF16), whole((Q, 2 * hl))),
        ],
        [], 1, 1 << 20, keep=grads_bc, after=[mine],
    )
    (mine,) = call(
        join_kernel, yv, (1,), [(mine, whole((8, hw))), (got_y, whole((8, hw)))],
        [(shape_of(2, 8, hw), whole((2, 8, hw)))], [], 1, 1 << 20, after=[gdt],
    )
    theirs = lax.ppermute(mine, "dp", pairs(lambda i: i ^ 1, dp_size))
    last = [pl.BlockSpec((16, v.shape[1]), lambda j, yr: (Q // 16 - 1, 0)) for v in (gx_all, gb, gc)]
    kept = [gx_all, gb, gc]
    grad_x, grad_b, grad_c, mark = pl.pallas_call(
        rim_kernel,
        out_shape=[shape_of(*v.shape, dtype=BF16) for v in kept] + [shape_of(8, 128)],
        grid_spec=pltpu.PrefetchScalarGridSpec(
            num_scalar_prefetch=1,
            grid=(1,),
            in_specs=[whole(next0.shape)] * 3 + [whole(conv_weight.shape)] + last,
            out_specs=last + [whole((8, 128))],
            scratch_shapes=[pltpu.VMEM((2, 16, cw), F32)],
        ),
        compiler_params=params(),
        cost_estimate=cost(1, 1 << 20),
        input_output_aliases={5: 0, 6: 1, 7: 2},
    )(yv, next0, next_e, next_o, conv_weight, *kept)

    per_dev = 2 * hl // devices

    def summed(*refs):
        sums_kernel(*refs, wide=xw, heads=hl)

    gw, gbias, gheads = call(
        summed, yv, (1,),
        [(mine, whole(mine.shape)), (theirs, whole(theirs.shape))],
        [
            (shape_of(4, bias.shape[1]), whole((4, bias.shape[1]))),
            (shape_of(1, bias.shape[1]), whole((1, bias.shape[1]))),
            (shape_of(3, per_dev), whole((3, per_dev))),
        ],
        [pltpu.VMEM((2, 8, base + xw), F32)], 1, 1 << 20, after=[mark],
    )

    return (
        y_all[None], grad_x[None], grad_b[None], grad_c[None], gdt[None], gw, gbias[0], gheads,
    )


def solution(mesh):
    rows = P("dp", "sp", None)
    in_specs = (rows, rows, rows, rows, P(), P(), P(), P(), P(), rows)
    out_specs = (rows, rows, rows, rows, rows, P(), P(), P(None, "sp"))
    return jax.shard_map(
        per_device, mesh=mesh, in_specs=in_specs, out_specs=out_specs, check_vma=False
    )
```

```python
import jax
import jax.numpy as jnp
import numpy as np
from jax import lax
from jax.experimental import pallas as pl
from jax.experimental.pallas import tpu as pltpu
from jax.sharding import PartitionSpec as P

N = 256
Q = 128
HEAD = 64
SUB = 256
LOG2E = 1.4426950408889634
F32 = jnp.float32
BF16 = jnp.bfloat16
NEG = -1e30


def params():
    return pltpu.CompilerParams(vmem_limit_bytes=14 * 1024 * 1024)


def cost(micros, nbytes):
    return pl.CostEstimate(flops=int(micros * 1e9), bytes_accessed=nbytes, transcendentals=0)


def dot(a, b):
    return jnp.dot(a, b, preferred_element_type=F32)


def dot_tb(a, b):
    return lax.dot_general(a, b, (((1,), (1,)), ((), ())), preferred_element_type=F32)


def dot_ta(a, b):
    return lax.dot_general(a, b, (((0,), (0,)), ((), ())), preferred_element_type=F32)


def halves(v):
    hi = v.astype(BF16)
    return hi, (v - hi.astype(F32)).astype(BF16)


def split_dot(v, m):
    hi, lo = halves(v)
    return dot(hi, m) + dot(lo, m)


def exact_dot(m, v):
    hi = v.astype(BF16)
    rest = v - hi.astype(F32)
    mid = rest.astype(BF16)
    low = (rest - mid.astype(F32)).astype(BF16)
    return dot(m, hi) + dot(m, mid) + dot(m, low)


def triangle(lower):
    row = lax.broadcasted_iota(jnp.int32, (Q, Q), 0)
    col = lax.broadcasted_iota(jnp.int32, (Q, Q), 1)
    return row >= col if lower else row <= col


def in_order(y, own, rec, dst, first=0):
    rows = own.shape[0]

    @pl.when(y == 0)
    def _():
        dst[first : first + rows] = own.astype(dst.dtype)
        dst[first + rows : first + 2 * rows] = rec.astype(dst.dtype)

    @pl.when(y != 0)
    def _():
        dst[first : first + rows] = rec.astype(dst.dtype)
        dst[first + rows : first + 2 * rows] = own.astype(dst.dtype)


def conv_sum(xs, w, bias, rows):
    total = bias[...]
    for k in range(4):
        total = total + w[k : k + 1] * xs[5 + k : 5 + k + rows]
    return total


def gates(s):
    sig = 0.5 + 0.5 * jnp.tanh(0.5 * s)
    out = s * sig
    return out, sig + out * (1.0 - sig)


def conv_back(ds, xs, gs, w, rows):
    gs[0:rows] = ds
    gs[rows : rows + 8] = jnp.zeros((8, ds.shape[1]), F32)
    dx = w[3:4] * ds
    for k in range(3):
        dx = dx + w[k : k + 1] * gs[3 - k : 3 - k + rows]
    dw = [jnp.sum(ds * xs[5 + k : 5 + k + rows], axis=0, keepdims=True) for k in range(4)]
    dw.append(jnp.sum(ds, axis=0, keepdims=True))
    dw.append(jnp.zeros((3, ds.shape[1]), F32))
    return dx, jnp.concatenate(dw, axis=0)


def copies(pairs, sems):
    moves = [pltpu.make_async_copy(src, dst, sems.at[i]) for i, (src, dst) in enumerate(pairs)]
    for m in moves:
        m.start()
    for m in moves:
        m.wait()


def pack_rim_kernel(yv, x, b, c, out, xt, bt, ct, sems):
    half = x.shape[1] // 2
    width = b.shape[1] // 2
    step = 2 * width
    copies([(src.at[pl.ds(Q - 16, 16)], dst) for src, dst in ((x, xt), (b, bt), (c, ct))], sems)
    x3, b3, c3 = [r[...].astype(F32)[13:16] for r in (xt, bt, ct)]
    blocks = half // step + 1
    for k in range(2):
        items = []
        for r in range(3):
            for i in range(blocks - 1):
                at = k * half + i * step
                items.append(x3[r : r + 1, at : at + step])
            mine = slice(k * width, (k + 1) * width)
            items.append(jnp.concatenate([b3[r : r + 1, mine], c3[r : r + 1, mine]], axis=1))
        items.append(jnp.zeros((16 - 3 * blocks, step), F32))
        out[16 * k : 16 * (k + 1)] = jnp.concatenate(items, axis=0).astype(BF16)


def pack_small_kernel(yv, b, c, dt, out, sems):
    width = b.shape[1] // 2
    at = pl.multiple_of((1 - yv[0]) * width, 128)
    copies(
        [
            (b.at[:, pl.ds(at, width)], out.at[pl.ds(0, Q), pl.ds(0, width)]),
            (c.at[:, pl.ds(at, width)], out.at[pl.ds(0, Q), pl.ds(width, width)]),
            (dt, out.at[pl.ds(0, Q), pl.ds(2 * width, dt.shape[1])]),
        ],
        sems,
    )


def pack_kernel(yv, x, dy, out, sems, *, chunk, chunks):
    width = out.shape[2]
    at = pl.multiple_of(((1 - yv[0]) * chunks + chunk) * width, 128)
    copies([(x.at[:, pl.ds(at, width)], out.at[0]), (dy.at[:, pl.ds(at, width)], out.at[1])], sems)


def unpack_kernel(yv, got, y_ref, gx_ref, mark, sems, *, chunk, chunks):
    width = got.shape[2]
    at = pl.multiple_of(((1 - yv[0]) * chunks + chunk) * width, 128)
    copies([(got.at[0], y_ref.at[:, pl.ds(at, width)]), (got.at[1], gx_ref.at[:, pl.ds(at, width)])], sems)
    mark[...] = jnp.zeros(mark.shape, F32)


def setup_kernel(
    yv, b_own, c_own, dt_own, rec, rim, rim_e, rim_o, wb, wc, bb, bc_, par, exp2,
    halo_ref, bc_ref, cc_ref, bt_ref, ct_ref, ds_ref, fe_ref, rows_ref, cols_ref, rowt_ref, st_ref,
    xs, dts, xs2, rims,
):
    y = yv[0]
    width = b_own.shape[1]
    heads = par.shape[1]
    half = halo_ref.shape[1] - 2 * width

    @pl.when(y == 0)
    def _():
        rims[...] = rim[0:16].astype(F32)

    @pl.when((y != 0) & (yv[2] == 0))
    def _():
        rims[...] = rim_o[16:32].astype(F32)

    @pl.when((y != 0) & (yv[2] != 0))
    def _():
        rims[...] = rim_e[16:32].astype(F32)

    blocks = halo_ref.shape[1] // rim.shape[1]
    keep = jnp.where(yv[1] == 0, 0.0, 1.0)
    halo_ref[...] = keep * jnp.concatenate(
        [jnp.zeros((5, halo_ref.shape[1]), F32)]
        + [
            jnp.concatenate([rims[r * blocks + i : r * blocks + i + 1] for i in range(blocks)], axis=1)
            for r in range(3)
        ],
        axis=0,
    )
    for i, (own, w, bias, out, out_t) in enumerate(
        ((b_own, wb, bb, bc_ref, bt_ref), (c_own, wc, bc_, cc_ref, ct_ref))
    ):
        at = i * width
        xs[0:8] = halo_ref[:, half + at : half + at + width]
        in_order(y, own[...], rec[0:Q, at : at + width], xs, 8)
        v, slope = gates(conv_sum(xs, w, bias, 2 * Q))
        out[...] = v.astype(BF16)
        out_t[...] = jnp.transpose(v).astype(BF16)
        ds_ref[i] = slope

    @pl.when(y == 0)
    def _():
        dts[0:Q] = dt_own[:, 0:heads].astype(F32)
        dts[Q : 2 * Q] = rec[0:Q, 2 * width : 2 * width + heads].astype(F32)

    @pl.when(y != 0)
    def _():
        dts[0:Q] = rec[0:Q, 2 * width + heads : 2 * width + 2 * heads].astype(F32)
        dts[Q : 2 * Q] = dt_own[:, heads : 2 * heads].astype(F32)

    raw = dts[...] + par[1:2]
    step = jnp.log1p(jnp.exp(raw))
    logs = -step * jnp.exp(par[0:1])
    tri = jnp.where(triangle(True), 1.0, 0.0).astype(BF16)
    run0 = exact_dot(tri, logs[0:Q])
    run1 = exact_dot(tri, logs[Q:])
    tot0, tot1 = run0[Q - 1 : Q], run1[Q - 1 : Q]
    run = jnp.concatenate([run0, run1], axis=0)
    to_end = jnp.concatenate([jnp.exp(tot0 - run0), jnp.exp(tot1 - run1)], axis=0)
    hi, lo = halves(step * to_end)
    fe_ref[0] = jnp.concatenate([hi, lo], axis=1)
    hi, lo = halves(jnp.exp(run))
    fe_ref[1] = jnp.concatenate([hi, lo], axis=1)
    st_ref[...] = jnp.concatenate([step, raw], axis=1)
    small = jnp.concatenate(
        [jnp.exp(tot0), jnp.exp(tot1), jnp.exp(tot0 + tot1), par[2:3], jnp.zeros((4, heads), F32)],
        axis=0,
    )
    hi, lo = halves(small)
    rows_ref[...] = dot(jnp.concatenate([hi, lo], axis=1), exp2[...])
    r2 = run * LOG2E
    q2 = (run - jnp.log(step)) * LOG2E
    xs2[...] = jnp.transpose(jnp.concatenate([r2, q2], axis=1))
    for j in range(heads // 4):
        cols_ref[j] = jnp.concatenate([r2[:, 4 * j : 4 * j + 4], q2[:, 4 * j : 4 * j + 4]], axis=1)
        rowt_ref[j] = jnp.concatenate(
            [xs2[4 * j : 4 * j + 4], xs2[heads + 4 * j : heads + 4 * j + 4]], axis=0
        )


def state_kernel(
    yv, x_own, dy_own, rec, halo, w, bias, bt, ct, fe, exp2, rows,
    t_ref, u_ref, xc_ref, dyo_ref, sl_ref, xs,
):
    y = yv[0]
    xs[0:8] = halo[...]
    in_order(y, x_own[...], rec[0], xs, 8)
    in_order(y, dy_own[...], rec[1], dyo_ref)
    v, slope = gates(conv_sum(xs, w, bias, 2 * Q))
    xc = v.astype(BF16)
    xc_ref[...] = xc
    sl_ref[...] = slope.astype(BF16)
    wt = (xc.astype(F32) * dot(fe[0], exp2[...])).astype(BF16)
    dyr = (dyo_ref[...].astype(F32) * dot(fe[1], exp2[...])).astype(BF16)
    top, end = slice(0, Q), slice(Q, 2 * Q)
    t_ref[0] = (rows[1:2] * dot(bt[:, top], wt[top]) + dot(bt[:, end], wt[end])).astype(BF16)
    u_ref[0] = (dot(ct[:, top], dyr[top]) + rows[0:1] * dot(ct[:, end], dyr[end])).astype(BF16)


def setup_whole(yv, b, c, dt, rec, rim, rim_e, rim_o, w, bias, par, exp2, *rest):
    width = rec.shape[1] // 2 - dt.shape[1] // 2
    first = w.shape[1] - 4 * width
    own = pl.ds(pl.multiple_of(yv[0] * width, width), width)

    def at(i):
        return pl.ds(pl.multiple_of(first + 2 * i * width + yv[0] * width, width), width)

    setup_kernel(
        yv, b.at[:, own], c.at[:, own], dt, rec, rim, rim_e, rim_o, w.at[:, at(0)], w.at[:, at(1)],
        bias.at[:, at(0)], bias.at[:, at(1)], par, exp2, *rest,
    )


def over_subs(width, body):
    for j in range(width // SUB):
        body(j, j * SUB)


def state_chunk(
    yv, x, dy, rec, halo, w, bias, bt, ct, fe, exp2, rows, t_all, u_all, xc, dyo, sl, xs, tu, sems,
    *, chunk, per_group,
):
    chunks, _, cw = t_all.shape
    g = chunk // per_group * N

    def body(j, lo):
        at = pl.ds(lo, SUB)
        own = pl.ds(pl.multiple_of((yv[0] * chunks + chunk) * cw + lo, SUB), SUB)
        band = pl.ds(pl.multiple_of(chunk * cw + lo, SUB), SUB)
        state_kernel(
            yv, x.at[:, own], dy.at[:, own], rec.at[:, :, at], halo.at[:, band], w.at[:, own],
            bias.at[:, own], bt.at[g : g + N], ct.at[g : g + N], fe, exp2.at[:, band],
            rows.at[:, band], tu.at[0:1, :, at], tu.at[1:2, :, at],
            xc.at[:, at], dyo.at[:, at], sl.at[:, at], xs,
        )

    over_subs(cw, body)
    copies([(tu.at[0], t_all.at[chunk]), (tu.at[1], u_all.at[chunk])], sems)


def hop_kernel(yv, in_e, in_o, t, u, rows, out_e, out_o, *, step):
    chunks, height, width = t.shape
    cf = jnp.clip(step - yv[1], 0, chunks - 1)
    cb = jnp.clip(step - yv[4], 0, chunks - 1)

    def decay(c, spot):
        at = pl.ds(pl.multiple_of(c * width, width), width)
        return rows[2:3, at] * jnp.where(spot == 0, 0.0, 1.0)

    row_f = decay(cf, yv[1])
    row_b = decay(cb, yv[4])

    def move(src, row, add, c, dst):
        for r in range(0, height, 32):
            at = slice(r, r + 32)
            dst[at] = (row * src[at].astype(F32) + add[c, at].astype(F32)).astype(BF16)

    @pl.when(yv[2] == 0)
    def _():
        move(in_o, row_f, t, cf, out_e)
        move(in_e, row_b, u, cb, out_o)

    @pl.when(yv[2] != 0)
    def _():
        move(in_e, row_f, t, cf, out_o)
        move(in_o, row_b, u, cb, out_e)


def within_chunk(yv, xc, dyo, cols, rowt, bc, cc, yi, dxi, dcb_ref, cb, *, chunk, per_group):
    cw = xc.shape[1]
    g = slice(chunk // per_group * N, chunk // per_group * N + N)
    dcb_ref[...] = jnp.zeros(dcb_ref.shape, F32)
    for b in range(2):
        at = slice(b * Q, b * Q + Q)
        cb[b] = dot_tb(cc[at, g], bc[at, g])
        cb[2 + b] = dot_tb(bc[at, g], cc[at, g])

    def body(j, lo):
        at = pl.ds(lo, SUB)
        item = pl.ds(chunk * (cw // SUB) + j, 1)
        within_kernel(
            yv, xc.at[:, at], dyo.at[:, at], cols.at[item], rowt.at[item], yi.at[:, at],
            dxi.at[:, at], dcb_ref, cb,
        )

    over_subs(cw, body)


def within_kernel(yv, xc, dyo, cols, rowt, yi_ref, dxi_ref, dcb_ref, cb):
    low = triangle(True)
    high = triangle(False)
    lane = lax.broadcasted_iota(jnp.int32, (1, 2 * HEAD), 1)
    first = jnp.where(lane < HEAD, 1.0, 0.0).astype(BF16)
    second = jnp.where(lane < HEAD, 0.0, 1.0).astype(BF16)
    for b in range(2):
        at = slice(b * Q, b * Q + Q)
        dcb = dcb_ref[b]
        for p in range(2):
            ls = slice(p * 2 * HEAD, (p + 1) * 2 * HEAD)
            xp = xc[at, ls]
            dyp = dyo[at, ls]
            xbd = jnp.concatenate([xp * first, xp * second], axis=0)
            dbd = jnp.concatenate([dyp * first, dyp * second], axis=0)
            decay, mix, mixt = [], [], []
            for i in range(2):
                h = 2 * p + i
                ex = cols[0, at, h : h + 1] - rowt[0, 4 + h : 5 + h, at]
                lt = jnp.exp2(jnp.where(low, ex, NEG))
                ext = rowt[0, h : h + 1, at] - cols[0, at, 4 + h : 5 + h]
                ltt = jnp.exp2(jnp.where(high, ext, NEG))
                decay.append(lt)
                mix.append((cb[b] * lt).astype(BF16))
                mixt.append((cb[2 + b] * ltt).astype(BF16))
            yi_ref[at, ls] = dot(jnp.concatenate(mix, axis=1), xbd)
            dxi_ref[at, ls] = dot(jnp.concatenate(mixt, axis=1), dbd)
            dm = dot_tb(dyp, xbd)
            dcb = dcb + dm[:, 0:Q] * decay[0] + dm[:, Q:] * decay[1]
        dcb_ref[b] = dcb


def fetch(spot, choices, dst, sem):
    @pl.when(spot == 0)
    def _():
        dst[...] = jnp.zeros(dst.shape, dst.dtype)

    for k, src in enumerate(choices, 1):

        @pl.when(spot == k)
        def _():
            pltpu.make_async_copy(src, dst, sem).start()


def arrive(spot, choices, dst, sem):
    @pl.when(spot != 0)
    def _():
        pltpu.make_async_copy(choices[0], dst, sem).wait()


def across_chunk(
    yv, x, rec, halo, w, xc, dyo, sl, yi, dxi, bc, cc, bt, ct, fe, exp2, seg, rows, *rest,
    chunk, chunks, per_group,
):
    hops = (len(rest) - 16) // 2
    ents, leas = rest[:hops], rest[hops : 2 * hops]
    (y_ref, gx_ref, red, head, send, dc, db, wv, ends) = rest[2 * hops : -7]
    xs, gs, gy, ent, lea, sems, more = rest[-7:]
    cw = xc.shape[1]
    fetch(yv[1], ents, ent, sems.at[0])
    fetch(yv[4], leas, lea, sems.at[1])
    dc[...] = jnp.zeros(dc.shape, F32)
    db[...] = jnp.zeros(db.shape, F32)
    wv[...] = jnp.zeros(wv.shape, F32)
    arrive(yv[1], ents, ent, sems.at[0])
    arrive(yv[4], leas, lea, sems.at[1])
    g = slice(chunk // per_group * N, chunk // per_group * N + N)

    def body(j, lo):
        at = pl.ds(lo, SUB)
        own = pl.ds(pl.multiple_of((yv[0] * chunks + chunk) * cw + lo, SUB), SUB)
        band = pl.ds(pl.multiple_of(chunk * cw + lo, SUB), SUB)
        across_kernel(
            yv, x.at[:, own], rec.at[:, :, at], halo.at[:, band], w.at[:, own], xc.at[:, at],
            dyo.at[:, at], sl.at[:, at], yi.at[:, at], dxi.at[:, at], bc.at[:, g], cc.at[:, g],
            bt.at[g], ct.at[g], fe, exp2.at[:, band], seg.at[band], rows.at[:, band],
            ent.at[:, at], lea.at[:, at], red.at[:, at], head.at[:, at], gy.at[:, :, at],
            dc, db, wv, ends.at[:, at], xs, gs,
        )

    over_subs(cw, body)
    mine = pl.ds(pl.multiple_of(yv[0] * Q, Q), Q)
    other = pl.ds(pl.multiple_of((1 - yv[0]) * Q, Q), Q)
    place = pl.ds(pl.multiple_of((yv[0] * chunks + chunk) * cw, cw), cw)
    copies(
        [
            (gy.at[:, other], send), (gy.at[0, mine], y_ref.at[:, place]),
            (gy.at[1, mine], gx_ref.at[:, place]),
        ],
        more,
    )


def across_kernel(
    yv, x_own, rec, halo, w, xc, dyo, sl, yi, dxi, bc, cc, bt, ct, fe, exp2, seg, rows, ent, lea,
    red_ref, head_ref, gy, dc_ref, db_ref, wv_ref, ends_ref, xs, gs,
):
    y = yv[0]
    xs[0:8] = halo[...]
    in_order(y, x_own[...], rec[0], xs, 8)
    x = xc[...].astype(F32)
    dy = dyo[...].astype(F32)
    f = dot(fe[0], exp2[...])
    er = dot(fe[1], exp2[...])
    wt = (x * f).astype(BF16)
    dyr = (dy * er).astype(BF16)
    d0, d1, skip = rows[0:1], rows[1:2], rows[3:4]
    top, end = slice(0, Q), slice(Q, 2 * Q)
    e0 = ent[...]
    r1 = lea[...]
    e1 = (d0 * e0.astype(F32) + dot(bt[:, top], wt[top])).astype(BF16)
    r0 = (d1 * r1.astype(F32) + dot(ct[:, end], dyr[end])).astype(BF16)
    over = jnp.concatenate([dot(cc[top], e0), dot(cc[end], e1)], axis=0) * er
    back = jnp.concatenate([dot(bc[top], r0), dot(bc[end], r1)], axis=0) * f
    yn = yi[...] + over
    dxn = dxi[...] + back
    dc_ref[top] += dot_tb(dyr[top], e0)
    dc_ref[end] += dot_tb(dyr[end], e1)
    db_ref[top] += dot_tb(wt[top], r0)
    db_ref[end] += dot_tb(wt[end], r1)
    wv_ref[0] += split_dot(dy * yn, seg[...])
    wv_ref[1] += split_dot(x * dxn, seg[...])
    xb = x * back
    ends_ref[...] = jnp.concatenate(
        [
            jnp.sum(xb[top], axis=0, keepdims=True)
            + d0 * jnp.sum(r0.astype(F32) * e0.astype(F32), axis=0, keepdims=True),
            jnp.sum(xb[end], axis=0, keepdims=True)
            + d1 * jnp.sum(r1.astype(F32) * e1.astype(F32), axis=0, keepdims=True),
            jnp.sum(x * dy, axis=0, keepdims=True),
            jnp.zeros((5, SUB), F32),
        ],
        axis=0,
    )
    ds = (dxn + skip * dy) * sl[...].astype(F32)
    gx, dw = conv_back(ds, xs, gs, w, 2 * Q)
    red_ref[...] = dw
    head_ref[...] = ds[0:8]
    gy[0] = (yn + skip * x).astype(BF16)
    gy[1] = gx.astype(BF16)


def finish_group(
    yv, b_own, c_own, b_rec, c_rec, b_halo, c_halo, wb, wc, slope, bc, cc, parts,
    gb_ref, gc_ref, red_ref, head_ref, send_ref, xs, gs, gv,
):
    y = yv[0]
    dc, db, dcb = [sum(r[...] for r in refs[1:]) + refs[0][...] for refs in zip(*parts)]
    dcb = dcb.astype(BF16)
    for b in range(2):
        at = slice(b * Q, b * Q + Q)
        gv[0, at] = db[at] + dot_ta(dcb[b], cc[at])
        gv[1, at] = dc[at] + dot(dcb[b], bc[at])
    for i, (own, rec, halo, w, out) in enumerate(
        ((b_own, b_rec, b_halo, wb, gb_ref), (c_own, c_rec, c_halo, wc, gc_ref))
    ):
        cs = slice(i * N, (i + 1) * N)
        xs[0:8] = halo[...]
        in_order(y, own[...], rec[...], xs, 8)
        ds = gv[i] * slope[i]
        gx, dw = conv_back(ds, xs, gs, w, 2 * Q)
        red_ref[:, cs] = dw
        head_ref[:, cs] = ds[0:8]

        @pl.when(y == 0)
        def _():
            out[...] = gx[0:Q].astype(BF16)
            send_ref[:, cs] = gx[Q:].astype(BF16)

        @pl.when(y != 0)
        def _():
            out[...] = gx[Q:].astype(BF16)
            send_ref[:, cs] = gx[0:Q].astype(BF16)


def finish_views(yv, g, b, c, rec, halo, w, slopes, bc, cc, gb, gc, red, head):
    groups = bc.shape[1] // N
    half = halo.shape[1] - 2 * groups * N
    wide = 2 * half
    gs = slice(g * N, (g + 1) * N)
    own = pl.ds(pl.multiple_of((yv[0] * groups + g) * N, N), N)

    def weights(i):
        return pl.ds(pl.multiple_of(wide + (2 * i * groups + yv[0] * groups + g) * N, N), N)

    return (
        b.at[:, own], c.at[:, own], rec.at[:, gs], rec.at[:, (groups + g) * N : (groups + g + 1) * N],
        halo.at[:, half + g * N : half + (g + 1) * N],
        halo.at[:, half + (groups + g) * N : half + (groups + g + 1) * N],
        w.at[:, weights(0)], w.at[:, weights(1)], slopes.at[:, :, gs], bc.at[:, gs], cc.at[:, gs],
    ), (gb, gc, red, head)


def finish_kernel(
    yv, b, c, rec, halo, w, slopes, bc, cc, dc0, db0, dcb0, dc1, db1, dcb1,
    red, head, gb, gc, send_ref, xs, gs, gv,
):
    ins, outs = finish_views(yv, 0, b, c, rec, halo, w, slopes, bc, cc, gb, gc, red, head)
    finish_group(yv, *ins, [(dc0, db0, dcb0), (dc1, db1, dcb1)], *outs, send_ref, xs, gs, gv)
    for ref in outs[2:]:
        ref[:, 2 * N :] = jnp.zeros((8, ref.shape[1] - 2 * N), F32)


def finish_last_kernel(
    yv, b, c, rec, halo, w, slopes, bc, cc, dc0, db0, dcb0, dc1, db1, dcb1, st, par, seg, before, *rest,
):
    chunks = (len(rest) - 11) // 3
    wvs, ends, tops = [rest[i * chunks : (i + 1) * chunks] for i in range(3)]
    rest = rest[3 * chunks :]
    red, head, gb, gc, send_ref, gdt_ref, next_ref, xs, gs, gv, gd = rest
    y = yv[0]
    ins, outs = finish_views(yv, 1, b, c, rec, halo, w, slopes, bc, cc, gb, gc, red, head)
    finish_group(yv, *ins, [(dc0, db0, dcb0), (dc1, db1, dcb1)], *outs, send_ref, xs, gs, gv)
    red_ref, head_ref = red, head
    heads = par.shape[1]
    step, raw = st[:, 0:heads], st[:, heads:]
    rate = jnp.exp(par[0:1])
    cw = ends[0].shape[1]
    w_sum = sum(wv[0] for wv in wvs[1:]) + wvs[0][0]
    v_sum = sum(wv[1] for wv in wvs[1:]) + wvs[0][1]
    e_sum = split_dot(ends[0][...], seg[0:cw])
    for i in range(1, chunks):
        e_sum = e_sum + split_dot(ends[i][...], seg[i * cw : (i + 1) * cw])
    tri = jnp.where(triangle(False), 1.0, 0.0).astype(BF16)
    diff = w_sum - v_sum
    dl = jnp.concatenate(
        [exact_dot(tri, diff[0:Q]) + e_sum[0:1], exact_dot(tri, diff[Q:]) + e_sum[1:2]], axis=0
    )
    draw = (v_sum / step - rate * dl) / (1.0 + jnp.exp(-raw))
    red_ref[:, 2 * N :] = jnp.concatenate(
        [
            jnp.concatenate(
                [
                    jnp.sum(dl * (-rate * step), axis=0, keepdims=True),
                    jnp.sum(draw, axis=0, keepdims=True),
                    e_sum[2:3],
                    jnp.zeros((5, heads), F32),
                ],
                axis=0,
            ),
            jnp.zeros((8, red_ref.shape[1] - 2 * N - heads), F32),
        ],
        axis=1,
    )
    head_ref[:, 2 * N :] = jnp.zeros((8, head_ref.shape[1] - 2 * N), F32)
    items = []
    for r in range(3):
        row = slice(r, r + 1)
        items += [v[row] for v in tops]
        items.append(
            jnp.concatenate(
                [
                    before[row, 0:N], head_ref[row, 0:N],
                    before[row, N : 2 * N], head_ref[row, N : 2 * N],
                ],
                axis=1,
            )
        )
    items.append(jnp.zeros((16 - 3 * (chunks + 1), cw), F32))
    next_ref[...] = jnp.concatenate(items, axis=0)
    gd[...] = jnp.concatenate([draw, draw], axis=1).astype(BF16)

    @pl.when(y == 0)
    def _():
        gdt_ref[...] = gd[0:Q]
        send_ref[:, 2 * N :] = gd[Q:]

    @pl.when(y != 0)
    def _():
        gdt_ref[...] = gd[Q:]
        send_ref[:, 2 * N :] = gd[0:Q]


def add_kernel(yv, *refs):
    total = refs[0][...]
    for r in refs[1:-1]:
        total = total + r[...]
    refs[-1][...] = total


def gather_kernel(yv, *refs, side, count):
    out = refs[-1]
    more = refs[2 * count : -1]

    def fill(k):
        at = 0
        for r in refs[k * count : (k + 1) * count]:
            width = r.shape[1]
            total = r[...]
            for m in more:
                total = total + m[:, at : at + width]
            out[:, at : at + width] = total
            at += width

    for core in range(2):

        @pl.when(yv[3] == core)
        def _():
            fill(1 - core if side else core)


def join_kernel(yv, first, second, out):
    out[0] = first[...]
    out[1] = second[...]


def spread(yv, own, got, dst):
    width = own[0].shape[1]
    for k in range(2):

        @pl.when(yv[0] == k)
        def _():
            for g in range(2):
                at = (k * 2 + g) * width
                dst[:, at : at + width] = own[g][...].astype(F32)
                at = ((1 - k) * 2 + g) * width
                dst[:, at : at + width] = got[g].astype(F32)


def rim_kernel(
    yv, next0, next_e, next_o, w, b0, b1, c0, c1, got0, got1, gdt_own, gx,
    gx_ref, gb_ref, gc_ref, gdt_ref, mark, both, full,
):
    mark[...] = jnp.zeros(mark.shape, F32)
    lane = lax.broadcasted_iota(jnp.int32, gdt_own.shape, 1)
    low = lane < gdt_own.shape[1] // 2
    own, got = gdt_own[...].astype(F32), got1[:, 2 * N :].astype(F32)

    @pl.when(yv[0] == 0)
    def _():
        gdt_ref[...] = jnp.where(low, own, got).astype(BF16)

    @pl.when(yv[0] != 0)
    def _():
        gdt_ref[...] = jnp.where(low, got, own).astype(BF16)

    spread(yv, (b0, b1), [r[:, 0:N] for r in (got0, got1)], full.at[0])
    spread(yv, (c0, c1), [r[:, N : 2 * N] for r in (got0, got1)], full.at[1])
    gb_ref[...] = full[0].astype(BF16)
    gc_ref[...] = full[1].astype(BF16)
    rows = slice(Q - 16, Q)
    both[0] = next0[...]

    @pl.when(yv[2] == 0)
    def _():
        both[1] = next_e[...]

    @pl.when(yv[2] != 0)
    def _():
        both[1] = next_o[...]

    step = next0.shape[1]
    blocks = gx.shape[1] // 2 // step
    keep = jnp.where((yv[0] == 0) | (yv[4] == 0), 0.0, 1.0)

    def add(src, dst, lo, half, block, at, width, to):
        h = [keep * both[half, r * (blocks + 1) + block : r * (blocks + 1) + block + 1, at : at + width] for r in range(3)]
        k = w[:, lo : lo + width]
        more = jnp.concatenate(
            [
                jnp.zeros((13, width), F32),
                k[0:1] * h[0],
                k[0:1] * h[1] + k[1:2] * h[0],
                k[0:1] * h[2] + k[1:2] * h[1] + k[2:3] * h[0],
            ],
            axis=0,
        )
        dst[:, to : to + width] = (src[:, to : to + width].astype(F32) + more).astype(BF16)

    for half in range(2):
        for i in range(blocks):
            at = (half * blocks + i) * step
            add(gx, gx_ref, at, half, i, 0, step, at)
        for i, (src, dst) in enumerate(((full.at[0, rows], gb_ref.at[rows]), (full.at[1, rows], gc_ref.at[rows]))):
            to = half * step // 2
            add(src, dst, (2 * blocks + i) * step + to, half, blocks, i * step // 2, step // 2, to)


def sums_kernel(yv, mine, theirs, gw_ref, gb_ref, gh_ref, both, *, wide, heads):
    width = mine.shape[2]

    @pl.when(yv[3] == 0)
    def _():
        both[:, :, 0:width] = mine[...]
        both[:, :, width:] = theirs[...]

    @pl.when(yv[3] != 0)
    def _():
        both[:, :, 0:width] = theirs[...]
        both[:, :, width:] = mine[...]

    step = width - wide // 2

    def fill(order):
        for k in range(2):
            v = both[order[k]]
            for i in range(2):
                to, at = k * wide + i * (wide // 2), i * width + step
                gw_ref[:, to : to + wide // 2] = v[0:4, at : at + wide // 2]
                gb_ref[:, to : to + wide // 2] = v[4:5, at : at + wide // 2]
            for i in range(2):
                for g in range(2):
                    to = 2 * wide + i * 4 * N + (2 * k + g) * N
                    gw_ref[:, to : to + N] = v[0:4, g * width + i * N : g * width + (i + 1) * N]
                    gb_ref[:, to : to + N] = v[4:5, g * width + i * N : g * width + (i + 1) * N]
        at = width + 2 * N
        values = jnp.concatenate(
            [both[order[0]][:, at : at + heads], both[order[1]][:, at : at + heads]], axis=1
        )
        per_dev = gh_ref.shape[1]
        row = lax.broadcasted_iota(jnp.int32, (2 * heads, per_dev), 0)
        col = lax.broadcasted_iota(jnp.int32, (2 * heads, per_dev), 1)
        pick = jnp.where(row == col + yv[5] * per_dev, 1.0, 0.0).astype(BF16)
        hi = values.astype(BF16)
        rest = values - hi.astype(F32)
        mid = rest.astype(BF16)
        low = (rest - mid.astype(F32)).astype(BF16)
        gh_ref[...] = (dot(hi, pick) + dot(mid, pick) + dot(low, pick))[0:3]

    @pl.when(yv[0] == 0)
    def _():
        fill((0, 1))

    @pl.when(yv[0] != 0)
    def _():
        fill((1, 0))


def whole(shape):
    return pl.BlockSpec(shape, lambda *_: (0,) * len(shape))


def shape_of(*dims, dtype=F32):
    return jax.ShapeDtypeStruct(dims, dtype)


def call(kernel, yv, ins, outs, scratch, micros, nbytes, keep=(), after=(), hbm=()):
    count = len(ins)
    extra = len(keep) + len(after)

    def run(yr, *refs):
        kernel(yr, *refs[:count], *refs[count + extra :])

    near = pl.BlockSpec(memory_space=pltpu.MemorySpace.VMEM)
    anywhere = pl.BlockSpec(memory_space=pl.ANY)
    ins = [i if isinstance(i, tuple) else (i, near) for i in ins]
    return pl.pallas_call(
        run,
        out_shape=outs,
        in_specs=[pl.BlockSpec(memory_space=pltpu.MemorySpace.SMEM)]
        + [i[1] for i in ins]
        + [anywhere if k in hbm else near for k in range(len(keep))]
        + [anywhere] * len(after),
        out_specs=[anywhere if k in hbm else near for k in range(len(outs))],
        scratch_shapes=scratch,
        compiler_params=params(),
        cost_estimate=cost(micros, nbytes),
        input_output_aliases={1 + count + k: k for k in range(len(keep))},
    )(yv, *[i[0] for i in ins], *keep, *after)


def per_device(
    ssm_input, b_input, c_input, dt_input, conv_weight, conv_bias, a_log, dt_bias, skip_gain, grad_out
):
    x_rows, b_rows, c_rows = ssm_input[0], b_input[0], c_input[0]
    dt_rows, dy_rows = dt_input[0], grad_out[0]
    devices = lax.axis_size("sp")
    dp_size = lax.axis_size("dp")
    spots = devices // 2
    me = lax.axis_index("sp")
    y = lax.rem(me, 2)
    z = me // 2
    core = lax.rem(lax.axis_index("dp"), 2)
    yv = jnp.stack([y, z, lax.rem(z, 2), core, spots - 1 - z, me]).astype(jnp.int32)
    xw = x_rows.shape[1] // 2
    bw = b_rows.shape[1] // 2
    hl = dt_rows.shape[1] // 2
    chunks = 4
    cw = xw // chunks
    subs = cw // SUB
    groups = bw // N
    per_group = chunks // groups
    two = 2 * Q
    piece = 2 * N + 2 * hl
    base = groups * piece
    bands = base // SUB
    bias = conv_bias[None]

    def pairs(fn, n=devices):
        return [(i, fn(i)) for i in range(n) if fn(i) is not None and 0 <= fn(i) < n]

    swap = pairs(lambda i: i ^ 1)

    def joint(v, fn):
        moves = []
        for d in range(dp_size):
            for i in range(devices):
                to = fn(i)
                if to is None or not 0 <= to < devices:
                    moves.append((d * devices + i, (d ^ 1) * devices + i))
                else:
                    moves.append((d * devices + i, d * devices + to))
        return lax.ppermute(v, ("dp", "sp"), moves)

    def slant(i):
        return i + 1 if i % 2 else i - 1

    def evens(i):
        return i ^ 2

    def odds(i):
        return ((i + 2) ^ 2) - 2 if 2 <= i < devices - 2 else None

    in_hbm = pl.BlockSpec(memory_space=pltpu.MemorySpace.HBM)
    anywhere = pl.BlockSpec(memory_space=pl.ANY)
    (msg,) = call(
        pack_small_kernel, yv, [(b_rows, in_hbm), (c_rows, in_hbm), (dt_rows, in_hbm)],
        [shape_of(Q, 2 * bw + 2 * hl, dtype=BF16)], [pltpu.SemaphoreType.DMA((3,))], 1, 1 << 20, hbm=(0,),
    )
    rec_bc = lax.ppermute(msg, "sp", swap)
    (rim_out,) = call(
        pack_rim_kernel, yv, [(x_rows, in_hbm), (b_rows, in_hbm), (c_rows, in_hbm)],
        [shape_of(32, 2 * bw, dtype=BF16)],
        [
            pltpu.VMEM((16, 2 * xw), BF16), pltpu.VMEM((16, 2 * bw), BF16),
            pltpu.VMEM((16, 2 * bw), BF16), pltpu.SemaphoreType.DMA((3,)),
        ],
        1, 1 << 20, after=[rec_bc],
    )
    rim = joint(rim_out, slant)
    rim_e = joint(rim_out, evens)
    rim_o = joint(rim_out, odds)
    rec = []

    def send_chunk(c, after):
        def kernel(*refs):
            pack_kernel(*refs, chunk=c, chunks=chunks)

        (out,) = call(
            kernel, yv, [(x_rows, in_hbm), (dy_rows, in_hbm)], [shape_of(2, Q, cw, dtype=BF16)],
            [pltpu.SemaphoreType.DMA((2,))], 1, 1 << 20, after=after, hbm=(0,),
        )
        rec.append(lax.ppermute(out, "sp", swap))

    send_chunk(0, [msg])

    par = lax.dynamic_slice_in_dim(
        jnp.concatenate([jnp.stack([a_log, dt_bias, skip_gain]), jnp.zeros((5, 2 * hl), F32)], 0),
        y * hl, hl, 1,
    )
    lanes = np.arange(xw) // HEAD
    expand = (np.arange(hl)[:, None] == lanes[None, :]).astype(BF16)
    exp2 = jnp.asarray(np.concatenate([expand, expand], axis=0))
    seg = jnp.asarray(np.ascontiguousarray(expand.T))

    nq = hl // 4
    halo, bcc, ccc, bct, cct, slopes, fe, rows, qcols, rowt, st = call(
        setup_whole, yv,
        [b_rows, c_rows, dt_rows, rec_bc, rim, rim_e, rim_o, conv_weight, bias, par, exp2],
        [
            shape_of(8, xw + 2 * bw), shape_of(two, bw, dtype=BF16), shape_of(two, bw, dtype=BF16),
            shape_of(bw, two, dtype=BF16), shape_of(bw, two, dtype=BF16), shape_of(2, two, bw),
            shape_of(2, two, 2 * hl, dtype=BF16), shape_of(8, xw), shape_of(nq, two, 8),
            shape_of(nq, 8, two), shape_of(two, 2 * hl),
        ],
        [
            pltpu.VMEM((two + 8, bw), F32), pltpu.VMEM((two, hl), F32),
            pltpu.VMEM((2 * hl, two), F32), pltpu.VMEM((16, rim.shape[1]), F32),
        ],
        4, 4 << 20,
    )
    send_chunk(1, [rec_bc])
    states = []
    xcs, dyos, sls = [], [], []
    long = pltpu.VMEM((two + 8, SUB), F32)

    def state(c, after):
        nonlocal states
        big = shape_of(chunks, N, cw, dtype=BF16)
        tall = shape_of(two, cw, dtype=BF16)

        def kernel(*refs):
            state_chunk(*refs, chunk=c, per_group=per_group)

        t, u, xc, dyo, sl = call(
            kernel, yv,
            [x_rows, dy_rows, rec[c], halo, conv_weight, bias, bct, cct, fe, exp2, rows],
            [big, big, tall, tall, tall],
            [long, pltpu.VMEM((2, N, cw), BF16), pltpu.SemaphoreType.DMA((2,))], 3, 4 << 20,
            keep=states, after=after, hbm=(0, 1),
        )
        states = [t, u]
        xcs.append(xc)
        dyos.append(dyo)
        sls.append(sl)
        return xc

    yis, dxis, dcbs = [], [], []

    def within(c, after):
        def kernel(*refs):
            within_chunk(*refs, chunk=c, per_group=per_group)

        yi, dxi, dcb = call(
            kernel, yv, [xcs[c], dyos[c], qcols, rowt, bcc, ccc],
            [shape_of(two, cw), shape_of(two, cw), shape_of(2, Q, Q)],
            [pltpu.VMEM((4, Q, Q), F32)], 3, 4 << 20, after=after,
        )
        yis.append(yi)
        dxis.append(dxi)
        dcbs.append(dcb)
        return dcb

    finals = []
    sums = []
    reds, edges = [], []
    got_x = []

    def across(c, ents, leas, after):
        nonlocal finals
        full = shape_of(Q, 2 * xw, dtype=BF16)
        strip = shape_of(8, cw)

        def kernel(*refs):
            across_chunk(*refs, chunk=c, chunks=chunks, per_group=per_group)

        out = call(
            kernel, yv,
            [
                x_rows, rec[c], halo, conv_weight, xcs[c], dyos[c], sls[c], yis[c], dxis[c],
                bcc, ccc, bct, cct, fe, exp2, seg, rows,
            ] + [(v, anywhere) for v in ents + leas],
            [
                full, full, strip, strip, shape_of(2, Q, cw, dtype=BF16), shape_of(two, N),
                shape_of(two, N), shape_of(2, two, hl), shape_of(8, cw),
            ],
            [
                long, long, pltpu.VMEM((2, two, cw), BF16), pltpu.VMEM((N, cw), BF16),
                pltpu.VMEM((N, cw), BF16), pltpu.SemaphoreType.DMA((2,)), pltpu.SemaphoreType.DMA((3,)),
            ],
            6, 6 << 20, keep=finals, after=after, hbm=(0, 1),
        )
        finals = list(out[:2])
        reds.append(out[2])
        edges.append(out[3])
        sums.append(out[5:])
        got_x.append(lax.ppermute(out[4], "sp", swap))
        return out[8]

    def unpack(c, after):
        full = shape_of(Q, 2 * xw, dtype=BF16)

        def kernel(*refs):
            unpack_kernel(*refs, chunk=c, chunks=chunks)

        *finals[:2], mark = call(
            kernel, yv, [(got_x[c], anywhere)], [full, full, shape_of(8, 128)],
            [pltpu.SemaphoreType.DMA((2,))], 1, 1 << 20, keep=finals[:2], after=after, hbm=(0, 1),
        )
        return mark

    grads_bc = []
    group_reds, group_edges = [], []

    def finish(g, last, after):
        own = shape_of(Q, N, dtype=BF16)
        strip = shape_of(8, piece)
        ins = [b_rows, c_rows, rec_bc, halo, conv_weight, slopes, bcc, ccc]
        for c in range(g * per_group, (g + 1) * per_group):
            ins += [sums[c][0], sums[c][1], dcbs[c]]
        outs = [strip, strip, own, own, shape_of(Q, piece if last else 2 * N, dtype=BF16)]
        narrow = pltpu.VMEM((two + 8, N), F32)
        scratch = [narrow, narrow, pltpu.VMEM((2, two, N), F32)]
        if last:
            ins += [st, par, seg, group_edges[0]] + [v[2] for v in sums] + [v[3] for v in sums] + edges
            outs += [shape_of(Q, 2 * hl, dtype=BF16), shape_of(16, cw)]
            scratch.append(pltpu.VMEM((two, 2 * hl), BF16))
        out = call(
            finish_last_kernel if last else finish_kernel, yv, ins, outs, scratch, 3, 4 << 20, after=after
        )
        group_reds.append(out[0])
        group_edges.append(out[1])
        grads_bc.append(out[2:4])
        return lax.ppermute(out[4], "sp", swap), out[4:]

    zero = jnp.zeros((N, cw), BF16)
    in_e, in_o = zero, zero
    ins_e, ins_o = [], []
    steps = chunks + spots - 2
    state(0, [])
    send_chunk(2, [rec[0]])
    got_bc = []
    waits = []
    for t in range(steps + 1):
        if t:
            ins_e.append(in_e)
            ins_o.append(in_o)
        token = []
        if t < steps:

            moving = shape_of(N, cw, dtype=BF16)

            def kernel(*refs, step=t):
                hop_kernel(*refs, step=step)

            out_e, out_o = call(
                kernel, yv, [in_e, in_o, states[0], states[1], rows], [moving, moving], [], 1, 3 << 20,
                after=waits,
            )
            token = [out_e]
            in_e = joint(out_e, evens)
            in_o = joint(out_o, odds)
        waits = []
        if t + 1 < chunks:
            waits.append(state(t + 1, token))
            if t + 3 < chunks:
                send_chunk(t + 3, [rec[t + 1]])
        if t < chunks:
            waits.append(within(t, token))
        c = t + 1 - spots
        if 0 <= c < chunks:
            ents = [(ins_o if k % 2 == 0 else ins_e)[c + k - 1] for k in range(1, spots)]
            leas = [(ins_o if (spots - 1 - k) % 2 else ins_e)[c + k - 1] for k in range(1, spots)]
            waits.append(across(c, ents, leas, token))
            if c == chunks - 2:
                mark = unpack(0, token)
                got, tok = finish(0, False, token)
                got_bc.append(got)
                waits += [tok[0], mark]
    got, (_, gdt_own, next_rows) = finish(1, True, [])
    got_bc.append(got)

    hw = (base + xw) // 2
    slab = shape_of(8, hw)

    def add(items, after=()):
        (out,) = call(add_kernel, yv, items, [slab], [], 1, 1 << 20, after=after)
        return out

    per_side = chunks // 2
    pieces = []
    for k in range(2):
        pieces += [group_reds[k]] + reds[k * per_side : (k + 1) * per_side]

    def gather(side, more):
        def kernel(*refs):
            gather_kernel(*refs, side=side, count=1 + per_side)

        (out,) = call(kernel, yv, pieces + more, [slab], [], 1, 1 << 20)
        return out

    theirs = gather(True, [])
    mine = gather(False, [lax.ppermute(theirs, "dp", pairs(lambda i: i ^ 1, dp_size))])
    size = 2
    while size < dp_size:
        got = lax.ppermute(mine, "dp", pairs(lambda i: i ^ size, dp_size))
        marks = []
        if size == 2:
            marks = [unpack(1, [mine]), unpack(2, [mine])]
        mine = add([mine, got], marks)
        size *= 2
    mark = unpack(3, [mine])
    y_all, gx_all = finals[:2]
    size = 2
    while size < devices:
        ways = 4 if size * 4 <= devices else 2
        got = [lax.ppermute(mine, "sp", pairs(lambda i: i ^ (size * k))) for k in range(1, ways)]
        size *= ways
        mine = add([mine] + got, [mark] if size >= devices else [])
    got_y = lax.ppermute(mine, "sp", swap)

    next0 = joint(next_rows, slant)
    next_e = joint(next_rows, evens)
    next_o = joint(next_rows, odds)
    (mine,) = call(join_kernel, yv, [mine, got_y], [shape_of(2, 8, hw)], [], 1, 1 << 20)
    theirs = lax.ppermute(mine, "dp", pairs(lambda i: i ^ 1, dp_size))
    last = pl.BlockSpec((16, 2 * xw), lambda j, yr: (Q // 16 - 1, 0))
    small = [next0, next_e, next_o, conv_weight] + [grads_bc[g][i] for i in range(2) for g in range(2)]
    small += [got_bc[0], got_bc[1], gdt_own]
    full = shape_of(Q, 2 * bw, dtype=BF16)
    grad_x, grad_b, grad_c, gdt, mark = pl.pallas_call(
        rim_kernel,
        out_shape=[shape_of(Q, 2 * xw, dtype=BF16), full, full, shape_of(Q, 2 * hl, dtype=BF16), shape_of(8, 128)],
        grid_spec=pltpu.PrefetchScalarGridSpec(
            num_scalar_prefetch=1,
            grid=(1,),
            in_specs=[whole(v.shape) for v in small] + [last],
            out_specs=[last, whole(full.shape), whole(full.shape), whole((Q, 2 * hl)), whole((8, 128))],
            scratch_shapes=[pltpu.VMEM((2, 16, cw), F32), pltpu.VMEM((2, Q, 2 * bw), F32)],
        ),
        compiler_params=params(),
        cost_estimate=cost(1, 1 << 20),
        input_output_aliases={1 + len(small): 0},
    )(yv, *small, gx_all)

    per_dev = 2 * hl // devices

    def summed(*refs):
        sums_kernel(*refs, wide=xw, heads=hl)

    gw, gbias, gheads = pl.pallas_call(
        lambda yr, a, b, unused, *refs: summed(yr, a, b, *refs),
        out_shape=[
            shape_of(4, bias.shape[1]), shape_of(1, bias.shape[1]), shape_of(3, per_dev),
        ],
        grid_spec=pltpu.PrefetchScalarGridSpec(
            num_scalar_prefetch=1,
            grid=(1,),
            in_specs=[whole(mine.shape), whole(theirs.shape), anywhere],
            out_specs=[
                whole((4, bias.shape[1])), whole((1, bias.shape[1])), whole((3, per_dev)),
            ],
            scratch_shapes=[pltpu.VMEM((2, 8, base + xw), F32)],
        ),
        compiler_params=params(),
        cost_estimate=cost(1, 1 << 20),
    )(yv, mine, theirs, mark)
    return (
        y_all[None], grad_x[None], grad_b[None], grad_c[None], gdt[None], gw, gbias[0], gheads,
    )


def solution(mesh):
    rows = P("dp", "sp", None)
    in_specs = (rows, rows, rows, rows, P(), P(), P(), P(), P(), rows)
    out_specs = (rows, rows, rows, rows, rows, P(), P(), P(None, "sp"))
    return jax.shard_map(
        per_device, mesh=mesh, in_specs=in_specs, out_specs=out_specs, check_vma=False
    )
```

```python
import jax
import jax.numpy as jnp
import numpy as np
from jax import lax
from jax.experimental import pallas as pl
from jax.experimental.pallas import tpu as pltpu
from jax.sharding import PartitionSpec as P

N = 256
Q = 128
HEAD = 64
SUB = 256
LOG2E = 1.4426950408889634
F32 = jnp.float32
BF16 = jnp.bfloat16
NEG = -1e30


def params():
    return pltpu.CompilerParams(vmem_limit_bytes=14 * 1024 * 1024)


def cost(micros, nbytes):
    return pl.CostEstimate(flops=int(micros * 1e9), bytes_accessed=nbytes, transcendentals=0)


def dot(a, b):
    return jnp.dot(a, b, preferred_element_type=F32)


def dot_tb(a, b):
    return lax.dot_general(a, b, (((1,), (1,)), ((), ())), preferred_element_type=F32)


def dot_ta(a, b):
    return lax.dot_general(a, b, (((0,), (0,)), ((), ())), preferred_element_type=F32)


def halves(v):
    hi = v.astype(BF16)
    return hi, (v - hi.astype(F32)).astype(BF16)


def split_dot(v, m):
    hi, lo = halves(v)
    return dot(hi, m) + dot(lo, m)


def exact_dot(m, v):
    hi = v.astype(BF16)
    rest = v - hi.astype(F32)
    mid = rest.astype(BF16)
    low = (rest - mid.astype(F32)).astype(BF16)
    return dot(m, hi) + dot(m, mid) + dot(m, low)


def triangle(lower):
    row = lax.broadcasted_iota(jnp.int32, (Q, Q), 0)
    col = lax.broadcasted_iota(jnp.int32, (Q, Q), 1)
    return row >= col if lower else row <= col


def in_order(y, own, rec, dst, first=0):
    rows = own.shape[0]

    @pl.when(y == 0)
    def _():
        dst[first : first + rows] = own.astype(dst.dtype)
        dst[first + rows : first + 2 * rows] = rec.astype(dst.dtype)

    @pl.when(y != 0)
    def _():
        dst[first : first + rows] = rec.astype(dst.dtype)
        dst[first + rows : first + 2 * rows] = own.astype(dst.dtype)


def conv_sum(xs, w, bias, rows):
    total = bias[...]
    for k in range(4):
        total = total + w[k : k + 1] * xs[5 + k : 5 + k + rows]
    return total


def gates(s):
    sig = 0.5 + 0.5 * jnp.tanh(0.5 * s)
    out = s * sig
    return out, sig + out * (1.0 - sig)


def conv_back(ds, xs, gs, w, rows):
    gs[0:rows] = ds
    gs[rows : rows + 8] = jnp.zeros((8, ds.shape[1]), F32)
    dx = w[3:4] * ds
    for k in range(3):
        dx = dx + w[k : k + 1] * gs[3 - k : 3 - k + rows]
    dw = [jnp.sum(ds * xs[5 + k : 5 + k + rows], axis=0, keepdims=True) for k in range(4)]
    dw.append(jnp.sum(ds, axis=0, keepdims=True))
    dw.append(jnp.zeros((3, ds.shape[1]), F32))
    return dx, jnp.concatenate(dw, axis=0)


def copies(pairs, sems):
    moves = [pltpu.make_async_copy(src, dst, sems.at[i]) for i, (src, dst) in enumerate(pairs)]
    for m in moves:
        m.start()
    for m in moves:
        m.wait()


def pack_rim_kernel(yv, x, b, c, out, xt, bt, ct, sems):
    half = x.shape[1] // 2
    width = b.shape[1] // 2
    step = 2 * width
    copies([(src.at[pl.ds(Q - 16, 16)], dst) for src, dst in ((x, xt), (b, bt), (c, ct))], sems)
    x3, b3, c3 = [r[...].astype(F32)[13:16] for r in (xt, bt, ct)]
    blocks = half // step + 1
    for k in range(2):
        items = []
        for r in range(3):
            for i in range(blocks - 1):
                at = k * half + i * step
                items.append(x3[r : r + 1, at : at + step])
            mine = slice(k * width, (k + 1) * width)
            items.append(jnp.concatenate([b3[r : r + 1, mine], c3[r : r + 1, mine]], axis=1))
        items.append(jnp.zeros((16 - 3 * blocks, step), F32))
        out[16 * k : 16 * (k + 1)] = jnp.concatenate(items, axis=0).astype(BF16)


def pack_small_kernel(yv, x, b, c, dt, out, rim, xt, bt, ct, sems, rim_sems):
    width = b.shape[1] // 2
    at = pl.multiple_of((1 - yv[0]) * width, 128)
    moves = [
        pltpu.make_async_copy(src, dst, sems.at[i])
        for i, (src, dst) in enumerate(
            (
                (b.at[:, pl.ds(at, width)], out.at[:, pl.ds(0, width)]),
                (c.at[:, pl.ds(at, width)], out.at[:, pl.ds(width, width)]),
                (dt, out.at[:, pl.ds(2 * width, dt.shape[1])]),
            )
        )
    ]
    for m in moves:
        m.start()
    pack_rim_kernel(yv, x, b, c, rim, xt, bt, ct, rim_sems)
    for m in moves:
        m.wait()


def gate_kernel(yv, src, dst):
    dst[...] = src[...]


def pack_kernel(yv, x, dy, out, sems, *, chunk, chunks):
    width = out.shape[2]
    at = pl.multiple_of(((1 - yv[0]) * chunks + chunk) * width, 128)
    copies([(x.at[:, pl.ds(at, width)], out.at[0]), (dy.at[:, pl.ds(at, width)], out.at[1])], sems)


def unpack_kernel(yv, got, y_ref, gx_ref, mark, sems, *, chunk, chunks):
    width = got.shape[2]
    at = pl.multiple_of(((1 - yv[0]) * chunks + chunk) * width, 128)
    copies([(got.at[0], y_ref.at[:, pl.ds(at, width)]), (got.at[1], gx_ref.at[:, pl.ds(at, width)])], sems)
    mark[...] = jnp.zeros(mark.shape, F32)


def setup_kernel(
    yv, b_own, c_own, dt_own, rec, rim, rim_e, rim_o, wb, wc, bb, bc_, par, exp2,
    halo_ref, bc_ref, cc_ref, bt_ref, ct_ref, ds_ref, fe_ref, rows_ref, cols_ref, rowt_ref, st_ref,
    xs, dts, xs2, rims,
):
    y = yv[0]
    width = b_own.shape[1]
    heads = par.shape[1]
    half = halo_ref.shape[1] - 2 * width

    @pl.when(y == 0)
    def _():
        rims[...] = rim[0:16].astype(F32)

    @pl.when((y != 0) & (yv[2] == 0))
    def _():
        rims[...] = rim_o[16:32].astype(F32)

    @pl.when((y != 0) & (yv[2] != 0))
    def _():
        rims[...] = rim_e[16:32].astype(F32)

    blocks = halo_ref.shape[1] // rim.shape[1]
    keep = jnp.where(yv[1] == 0, 0.0, 1.0)
    halo_ref[...] = keep * jnp.concatenate(
        [jnp.zeros((5, halo_ref.shape[1]), F32)]
        + [
            jnp.concatenate([rims[r * blocks + i : r * blocks + i + 1] for i in range(blocks)], axis=1)
            for r in range(3)
        ],
        axis=0,
    )
    for i, (own, w, bias, out, out_t) in enumerate(
        ((b_own, wb, bb, bc_ref, bt_ref), (c_own, wc, bc_, cc_ref, ct_ref))
    ):
        at = i * width
        xs[0:8] = halo_ref[:, half + at : half + at + width]
        in_order(y, own[...], rec[0:Q, at : at + width], xs, 8)
        v, slope = gates(conv_sum(xs, w, bias, 2 * Q))
        out[...] = v.astype(BF16)
        out_t[...] = jnp.transpose(v).astype(BF16)
        ds_ref[i] = slope

    @pl.when(y == 0)
    def _():
        dts[0:Q] = dt_own[:, 0:heads].astype(F32)
        dts[Q : 2 * Q] = rec[0:Q, 2 * width : 2 * width + heads].astype(F32)

    @pl.when(y != 0)
    def _():
        dts[0:Q] = rec[0:Q, 2 * width + heads : 2 * width + 2 * heads].astype(F32)
        dts[Q : 2 * Q] = dt_own[:, heads : 2 * heads].astype(F32)

    raw = dts[...] + par[1:2]
    step = jnp.log1p(jnp.exp(raw))
    logs = -step * jnp.exp(par[0:1])
    tri = jnp.where(triangle(True), 1.0, 0.0).astype(BF16)
    run0 = exact_dot(tri, logs[0:Q])
    run1 = exact_dot(tri, logs[Q:])
    tot0, tot1 = run0[Q - 1 : Q], run1[Q - 1 : Q]
    run = jnp.concatenate([run0, run1], axis=0)
    to_end = jnp.concatenate([jnp.exp(tot0 - run0), jnp.exp(tot1 - run1)], axis=0)
    hi, lo = halves(step * to_end)
    fe_ref[0] = jnp.concatenate([hi, lo], axis=1)
    hi, lo = halves(jnp.exp(run))
    fe_ref[1] = jnp.concatenate([hi, lo], axis=1)
    st_ref[...] = jnp.concatenate([step, raw], axis=1)
    small = jnp.concatenate(
        [jnp.exp(tot0), jnp.exp(tot1), jnp.exp(tot0 + tot1), par[2:3], jnp.zeros((4, heads), F32)],
        axis=0,
    )
    hi, lo = halves(small)
    rows_ref[...] = dot(jnp.concatenate([hi, lo], axis=1), exp2[...])
    r2 = run * LOG2E
    q2 = (run - jnp.log(step)) * LOG2E
    xs2[...] = jnp.transpose(jnp.concatenate([r2, q2], axis=1))
    for j in range(heads // 4):
        cols_ref[j] = jnp.concatenate([r2[:, 4 * j : 4 * j + 4], q2[:, 4 * j : 4 * j + 4]], axis=1)
        rowt_ref[j] = jnp.concatenate(
            [xs2[4 * j : 4 * j + 4], xs2[heads + 4 * j : heads + 4 * j + 4]], axis=0
        )


def state_kernel(
    yv, x_own, dy_own, rec, halo, w, bias, bt, ct, fe, exp2, rows,
    t_ref, u_ref, xc_ref, dyo_ref, sl_ref, xs,
):
    y = yv[0]
    xs[0:8] = halo[...]
    in_order(y, x_own[...], rec[0], xs, 8)
    in_order(y, dy_own[...], rec[1], dyo_ref)
    v, slope = gates(conv_sum(xs, w, bias, 2 * Q))
    xc = v.astype(BF16)
    xc_ref[...] = xc
    sl_ref[...] = slope.astype(BF16)
    wt = (xc.astype(F32) * dot(fe[0], exp2[...])).astype(BF16)
    dyr = (dyo_ref[...].astype(F32) * dot(fe[1], exp2[...])).astype(BF16)
    top, end = slice(0, Q), slice(Q, 2 * Q)
    t_ref[0] = (rows[1:2] * dot(bt[:, top], wt[top]) + dot(bt[:, end], wt[end])).astype(BF16)
    u_ref[0] = (dot(ct[:, top], dyr[top]) + rows[0:1] * dot(ct[:, end], dyr[end])).astype(BF16)


def setup_whole(yv, b, c, dt, rec, rim, rim_e, rim_o, w, bias, par, exp2, *rest):
    width = rec.shape[1] // 2 - dt.shape[1] // 2
    first = w.shape[1] - 4 * width
    own = pl.ds(pl.multiple_of(yv[0] * width, width), width)

    def at(i):
        return pl.ds(pl.multiple_of(first + 2 * i * width + yv[0] * width, width), width)

    setup_kernel(
        yv, b.at[:, own], c.at[:, own], dt, rec, rim, rim_e, rim_o, w.at[:, at(0)], w.at[:, at(1)],
        bias.at[:, at(0)], bias.at[:, at(1)], par, exp2, *rest,
    )


def over_subs(width, body):
    for j in range(width // SUB):
        body(j, j * SUB)


def state_chunk(
    yv, x, dy, rec, halo, w, bias, bt, ct, fe, exp2, rows, t_all, u_all, xc, dyo, sl, xs, tu, sems,
    *, chunk, per_group,
):
    chunks, _, cw = t_all.shape
    g = chunk // per_group * N

    def body(j, lo):
        at = pl.ds(lo, SUB)
        own = pl.ds(pl.multiple_of((yv[0] * chunks + chunk) * cw + lo, SUB), SUB)
        band = pl.ds(pl.multiple_of(chunk * cw + lo, SUB), SUB)
        state_kernel(
            yv, x.at[:, own], dy.at[:, own], rec.at[:, :, at], halo.at[:, band], w.at[:, own],
            bias.at[:, own], bt.at[g : g + N], ct.at[g : g + N], fe, exp2.at[:, band],
            rows.at[:, band], tu.at[0:1, :, at], tu.at[1:2, :, at],
            xc.at[:, at], dyo.at[:, at], sl.at[:, at], xs,
        )

    over_subs(cw, body)
    copies([(tu.at[0], t_all.at[chunk]), (tu.at[1], u_all.at[chunk])], sems)


def hop_kernel(yv, in_e, in_o, t, u, rows, out_e, out_o, *, step, part):
    chunks, height, whole_width = t.shape
    width = out_e.shape[1]
    cf = jnp.clip(step - yv[1], 0, chunks - 1)
    cb = jnp.clip(step - yv[4], 0, chunks - 1)
    lanes = slice(part * width, (part + 1) * width)

    def decay(c, spot):
        at = pl.ds(pl.multiple_of(c * whole_width + part * width, width), width)
        return rows[2:3, at] * jnp.where(spot == 0, 0.0, 1.0)

    row_f = decay(cf, yv[1])
    row_b = decay(cb, yv[4])

    def move(src, row, add, c, dst):
        for r in range(0, height, 32):
            at = slice(r, r + 32)
            more = add[c, at, lanes]
            dst[at] = (row * src[at].astype(F32) + more.astype(F32)).astype(BF16)

    @pl.when(yv[2] == 0)
    def _():
        move(in_o, row_f, t, cf, out_e)
        move(in_e, row_b, u, cb, out_o)

    @pl.when(yv[2] != 0)
    def _():
        move(in_e, row_f, t, cf, out_o)
        move(in_o, row_b, u, cb, out_e)


def within_chunk(yv, xc, dyo, cols, rowt, bc, cc, yi, dxi, dcb_ref, cb, *, chunk, per_group):
    cw = xc.shape[1]
    g = slice(chunk // per_group * N, chunk // per_group * N + N)
    dcb_ref[...] = jnp.zeros(dcb_ref.shape, F32)
    for b in range(2):
        at = slice(b * Q, b * Q + Q)
        cb[b] = dot_tb(cc[at, g], bc[at, g])
        cb[2 + b] = dot_tb(bc[at, g], cc[at, g])

    def body(j, lo):
        at = pl.ds(lo, SUB)
        item = pl.ds(chunk * (cw // SUB) + j, 1)
        within_kernel(
            yv, xc.at[:, at], dyo.at[:, at], cols.at[item], rowt.at[item], yi.at[:, at],
            dxi.at[:, at], dcb_ref, cb,
        )

    over_subs(cw, body)


def within_kernel(yv, xc, dyo, cols, rowt, yi_ref, dxi_ref, dcb_ref, cb):
    low = triangle(True)
    high = triangle(False)
    lane = lax.broadcasted_iota(jnp.int32, (1, 2 * HEAD), 1)
    first = jnp.where(lane < HEAD, 1.0, 0.0).astype(BF16)
    second = jnp.where(lane < HEAD, 0.0, 1.0).astype(BF16)
    for b in range(2):
        at = slice(b * Q, b * Q + Q)
        dcb = dcb_ref[b]
        for p in range(2):
            ls = slice(p * 2 * HEAD, (p + 1) * 2 * HEAD)
            xp = xc[at, ls]
            dyp = dyo[at, ls]
            xbd = jnp.concatenate([xp * first, xp * second], axis=0)
            dbd = jnp.concatenate([dyp * first, dyp * second], axis=0)
            decay, mix, mixt = [], [], []
            for i in range(2):
                h = 2 * p + i
                ex = cols[0, at, h : h + 1] - rowt[0, 4 + h : 5 + h, at]
                lt = jnp.exp2(jnp.where(low, ex, NEG))
                ext = rowt[0, h : h + 1, at] - cols[0, at, 4 + h : 5 + h]
                ltt = jnp.exp2(jnp.where(high, ext, NEG))
                decay.append(lt)
                mix.append((cb[b] * lt).astype(BF16))
                mixt.append((cb[2 + b] * ltt).astype(BF16))
            yi_ref[at, ls] = dot(jnp.concatenate(mix, axis=1), xbd)
            dxi_ref[at, ls] = dot(jnp.concatenate(mixt, axis=1), dbd)
            dm = dot_tb(dyp, xbd)
            dcb = dcb + dm[:, 0:Q] * decay[0] + dm[:, Q:] * decay[1]
        dcb_ref[b] = dcb


def fetch(spot, choices, dst, sem):
    @pl.when(spot == 0)
    def _():
        dst[...] = jnp.zeros(dst.shape, dst.dtype)

    for k, src in enumerate(choices, 1):

        @pl.when(spot == k)
        def _():
            pltpu.make_async_copy(src, dst, sem).start()


def arrive(spot, choices, dst, sem):
    @pl.when(spot != 0)
    def _():
        pltpu.make_async_copy(choices[0], dst, sem).wait()


def across_chunk(
    yv, x, rec, halo, w, xc, dyo, sl, yi, dxi, bc, cc, bt, ct, fe, exp2, seg, rows, *rest,
    chunk, chunks, per_group,
):
    hops = (len(rest) - 16) // 2
    ents, leas = rest[:hops], rest[hops : 2 * hops]
    (y_ref, gx_ref, red, head, send, dc, db, wv, ends) = rest[2 * hops : -7]
    xs, gs, gy, ent, lea, sems, more = rest[-7:]
    cw = xc.shape[1]
    parts = ents[0].shape[1]
    count = cw // parts
    jobs = []
    for i in range(count):
        at = slice(i * parts, (i + 1) * parts)
        jobs.append((yv[1], ents[i::count], ent.at[:, at], sems.at[2 * i]))
        jobs.append((yv[4], leas[i::count], lea.at[:, at], sems.at[2 * i + 1]))
    for job in jobs:
        fetch(*job)
    dc[...] = jnp.zeros(dc.shape, F32)
    db[...] = jnp.zeros(db.shape, F32)
    wv[...] = jnp.zeros(wv.shape, F32)
    for job in jobs:
        arrive(*job)
    g = slice(chunk // per_group * N, chunk // per_group * N + N)

    def body(j, lo):
        at = pl.ds(lo, SUB)
        own = pl.ds(pl.multiple_of((yv[0] * chunks + chunk) * cw + lo, SUB), SUB)
        band = pl.ds(pl.multiple_of(chunk * cw + lo, SUB), SUB)
        across_kernel(
            yv, x.at[:, own], rec.at[:, :, at], halo.at[:, band], w.at[:, own], xc.at[:, at],
            dyo.at[:, at], sl.at[:, at], yi.at[:, at], dxi.at[:, at], bc.at[:, g], cc.at[:, g],
            bt.at[g], ct.at[g], fe, exp2.at[:, band], seg.at[band], rows.at[:, band],
            ent.at[:, at], lea.at[:, at], red.at[:, at], head.at[:, at], gy.at[:, :, at],
            dc, db, wv, ends.at[:, at], xs, gs,
        )

    over_subs(cw, body)
    mine = pl.ds(pl.multiple_of(yv[0] * Q, Q), Q)
    other = pl.ds(pl.multiple_of((1 - yv[0]) * Q, Q), Q)
    place = pl.ds(pl.multiple_of((yv[0] * chunks + chunk) * cw, cw), cw)
    copies(
        [
            (gy.at[:, other], send), (gy.at[0, mine], y_ref.at[:, place]),
            (gy.at[1, mine], gx_ref.at[:, place]),
        ],
        more,
    )


def across_kernel(
    yv, x_own, rec, halo, w, xc, dyo, sl, yi, dxi, bc, cc, bt, ct, fe, exp2, seg, rows, ent, lea,
    red_ref, head_ref, gy, dc_ref, db_ref, wv_ref, ends_ref, xs, gs,
):
    y = yv[0]
    xs[0:8] = halo[...]
    in_order(y, x_own[...], rec[0], xs, 8)
    x = xc[...].astype(F32)
    dy = dyo[...].astype(F32)
    f = dot(fe[0], exp2[...])
    er = dot(fe[1], exp2[...])
    wt = (x * f).astype(BF16)
    dyr = (dy * er).astype(BF16)
    d0, d1, skip = rows[0:1], rows[1:2], rows[3:4]
    top, end = slice(0, Q), slice(Q, 2 * Q)
    e0 = ent[...]
    r1 = lea[...]
    e1 = (d0 * e0.astype(F32) + dot(bt[:, top], wt[top])).astype(BF16)
    r0 = (d1 * r1.astype(F32) + dot(ct[:, end], dyr[end])).astype(BF16)
    over = jnp.concatenate([dot(cc[top], e0), dot(cc[end], e1)], axis=0) * er
    back = jnp.concatenate([dot(bc[top], r0), dot(bc[end], r1)], axis=0) * f
    yn = yi[...] + over
    dxn = dxi[...] + back
    dc_ref[top] += dot_tb(dyr[top], e0)
    dc_ref[end] += dot_tb(dyr[end], e1)
    db_ref[top] += dot_tb(wt[top], r0)
    db_ref[end] += dot_tb(wt[end], r1)
    wv_ref[0] += dot((dy * yn).astype(BF16), seg[...])
    wv_ref[1] += dot((x * dxn).astype(BF16), seg[...])
    xb = x * back
    ends_ref[...] = jnp.concatenate(
        [
            jnp.sum(xb[top], axis=0, keepdims=True)
            + d0 * jnp.sum(r0.astype(F32) * e0.astype(F32), axis=0, keepdims=True),
            jnp.sum(xb[end], axis=0, keepdims=True)
            + d1 * jnp.sum(r1.astype(F32) * e1.astype(F32), axis=0, keepdims=True),
            jnp.sum(x * dy, axis=0, keepdims=True),
            jnp.zeros((5, SUB), F32),
        ],
        axis=0,
    )
    ds = (dxn + skip * dy) * sl[...].astype(F32)
    gx, dw = conv_back(ds, xs, gs, w, 2 * Q)
    red_ref[...] = dw
    head_ref[...] = ds[0:8]
    gy[0] = (yn + skip * x).astype(BF16)
    gy[1] = gx.astype(BF16)


def finish_group(
    yv, b_own, c_own, b_rec, c_rec, b_halo, c_halo, wb, wc, slope, bc, cc, parts,
    gb_ref, gc_ref, red_ref, head_ref, send_ref, xs, gs, gv,
):
    y = yv[0]
    dc, db, dcb = [sum(r[...] for r in refs[1:]) + refs[0][...] for refs in zip(*parts)]
    dcb = dcb.astype(BF16)
    for b in range(2):
        at = slice(b * Q, b * Q + Q)
        gv[0, at] = db[at] + dot_ta(dcb[b], cc[at])
        gv[1, at] = dc[at] + dot(dcb[b], bc[at])
    for i, (own, rec, halo, w, out) in enumerate(
        ((b_own, b_rec, b_halo, wb, gb_ref), (c_own, c_rec, c_halo, wc, gc_ref))
    ):
        cs = slice(i * N, (i + 1) * N)
        xs[0:8] = halo[...]
        in_order(y, own[...], rec[...], xs, 8)
        ds = gv[i] * slope[i]
        gx, dw = conv_back(ds, xs, gs, w, 2 * Q)
        red_ref[:, cs] = dw
        head_ref[:, cs] = ds[0:8]

        @pl.when(y == 0)
        def _():
            out[...] = gx[0:Q].astype(BF16)
            send_ref[:, cs] = gx[Q:].astype(BF16)

        @pl.when(y != 0)
        def _():
            out[...] = gx[Q:].astype(BF16)
            send_ref[:, cs] = gx[0:Q].astype(BF16)


def finish_views(yv, g, b, c, rec, halo, w, slopes, bc, cc, gb, gc, red, head):
    groups = bc.shape[1] // N
    half = halo.shape[1] - 2 * groups * N
    wide = 2 * half
    gs = slice(g * N, (g + 1) * N)
    own = pl.ds(pl.multiple_of((yv[0] * groups + g) * N, N), N)

    def weights(i):
        return pl.ds(pl.multiple_of(wide + (2 * i * groups + yv[0] * groups + g) * N, N), N)

    return (
        b.at[:, own], c.at[:, own], rec.at[:, gs], rec.at[:, (groups + g) * N : (groups + g + 1) * N],
        halo.at[:, half + g * N : half + (g + 1) * N],
        halo.at[:, half + (groups + g) * N : half + (groups + g + 1) * N],
        w.at[:, weights(0)], w.at[:, weights(1)], slopes.at[:, :, gs], bc.at[:, gs], cc.at[:, gs],
    ), (gb, gc, red, head)


def finish_kernel(
    yv, b, c, rec, halo, w, slopes, bc, cc, dc0, db0, dcb0, dc1, db1, dcb1,
    red, head, gb, gc, send_ref, xs, gs, gv,
):
    ins, outs = finish_views(yv, 0, b, c, rec, halo, w, slopes, bc, cc, gb, gc, red, head)
    finish_group(yv, *ins, [(dc0, db0, dcb0), (dc1, db1, dcb1)], *outs, send_ref, xs, gs, gv)
    for ref in outs[2:]:
        ref[:, 2 * N :] = jnp.zeros((8, ref.shape[1] - 2 * N), F32)


def finish_last_kernel(
    yv, b, c, rec, halo, w, slopes, bc, cc, dc0, db0, dcb0, dc1, db1, dcb1, st, par, seg, before, *rest,
):
    chunks = (len(rest) - 11) // 3
    wvs, ends, tops = [rest[i * chunks : (i + 1) * chunks] for i in range(3)]
    rest = rest[3 * chunks :]
    red, head, gb, gc, send_ref, gdt_ref, next_ref, xs, gs, gv, gd = rest
    y = yv[0]
    ins, outs = finish_views(yv, 1, b, c, rec, halo, w, slopes, bc, cc, gb, gc, red, head)
    finish_group(yv, *ins, [(dc0, db0, dcb0), (dc1, db1, dcb1)], *outs, send_ref, xs, gs, gv)
    red_ref, head_ref = red, head
    heads = par.shape[1]
    step, raw = st[:, 0:heads], st[:, heads:]
    rate = jnp.exp(par[0:1])
    cw = ends[0].shape[1]
    w_sum = sum(wv[0] for wv in wvs[1:]) + wvs[0][0]
    v_sum = sum(wv[1] for wv in wvs[1:]) + wvs[0][1]
    e_sum = split_dot(ends[0][...], seg[0:cw])
    for i in range(1, chunks):
        e_sum = e_sum + split_dot(ends[i][...], seg[i * cw : (i + 1) * cw])
    tri = jnp.where(triangle(False), 1.0, 0.0).astype(BF16)
    diff = w_sum - v_sum
    dl = jnp.concatenate(
        [exact_dot(tri, diff[0:Q]) + e_sum[0:1], exact_dot(tri, diff[Q:]) + e_sum[1:2]], axis=0
    )
    draw = (v_sum / step - rate * dl) / (1.0 + jnp.exp(-raw))
    red_ref[:, 2 * N :] = jnp.concatenate(
        [
            jnp.concatenate(
                [
                    jnp.sum(dl * (-rate * step), axis=0, keepdims=True),
                    jnp.sum(draw, axis=0, keepdims=True),
                    e_sum[2:3],
                    jnp.zeros((5, heads), F32),
                ],
                axis=0,
            ),
            jnp.zeros((8, red_ref.shape[1] - 2 * N - heads), F32),
        ],
        axis=1,
    )
    head_ref[:, 2 * N :] = jnp.zeros((8, head_ref.shape[1] - 2 * N), F32)
    items = []
    for r in range(3):
        row = slice(r, r + 1)
        items += [v[row] for v in tops]
        items.append(
            jnp.concatenate(
                [
                    before[row, 0:N], head_ref[row, 0:N],
                    before[row, N : 2 * N], head_ref[row, N : 2 * N],
                ],
                axis=1,
            )
        )
    items.append(jnp.zeros((16 - 3 * (chunks + 1), cw), F32))
    next_ref[...] = jnp.concatenate(items, axis=0)
    gd[...] = jnp.concatenate([draw, draw], axis=1).astype(BF16)

    @pl.when(y == 0)
    def _():
        gdt_ref[...] = gd[0:Q]
        send_ref[:, 2 * N :] = gd[Q:]

    @pl.when(y != 0)
    def _():
        gdt_ref[...] = gd[Q:]
        send_ref[:, 2 * N :] = gd[0:Q]


def add_kernel(yv, *refs):
    total = refs[0][...]
    for r in refs[1:-1]:
        total = total + r[...]
    refs[-1][...] = total


def gather_kernel(yv, *refs, side, count):
    out = refs[-1]
    more = refs[2 * count : -1]

    def fill(k):
        at = 0
        for r in refs[k * count : (k + 1) * count]:
            width = r.shape[1]
            total = r[...]
            for m in more:
                total = total + m[:, at : at + width]
            out[:, at : at + width] = total
            at += width

    for core in range(2):

        @pl.when(yv[3] == core)
        def _():
            fill(1 - core if side else core)


def join_kernel(yv, first, second, out):
    out[0] = first[...]
    out[1] = second[...]


def spread(yv, own, got, dst):
    width = own[0].shape[1]
    for k in range(2):

        @pl.when(yv[0] == k)
        def _():
            for g in range(2):
                at = (k * 2 + g) * width
                dst[:, at : at + width] = own[g][...].astype(F32)
                at = ((1 - k) * 2 + g) * width
                dst[:, at : at + width] = got[g].astype(F32)


def rim_kernel(
    yv, next0, next_e, next_o, w, b0, b1, c0, c1, got0, got1, gdt_own, gx,
    gx_ref, gb_ref, gc_ref, gdt_ref, mark, both, full,
):
    mark[...] = jnp.zeros(mark.shape, F32)
    lane = lax.broadcasted_iota(jnp.int32, gdt_own.shape, 1)
    low = lane < gdt_own.shape[1] // 2
    own, got = gdt_own[...].astype(F32), got1[:, 2 * N :].astype(F32)

    @pl.when(yv[0] == 0)
    def _():
        gdt_ref[...] = jnp.where(low, own, got).astype(BF16)

    @pl.when(yv[0] != 0)
    def _():
        gdt_ref[...] = jnp.where(low, got, own).astype(BF16)

    spread(yv, (b0, b1), [r[:, 0:N] for r in (got0, got1)], full.at[0])
    spread(yv, (c0, c1), [r[:, N : 2 * N] for r in (got0, got1)], full.at[1])
    gb_ref[...] = full[0].astype(BF16)
    gc_ref[...] = full[1].astype(BF16)
    rows = slice(Q - 16, Q)
    both[0] = next0[...]

    @pl.when(yv[2] == 0)
    def _():
        both[1] = next_e[...]

    @pl.when(yv[2] != 0)
    def _():
        both[1] = next_o[...]

    step = next0.shape[1]
    blocks = gx.shape[1] // 2 // step
    keep = jnp.where((yv[0] == 0) | (yv[4] == 0), 0.0, 1.0)

    def add(src, dst, lo, half, block, at, width, to):
        h = [keep * both[half, r * (blocks + 1) + block : r * (blocks + 1) + block + 1, at : at + width] for r in range(3)]
        k = w[:, lo : lo + width]
        more = jnp.concatenate(
            [
                jnp.zeros((13, width), F32),
                k[0:1] * h[0],
                k[0:1] * h[1] + k[1:2] * h[0],
                k[0:1] * h[2] + k[1:2] * h[1] + k[2:3] * h[0],
            ],
            axis=0,
        )
        dst[:, to : to + width] = (src[:, to : to + width].astype(F32) + more).astype(BF16)

    for half in range(2):
        for i in range(blocks):
            at = (half * blocks + i) * step
            add(gx, gx_ref, at, half, i, 0, step, at)
        for i, (src, dst) in enumerate(((full.at[0, rows], gb_ref.at[rows]), (full.at[1, rows], gc_ref.at[rows]))):
            to = half * step // 2
            add(src, dst, (2 * blocks + i) * step + to, half, blocks, i * step // 2, step // 2, to)


def sums_kernel(yv, mine, theirs, gw_ref, gb_ref, gh_ref, both, *, wide, heads):
    width = mine.shape[2]

    @pl.when(yv[3] == 0)
    def _():
        both[:, :, 0:width] = mine[...]
        both[:, :, width:] = theirs[...]

    @pl.when(yv[3] != 0)
    def _():
        both[:, :, 0:width] = theirs[...]
        both[:, :, width:] = mine[...]

    step = width - wide // 2

    def fill(order):
        for k in range(2):
            v = both[order[k]]
            for i in range(2):
                to, at = k * wide + i * (wide // 2), i * width + step
                gw_ref[:, to : to + wide // 2] = v[0:4, at : at + wide // 2]
                gb_ref[:, to : to + wide // 2] = v[4:5, at : at + wide // 2]
            for i in range(2):
                for g in range(2):
                    to = 2 * wide + i * 4 * N + (2 * k + g) * N
                    gw_ref[:, to : to + N] = v[0:4, g * width + i * N : g * width + (i + 1) * N]
                    gb_ref[:, to : to + N] = v[4:5, g * width + i * N : g * width + (i + 1) * N]
        at = width + 2 * N
        values = jnp.concatenate(
            [both[order[0]][:, at : at + heads], both[order[1]][:, at : at + heads]], axis=1
        )
        per_dev = gh_ref.shape[1]
        row = lax.broadcasted_iota(jnp.int32, (2 * heads, per_dev), 0)
        col = lax.broadcasted_iota(jnp.int32, (2 * heads, per_dev), 1)
        pick = jnp.where(row == col + yv[5] * per_dev, 1.0, 0.0).astype(BF16)
        hi = values.astype(BF16)
        rest = values - hi.astype(F32)
        mid = rest.astype(BF16)
        low = (rest - mid.astype(F32)).astype(BF16)
        gh_ref[...] = (dot(hi, pick) + dot(mid, pick) + dot(low, pick))[0:3]

    @pl.when(yv[0] == 0)
    def _():
        fill((0, 1))

    @pl.when(yv[0] != 0)
    def _():
        fill((1, 0))


def whole(shape):
    return pl.BlockSpec(shape, lambda *_: (0,) * len(shape))


def shape_of(*dims, dtype=F32):
    return jax.ShapeDtypeStruct(dims, dtype)


def call(kernel, yv, ins, outs, scratch, micros, nbytes, keep=(), after=(), hbm=()):
    count = len(ins)
    extra = len(keep) + len(after)

    def run(yr, *refs):
        kernel(yr, *refs[:count], *refs[count + extra :])

    near = pl.BlockSpec(memory_space=pltpu.MemorySpace.VMEM)
    anywhere = pl.BlockSpec(memory_space=pl.ANY)
    ins = [i if isinstance(i, tuple) else (i, near) for i in ins]
    return pl.pallas_call(
        run,
        out_shape=outs,
        in_specs=[pl.BlockSpec(memory_space=pltpu.MemorySpace.SMEM)]
        + [i[1] for i in ins]
        + [anywhere if k in hbm else near for k in range(len(keep))]
        + [anywhere] * len(after),
        out_specs=[anywhere if k in hbm else near for k in range(len(outs))],
        scratch_shapes=scratch,
        compiler_params=params(),
        cost_estimate=cost(micros, nbytes),
        input_output_aliases={1 + count + k: k for k in range(len(keep))},
    )(yv, *[i[0] for i in ins], *keep, *after)


def per_device(
    ssm_input, b_input, c_input, dt_input, conv_weight, conv_bias, a_log, dt_bias, skip_gain, grad_out
):
    x_rows, b_rows, c_rows = ssm_input[0], b_input[0], c_input[0]
    dt_rows, dy_rows = dt_input[0], grad_out[0]
    devices = lax.axis_size("sp")
    dp_size = lax.axis_size("dp")
    spots = devices // 2
    me = lax.axis_index("sp")
    y = lax.rem(me, 2)
    z = me // 2
    core = lax.rem(lax.axis_index("dp"), 2)
    yv = jnp.stack([y, z, lax.rem(z, 2), core, spots - 1 - z, me]).astype(jnp.int32)
    xw = x_rows.shape[1] // 2
    bw = b_rows.shape[1] // 2
    hl = dt_rows.shape[1] // 2
    chunks = 4
    cw = xw // chunks
    subs = cw // SUB
    groups = bw // N
    per_group = chunks // groups
    two = 2 * Q
    piece = 2 * N + 2 * hl
    base = groups * piece
    bands = base // SUB
    bias = conv_bias[None]

    def pairs(fn, n=devices):
        return [(i, fn(i)) for i in range(n) if fn(i) is not None and 0 <= fn(i) < n]

    swap = pairs(lambda i: i ^ 1)

    def joint(v, fn):
        moves = []
        for d in range(dp_size):
            for i in range(devices):
                to = fn(i)
                if to is None or not 0 <= to < devices:
                    moves.append((d * devices + i, (d ^ 1) * devices + i))
                else:
                    moves.append((d * devices + i, d * devices + to))
        return lax.ppermute(v, ("dp", "sp"), moves)

    def slant(i):
        return i + 1 if i % 2 else i - 1

    def evens(i):
        return i ^ 2

    def odds(i):
        return ((i + 2) ^ 2) - 2 if 2 <= i < devices - 2 else None

    in_hbm = pl.BlockSpec(memory_space=pltpu.MemorySpace.HBM)
    anywhere = pl.BlockSpec(memory_space=pl.ANY)
    msg, rim_out = call(
        pack_small_kernel, yv, [(x_rows, in_hbm), b_rows, c_rows, dt_rows],
        [shape_of(Q, 2 * bw + 2 * hl, dtype=BF16), shape_of(32, 2 * bw, dtype=BF16)],
        [
            pltpu.VMEM((16, 2 * xw), BF16), pltpu.VMEM((16, 2 * bw), BF16),
            pltpu.VMEM((16, 2 * bw), BF16), pltpu.SemaphoreType.DMA((3,)), pltpu.SemaphoreType.DMA((3,)),
        ],
        1, 1 << 20, hbm=(0,),
    )
    rec_bc = lax.ppermute(msg, "sp", swap)
    (rim_out,) = call(
        gate_kernel, yv, [rim_out], [shape_of(32, 2 * bw, dtype=BF16)], [], 1, 1 << 10, after=[rec_bc]
    )
    rim = joint(rim_out, slant)
    rim_e = joint(rim_out, evens)
    rim_o = joint(rim_out, odds)
    rec = []

    def send_chunk(c, after):
        def kernel(*refs):
            pack_kernel(*refs, chunk=c, chunks=chunks)

        (out,) = call(
            kernel, yv, [x_rows, dy_rows], [shape_of(2, Q, cw, dtype=BF16)],
            [pltpu.SemaphoreType.DMA((2,))], 1, 1 << 20, after=after, hbm=(0,),
        )
        rec.append(lax.ppermute(out, "sp", swap))

    send_chunk(0, [msg])

    par = lax.dynamic_slice_in_dim(
        jnp.concatenate([jnp.stack([a_log, dt_bias, skip_gain]), jnp.zeros((5, 2 * hl), F32)], 0),
        y * hl, hl, 1,
    )
    lanes = np.arange(xw) // HEAD
    expand = (np.arange(hl)[:, None] == lanes[None, :]).astype(BF16)
    exp2 = jnp.asarray(np.concatenate([expand, expand], axis=0))
    seg = jnp.asarray(np.ascontiguousarray(expand.T))

    nq = hl // 4
    halo, bcc, ccc, bct, cct, slopes, fe, rows, qcols, rowt, st = call(
        setup_whole, yv,
        [b_rows, c_rows, dt_rows, rec_bc, rim, rim_e, rim_o, conv_weight, bias, par, exp2],
        [
            shape_of(8, xw + 2 * bw), shape_of(two, bw, dtype=BF16), shape_of(two, bw, dtype=BF16),
            shape_of(bw, two, dtype=BF16), shape_of(bw, two, dtype=BF16), shape_of(2, two, bw),
            shape_of(2, two, 2 * hl, dtype=BF16), shape_of(8, xw), shape_of(nq, two, 8),
            shape_of(nq, 8, two), shape_of(two, 2 * hl),
        ],
        [
            pltpu.VMEM((two + 8, bw), F32), pltpu.VMEM((two, hl), F32),
            pltpu.VMEM((2 * hl, two), F32), pltpu.VMEM((16, rim.shape[1]), F32),
        ],
        4, 4 << 20,
    )
    send_chunk(1, [rec_bc])
    states = []
    xcs, dyos, sls = [], [], []
    long = pltpu.VMEM((two + 8, SUB), F32)

    def state(c, after):
        nonlocal states
        big = shape_of(chunks, N, cw, dtype=BF16)
        tall = shape_of(two, cw, dtype=BF16)

        def kernel(*refs):
            state_chunk(*refs, chunk=c, per_group=per_group)

        t, u, xc, dyo, sl = call(
            kernel, yv,
            [x_rows, dy_rows, rec[c], halo, conv_weight, bias, bct, cct, fe, exp2, rows],
            [big, big, tall, tall, tall],
            [long, pltpu.VMEM((2, N, cw), BF16), pltpu.SemaphoreType.DMA((2,))], 3, 4 << 20,
            keep=states, after=after, hbm=(0, 1),
        )
        states = [t, u]
        xcs.append(xc)
        dyos.append(dyo)
        sls.append(sl)
        return xc

    yis, dxis, dcbs = [], [], []

    def within(c, after):
        def kernel(*refs):
            within_chunk(*refs, chunk=c, per_group=per_group)

        yi, dxi, dcb = call(
            kernel, yv, [xcs[c], dyos[c], qcols, rowt, bcc, ccc],
            [shape_of(two, cw), shape_of(two, cw), shape_of(2, Q, Q)],
            [pltpu.VMEM((4, Q, Q), F32)], 3, 4 << 20, after=after,
        )
        yis.append(yi)
        dxis.append(dxi)
        dcbs.append(dcb)
        return dcb

    finals = []
    sums = []
    reds, edges = [], []
    got_x = []

    def across(c, ents, leas, after):
        nonlocal finals
        full = shape_of(Q, 2 * xw, dtype=BF16)
        strip = shape_of(8, cw)

        def kernel(*refs):
            across_chunk(*refs, chunk=c, chunks=chunks, per_group=per_group)

        out = call(
            kernel, yv,
            [
                x_rows, rec[c], halo, conv_weight, xcs[c], dyos[c], sls[c], yis[c], dxis[c],
                bcc, ccc, bct, cct, fe, exp2, seg, rows,
            ] + [(v, anywhere) for v in ents + leas],
            [
                full, full, strip, strip, shape_of(2, Q, cw, dtype=BF16), shape_of(two, N),
                shape_of(two, N), shape_of(2, two, hl), shape_of(8, cw),
            ],
            [
                long, long, pltpu.VMEM((2, two, cw), BF16), pltpu.VMEM((N, cw), BF16),
                pltpu.VMEM((N, cw), BF16), pltpu.SemaphoreType.DMA((2 * halves_,)), pltpu.SemaphoreType.DMA((3,)),
            ],
            6, 6 << 20, keep=finals, after=after, hbm=(0, 1),
        )
        finals = list(out[:2])
        reds.append(out[2])
        edges.append(out[3])
        sums.append(out[5:])
        got_x.append(lax.ppermute(out[4], "sp", swap))
        return out[8]

    def unpack(c, after):
        full = shape_of(Q, 2 * xw, dtype=BF16)

        def kernel(*refs):
            unpack_kernel(*refs, chunk=c, chunks=chunks)

        *finals[:2], mark = call(
            kernel, yv, [(got_x[c], anywhere)], [full, full, shape_of(8, 128)],
            [pltpu.SemaphoreType.DMA((2,))], 1, 1 << 20, keep=finals[:2], after=after, hbm=(0, 1),
        )
        return mark

    grads_bc = []
    group_reds, group_edges = [], []

    def finish(g, last, after):
        own = shape_of(Q, N, dtype=BF16)
        strip = shape_of(8, piece)
        ins = [b_rows, c_rows, rec_bc, halo, conv_weight, slopes, bcc, ccc]
        for c in range(g * per_group, (g + 1) * per_group):
            ins += [sums[c][0], sums[c][1], dcbs[c]]
        outs = [strip, strip, own, own, shape_of(Q, piece if last else 2 * N, dtype=BF16)]
        narrow = pltpu.VMEM((two + 8, N), F32)
        scratch = [narrow, narrow, pltpu.VMEM((2, two, N), F32)]
        if last:
            ins += [st, par, seg, group_edges[0]] + [v[2] for v in sums] + [v[3] for v in sums] + edges
            outs += [shape_of(Q, 2 * hl, dtype=BF16), shape_of(16, cw)]
            scratch.append(pltpu.VMEM((two, 2 * hl), BF16))
        out = call(
            finish_last_kernel if last else finish_kernel, yv, ins, outs, scratch, 3, 4 << 20, after=after
        )
        group_reds.append(out[0])
        group_edges.append(out[1])
        grads_bc.append(out[2:4])
        return lax.ppermute(out[4], "sp", swap), out[4:]

    halves_ = 2
    part = cw // halves_
    zero = jnp.zeros((N, part), BF16)
    ins_e = [[zero] for _ in range(halves_)]
    ins_o = [[zero] for _ in range(halves_)]
    steps = chunks + spots - 2
    state(0, [])
    got_bc = []
    waits = []
    for t in range(steps + 1):
        for i in range(halves_):
            token = []
            if t < steps:
                moving = shape_of(N, part, dtype=BF16)

                def kernel(*refs, step=t, lane=i):
                    hop_kernel(*refs, step=step, part=lane)

                out_e, out_o = call(
                    kernel, yv, [ins_e[i][-1], ins_o[i][-1], states[0], states[1], rows],
                    [moving, moving], [], 1, 3 << 20, after=waits,
                )
                token = [out_e]
                ins_e[i].append(joint(out_e, evens))
                ins_o[i].append(joint(out_o, odds))
            if t == 0 and i == 0:
                send_chunk(2, token)
            waits = []
            if i == 0 and t < chunks - 1:
                waits.append(within(t, token))
            if i == 1 and t + 1 < chunks:
                waits.append(state(t + 1, token))
                if t + 3 < chunks:
                    send_chunk(t + 3, [rec[t + 1]])
            c = t + 1 - spots
            if i == 0 and 0 <= c < chunks:
                if c == chunks - 1:
                    token = []
                ents, leas = [], []
                for k in range(1, spots):
                    for h in range(halves_):
                        ents.append((ins_o if k % 2 == 0 else ins_e)[h][c + k])
                        leas.append((ins_o if (spots - 1 - k) % 2 else ins_e)[h][c + k])
                waits.append(across(c, ents, leas, token))
            if i == 1 and c == 0:
                waits.append(within(chunks - 1, token))
            if i == 1 and c == chunks - 2:
                mark = unpack(0, token)
                got, tok = finish(0, False, token)
                got_bc.append(got)
                waits += [tok[0], mark]
    got, (_, gdt_own, next_rows) = finish(1, True, [])
    got_bc.append(got)

    hw = (base + xw) // 2
    slab = shape_of(8, hw)

    def add(items, after=()):
        (out,) = call(add_kernel, yv, items, [slab], [], 1, 1 << 20, after=after)
        return out

    per_side = chunks // 2
    pieces = []
    for k in range(2):
        pieces += [group_reds[k]] + reds[k * per_side : (k + 1) * per_side]

    def gather(side, more):
        def kernel(*refs):
            gather_kernel(*refs, side=side, count=1 + per_side)

        (out,) = call(kernel, yv, pieces + more, [slab], [], 1, 1 << 20)
        return out

    theirs = gather(True, [])
    mine = gather(False, [lax.ppermute(theirs, "dp", pairs(lambda i: i ^ 1, dp_size))])
    size = 2
    while size < dp_size:
        got = lax.ppermute(mine, "dp", pairs(lambda i: i ^ size, dp_size))
        marks = []
        if size == 2:
            marks = [unpack(1, [mine]), unpack(2, [mine])]
        mine = add([mine, got], marks)
        size *= 2
    mark = unpack(3, [mine])
    y_all, gx_all = finals[:2]
    next0 = joint(next_rows, slant)
    next_e = joint(next_rows, evens)
    next_o = joint(next_rows, odds)
    last = pl.BlockSpec((16, 2 * xw), lambda j, yr: (Q // 16 - 1, 0))
    small = [next0, next_e, next_o, conv_weight] + [grads_bc[g][i] for i in range(2) for g in range(2)]
    small += [got_bc[0], got_bc[1], gdt_own]
    full = shape_of(Q, 2 * bw, dtype=BF16)
    grad_x, grad_b, grad_c, gdt, rim_mark = pl.pallas_call(
        rim_kernel,
        out_shape=[shape_of(Q, 2 * xw, dtype=BF16), full, full, shape_of(Q, 2 * hl, dtype=BF16), shape_of(8, 128)],
        grid_spec=pltpu.PrefetchScalarGridSpec(
            num_scalar_prefetch=1,
            grid=(1,),
            in_specs=[whole(v.shape) for v in small] + [last],
            out_specs=[last, whole(full.shape), whole(full.shape), whole((Q, 2 * hl)), whole((8, 128))],
            scratch_shapes=[pltpu.VMEM((2, 16, cw), F32), pltpu.VMEM((2, Q, 2 * bw), F32)],
        ),
        compiler_params=params(),
        cost_estimate=cost(1, 1 << 20),
        input_output_aliases={1 + len(small): 0},
    )(yv, *small, gx_all)

    size = 2
    while size < devices:
        ways = 4 if size * 4 <= devices else 2
        got = [lax.ppermute(mine, "sp", pairs(lambda i: i ^ (size * k))) for k in range(1, ways)]
        size *= ways
        mine = add([mine] + got, [mark] if size >= devices else [])
    got_y = lax.ppermute(mine, "sp", swap)

    (mine,) = call(
        join_kernel, yv, [mine, got_y], [shape_of(2, 8, hw)], [], 1, 1 << 20, after=[rim_mark]
    )
    theirs = lax.ppermute(mine, "dp", pairs(lambda i: i ^ 1, dp_size))
    per_dev = 2 * hl // devices

    def summed(*refs):
        sums_kernel(*refs, wide=xw, heads=hl)

    gw, gbias, gheads = pl.pallas_call(
        lambda yr, a, b, unused, *refs: summed(yr, a, b, *refs),
        out_shape=[
            shape_of(4, bias.shape[1]), shape_of(1, bias.shape[1]), shape_of(3, per_dev),
        ],
        grid_spec=pltpu.PrefetchScalarGridSpec(
            num_scalar_prefetch=1,
            grid=(1,),
            in_specs=[whole(mine.shape), whole(theirs.shape), anywhere],
            out_specs=[
                whole((4, bias.shape[1])), whole((1, bias.shape[1])), whole((3, per_dev)),
            ],
            scratch_shapes=[pltpu.VMEM((2, 8, base + xw), F32)],
        ),
        compiler_params=params(),
        cost_estimate=cost(1, 1 << 20),
    )(yv, mine, theirs, rim_mark)
    return (
        y_all[None], grad_x[None], grad_b[None], grad_c[None], gdt[None], gw, gbias[0], gheads,
    )


def solution(mesh):
    rows = P("dp", "sp", None)
    in_specs = (rows, rows, rows, rows, P(), P(), P(), P(), P(), rows)
    out_specs = (rows, rows, rows, rows, rows, P(), P(), P(None, "sp"))
    return jax.shard_map(
        per_device, mesh=mesh, in_specs=in_specs, out_specs=out_specs, check_vma=False
    )
```

```python
import jax
import jax.numpy as jnp
from jax import lax
from jax.experimental import pallas as pl
from jax.experimental.pallas import tpu as pltpu
from jax.sharding import PartitionSpec as P

N = 256
Q = 128
HEAD = 64
SUB = 256
LOG2E = 1.4426950408889634
F32 = jnp.float32
BF16 = jnp.bfloat16
NEG = -1e30


def params():
    return pltpu.CompilerParams(vmem_limit_bytes=14 * 1024 * 1024)


def cost(micros, nbytes):
    return pl.CostEstimate(flops=int(micros * 1e9), bytes_accessed=nbytes, transcendentals=0)


def dot(a, b):
    return jnp.dot(a, b, preferred_element_type=F32)


def dot_tb(a, b):
    return lax.dot_general(a, b, (((1,), (1,)), ((), ())), preferred_element_type=F32)


def dot_ta(a, b):
    return lax.dot_general(a, b, (((0,), (0,)), ((), ())), preferred_element_type=F32)


def halves(v):
    hi = v.astype(BF16)
    return hi, (v - hi.astype(F32)).astype(BF16)


def split_dot(v, m):
    hi, lo = halves(v)
    return dot(hi, m) + dot(lo, m)


def exact_dot(m, v):
    hi = v.astype(BF16)
    rest = v - hi.astype(F32)
    mid = rest.astype(BF16)
    low = (rest - mid.astype(F32)).astype(BF16)
    return dot(m, hi) + dot(m, mid) + dot(m, low)


def triangle(lower):
    row = lax.broadcasted_iota(jnp.int32, (Q, Q), 0)
    col = lax.broadcasted_iota(jnp.int32, (Q, Q), 1)
    return row >= col if lower else row <= col


def in_order(y, own, rec, dst, first=0):
    rows = own.shape[0]

    @pl.when(y == 0)
    def _():
        dst[first : first + rows] = own.astype(dst.dtype)
        dst[first + rows : first + 2 * rows] = rec.astype(dst.dtype)

    @pl.when(y != 0)
    def _():
        dst[first : first + rows] = rec.astype(dst.dtype)
        dst[first + rows : first + 2 * rows] = own.astype(dst.dtype)


def conv_sum(xs, w, bias, rows):
    total = bias[...]
    for k in range(4):
        total = total + w[k : k + 1] * xs[5 + k : 5 + k + rows]
    return total


def gates(s):
    sig = 0.5 + 0.5 * jnp.tanh(0.5 * s)
    out = s * sig
    return out, sig + out * (1.0 - sig)


def conv_back(ds, xs, gs, w, rows):
    gs[0:rows] = ds
    gs[rows : rows + 8] = jnp.zeros((8, ds.shape[1]), F32)
    dx = w[3:4] * ds
    for k in range(3):
        dx = dx + w[k : k + 1] * gs[3 - k : 3 - k + rows]
    dw = [jnp.sum(ds * xs[5 + k : 5 + k + rows], axis=0, keepdims=True) for k in range(4)]
    dw.append(jnp.sum(ds, axis=0, keepdims=True))
    dw.append(jnp.zeros((3, ds.shape[1]), F32))
    return dx, jnp.concatenate(dw, axis=0)


def copies(pairs, sems):
    moves = [pltpu.make_async_copy(src, dst, sems.at[i]) for i, (src, dst) in enumerate(pairs)]
    for m in moves:
        m.start()
    for m in moves:
        m.wait()


def pack_rim_kernel(yv, x, b, c, out, xt, bt, ct, sems):
    half = x.shape[1] // 2
    width = b.shape[1] // 2
    step = 2 * width
    copies([(src.at[pl.ds(Q - 16, 16)], dst) for src, dst in ((x, xt), (b, bt), (c, ct))], sems)
    x3, b3, c3 = [r[...].astype(F32)[13:16] for r in (xt, bt, ct)]
    blocks = half // step + 1
    for k in range(2):
        items = []
        for r in range(3):
            for i in range(blocks - 1):
                at = k * half + i * step
                items.append(x3[r : r + 1, at : at + step])
            mine = slice(k * width, (k + 1) * width)
            items.append(jnp.concatenate([b3[r : r + 1, mine], c3[r : r + 1, mine]], axis=1))
        items.append(jnp.zeros((16 - 3 * blocks, step), F32))
        out[16 * k : 16 * (k + 1)] = jnp.concatenate(items, axis=0).astype(BF16)


def pack_small_kernel(yv, x, b, c, dt, out, rim, xt, bt, ct, sems, rim_sems):
    width = b.shape[1] // 2
    at = pl.multiple_of((1 - yv[0]) * width, 128)
    moves = [
        pltpu.make_async_copy(src, dst, sems.at[i])
        for i, (src, dst) in enumerate(
            (
                (b.at[:, pl.ds(at, width)], out.at[:, pl.ds(0, width)]),
                (c.at[:, pl.ds(at, width)], out.at[:, pl.ds(width, width)]),
                (dt, out.at[:, pl.ds(2 * width, dt.shape[1])]),
            )
        )
    ]
    for m in moves:
        m.start()
    pack_rim_kernel(yv, x, b, c, rim, xt, bt, ct, rim_sems)
    for m in moves:
        m.wait()


def gate_kernel(yv, src, dst):
    dst[...] = src[...]


def pack_kernel(yv, x, dy, out, sems, *, chunk, chunks):
    width = out.shape[2]
    at = pl.multiple_of(((1 - yv[0]) * chunks + chunk) * width, 128)
    copies([(x.at[:, pl.ds(at, width)], out.at[0]), (dy.at[:, pl.ds(at, width)], out.at[1])], sems)


def unpack_kernel(yv, got, y_ref, gx_ref, mark, sems, *, chunk, chunks):
    width = got.shape[2]
    at = pl.multiple_of(((1 - yv[0]) * chunks + chunk) * width, 128)
    copies([(got.at[0], y_ref.at[:, pl.ds(at, width)]), (got.at[1], gx_ref.at[:, pl.ds(at, width)])], sems)
    mark[...] = jnp.zeros(mark.shape, F32)


def setup_kernel(
    yv, b_own, c_own, dt_own, rec, rim, rim_e, rim_o, wb, wc, bb, bc_, par, exp2, seg_ref,
    halo_ref, bc_ref, cc_ref, bt_ref, ct_ref, ds_ref, fe_ref, rows_ref, cols_ref, rowt_ref, st_ref,
    xs, dts, xs2, rims,
):
    y = yv[0]
    width = b_own.shape[1]
    heads = par.shape[1]
    row = lax.broadcasted_iota(jnp.int32, exp2.shape, 0)
    lane = lax.broadcasted_iota(jnp.int32, exp2.shape, 1)
    exp2[...] = jnp.where(lane // HEAD == lax.rem(row, heads), 1.0, 0.0).astype(BF16)
    row = lax.broadcasted_iota(jnp.int32, seg_ref.shape, 0)
    lane = lax.broadcasted_iota(jnp.int32, seg_ref.shape, 1)
    seg_ref[...] = jnp.where(row // HEAD == lane, 1.0, 0.0).astype(BF16)
    half = halo_ref.shape[1] - 2 * width

    @pl.when(y == 0)
    def _():
        rims[...] = rim[0:16].astype(F32)

    @pl.when((y != 0) & (yv[2] == 0))
    def _():
        rims[...] = rim_o[16:32].astype(F32)

    @pl.when((y != 0) & (yv[2] != 0))
    def _():
        rims[...] = rim_e[16:32].astype(F32)

    blocks = halo_ref.shape[1] // rim.shape[1]
    keep = jnp.where(yv[1] == 0, 0.0, 1.0)
    halo_ref[...] = keep * jnp.concatenate(
        [jnp.zeros((5, halo_ref.shape[1]), F32)]
        + [
            jnp.concatenate([rims[r * blocks + i : r * blocks + i + 1] for i in range(blocks)], axis=1)
            for r in range(3)
        ],
        axis=0,
    )
    for i, (own, w, bias, out, out_t) in enumerate(
        ((b_own, wb, bb, bc_ref, bt_ref), (c_own, wc, bc_, cc_ref, ct_ref))
    ):
        at = i * width
        xs[0:8] = halo_ref[:, half + at : half + at + width]
        in_order(y, own[...], rec[0:Q, at : at + width], xs, 8)
        v, slope = gates(conv_sum(xs, w, bias, 2 * Q))
        out[...] = v.astype(BF16)
        out_t[...] = jnp.transpose(v).astype(BF16)
        ds_ref[i] = slope

    @pl.when(y == 0)
    def _():
        dts[0:Q] = dt_own[:, 0:heads].astype(F32)
        dts[Q : 2 * Q] = rec[0:Q, 2 * width : 2 * width + heads].astype(F32)

    @pl.when(y != 0)
    def _():
        dts[0:Q] = rec[0:Q, 2 * width + heads : 2 * width + 2 * heads].astype(F32)
        dts[Q : 2 * Q] = dt_own[:, heads : 2 * heads].astype(F32)

    raw = dts[...] + par[1:2]
    step = jnp.log1p(jnp.exp(raw))
    logs = -step * jnp.exp(par[0:1])
    tri = jnp.where(triangle(True), 1.0, 0.0).astype(BF16)
    run0 = exact_dot(tri, logs[0:Q])
    run1 = exact_dot(tri, logs[Q:])
    tot0, tot1 = run0[Q - 1 : Q], run1[Q - 1 : Q]
    run = jnp.concatenate([run0, run1], axis=0)
    to_end = jnp.concatenate([jnp.exp(tot0 - run0), jnp.exp(tot1 - run1)], axis=0)
    hi, lo = halves(step * to_end)
    fe_ref[0] = jnp.concatenate([hi, lo], axis=1)
    hi, lo = halves(jnp.exp(run))
    fe_ref[1] = jnp.concatenate([hi, lo], axis=1)
    st_ref[...] = jnp.concatenate([step, raw], axis=1)
    small = jnp.concatenate(
        [jnp.exp(tot0), jnp.exp(tot1), jnp.exp(tot0 + tot1), par[2:3], jnp.zeros((4, heads), F32)],
        axis=0,
    )
    hi, lo = halves(small)
    rows_ref[...] = dot(jnp.concatenate([hi, lo], axis=1), exp2[...])
    r2 = run * LOG2E
    q2 = (run - jnp.log(step)) * LOG2E
    xs2[...] = jnp.transpose(jnp.concatenate([r2, q2], axis=1))
    for j in range(heads // 4):
        cols_ref[j] = jnp.concatenate([r2[:, 4 * j : 4 * j + 4], q2[:, 4 * j : 4 * j + 4]], axis=1)
        rowt_ref[j] = jnp.concatenate(
            [xs2[4 * j : 4 * j + 4], xs2[heads + 4 * j : heads + 4 * j + 4]], axis=0
        )


def state_kernel(
    yv, x_own, dy_own, rec, halo, w, bias, bt, ct, fe, exp2, rows,
    t_ref, u_ref, xc_ref, dyo_ref, sl_ref, xs,
):
    y = yv[0]
    xs[0:8] = halo[...]
    in_order(y, x_own[...], rec[0], xs, 8)
    in_order(y, dy_own[...], rec[1], dyo_ref)
    v, slope = gates(conv_sum(xs, w, bias, 2 * Q))
    xc = v.astype(BF16)
    xc_ref[...] = xc
    sl_ref[...] = slope.astype(BF16)
    top, end = slice(0, Q), slice(Q, 2 * Q)
    d0, d1 = rows[0:1], rows[1:2]
    wf = xc.astype(F32) * dot(fe[0], exp2[...])
    df = dyo_ref[...].astype(F32) * dot(fe[1], exp2[...])
    wt = jnp.concatenate([(wf[top] * d1).astype(BF16), wf[end].astype(BF16)], axis=0)
    dyr = jnp.concatenate([df[top].astype(BF16), (df[end] * d0).astype(BF16)], axis=0)
    t_ref[0] = dot(bt[...], wt).astype(BF16)
    u_ref[0] = dot(ct[...], dyr).astype(BF16)


def setup_whole(yv, b, c, dt, rec, rim, rim_e, rim_o, w, bias, par, *rest):
    width = rec.shape[1] // 2 - dt.shape[1] // 2
    first = w.shape[1] - 4 * width
    own = pl.ds(pl.multiple_of(yv[0] * width, width), width)

    def at(i):
        return pl.ds(pl.multiple_of(first + 2 * i * width + yv[0] * width, width), width)

    setup_kernel(
        yv, b.at[:, own], c.at[:, own], dt, rec, rim, rim_e, rim_o, w.at[:, at(0)], w.at[:, at(1)],
        bias.at[:, at(0)], bias.at[:, at(1)], par, *rest,
    )


def over_subs(width, body, roll):
    if not roll:
        for j in range(width // SUB):
            body(j, j * SUB)
        return

    def step(j, _):
        body(j, pl.multiple_of(j * SUB, SUB))
        return 0

    lax.fori_loop(0, width // SUB, step, 0)


def state_chunk(
    yv, x, dy, rec, halo, w, bias, bt, ct, fe, exp2, rows, t_all, u_all, xc, dyo, sl, xs, tu, sems,
    *, chunk, per_group,
):
    chunks, _, cw = t_all.shape
    g = chunk // per_group * N

    def body(j, lo):
        at = pl.ds(lo, SUB)
        own = pl.ds(pl.multiple_of((yv[0] * chunks + chunk) * cw + lo, SUB), SUB)
        band = pl.ds(pl.multiple_of(chunk * cw + lo, SUB), SUB)
        state_kernel(
            yv, x.at[:, own], dy.at[:, own], rec.at[:, :, at], halo.at[:, band], w.at[:, own],
            bias.at[:, own], bt.at[g : g + N], ct.at[g : g + N], fe, exp2.at[:, band],
            rows.at[:, band], tu.at[0:1, :, at], tu.at[1:2, :, at],
            xc.at[:, at], dyo.at[:, at], sl.at[:, at], xs,
        )

    over_subs(cw, body, False)
    copies([(tu.at[0], t_all.at[chunk]), (tu.at[1], u_all.at[chunk])], sems)


def hop_kernel(yv, in_e, in_o, t, u, rows, out_e, out_o, *, step, part):
    chunks, height, whole_width = t.shape
    width = out_e.shape[1]
    cf = jnp.clip(step - yv[1], 0, chunks - 1)
    cb = jnp.clip(step - yv[4], 0, chunks - 1)
    lanes = slice(part * width, (part + 1) * width)

    def decay(c, spot):
        at = pl.ds(pl.multiple_of(c * whole_width + part * width, width), width)
        return rows[2:3, at] * jnp.where(spot == 0, 0.0, 1.0)

    row_f = decay(cf, yv[1])
    row_b = decay(cb, yv[4])

    def move(src, row, add, c, dst):
        for r in range(0, height, 32):
            at = slice(r, r + 32)
            more = add[c, at, lanes]
            dst[at] = (row * src[at].astype(F32) + more.astype(F32)).astype(BF16)

    @pl.when(yv[2] == 0)
    def _():
        move(in_o, row_f, t, cf, out_e)
        move(in_e, row_b, u, cb, out_o)

    @pl.when(yv[2] != 0)
    def _():
        move(in_e, row_f, t, cf, out_o)
        move(in_o, row_b, u, cb, out_e)


def within_chunk(yv, xc, dyo, cols, rowt, bc, cc, yi, dxi, dcb_ref, cb, *, chunk, per_group):
    cw = xc.shape[1]
    g = slice(chunk // per_group * N, chunk // per_group * N + N)
    dcb_ref[...] = jnp.zeros(dcb_ref.shape, F32)
    for b in range(2):
        at = slice(b * Q, b * Q + Q)
        cb[b] = dot_tb(cc[at, g], bc[at, g])
        cb[2 + b] = dot_tb(bc[at, g], cc[at, g])

    def body(j, lo):
        at = pl.ds(lo, SUB)
        item = pl.ds(chunk * (cw // SUB) + j, 1)
        within_kernel(
            yv, xc.at[:, at], dyo.at[:, at], cols.at[item], rowt.at[item], yi.at[:, at],
            dxi.at[:, at], dcb_ref, cb,
        )

    over_subs(cw, body, False)


def within_kernel(yv, xc, dyo, cols, rowt, yi_ref, dxi_ref, dcb_ref, cb):
    low = triangle(True)
    high = triangle(False)
    lane = lax.broadcasted_iota(jnp.int32, (1, 2 * HEAD), 1)
    first = jnp.where(lane < HEAD, 1.0, 0.0).astype(BF16)
    second = jnp.where(lane < HEAD, 0.0, 1.0).astype(BF16)
    for b in range(2):
        at = slice(b * Q, b * Q + Q)
        dcb = dcb_ref[b]
        for p in range(2):
            ls = slice(p * 2 * HEAD, (p + 1) * 2 * HEAD)
            xp = xc[at, ls]
            dyp = dyo[at, ls]
            xbd = jnp.concatenate([xp * first, xp * second], axis=0)
            dbd = jnp.concatenate([dyp * first, dyp * second], axis=0)
            decay, mix, mixt = [], [], []
            for i in range(2):
                h = 2 * p + i
                ex = cols[0, at, h : h + 1] - rowt[0, 4 + h : 5 + h, at]
                lt = jnp.exp2(jnp.where(low, ex, NEG))
                ext = rowt[0, h : h + 1, at] - cols[0, at, 4 + h : 5 + h]
                ltt = jnp.exp2(jnp.where(high, ext, NEG))
                decay.append(lt)
                mix.append((cb[b] * lt).astype(BF16))
                mixt.append((cb[2 + b] * ltt).astype(BF16))
            yi_ref[at, ls] = dot(jnp.concatenate(mix, axis=1), xbd)
            dxi_ref[at, ls] = dot(jnp.concatenate(mixt, axis=1), dbd)
            dm = dot_tb(dyp, xbd)
            dcb = dcb + dm[:, 0:Q] * decay[0] + dm[:, Q:] * decay[1]
        dcb_ref[b] = dcb


def fetch(spot, choices, dst, sem):
    @pl.when(spot == 0)
    def _():
        dst[...] = jnp.zeros(dst.shape, dst.dtype)

    for k, src in enumerate(choices, 1):

        @pl.when(spot == k)
        def _():
            pltpu.make_async_copy(src, dst, sem).start()


def arrive(spot, choices, dst, sem):
    @pl.when(spot != 0)
    def _():
        pltpu.make_async_copy(choices[0], dst, sem).wait()


def across_chunk(
    yv, x, rec, halo, w, xc, dyo, sl, yi, dxi, bc, cc, fe, exp2, seg, rows, *rest,
    chunk, chunks, per_group,
):
    hops = (len(rest) - 18) // 2
    ents, leas = rest[:hops], rest[hops : 2 * hops]
    (y_ref, gx_ref, red, head, send, dc, db, wv, ends, cross) = rest[2 * hops : -8]
    xs, gs, gy, ent, lea, between, sems, more = rest[-8:]
    cw = xc.shape[1]
    parts = ents[0].shape[1]
    count = cw // parts
    jobs = []
    for i in range(count):
        at = slice(i * parts, (i + 1) * parts)
        jobs.append((yv[1], ents[i::count], ent.at[:, at], sems.at[2 * i]))
        jobs.append((yv[4], leas[i::count], lea.at[:, at], sems.at[2 * i + 1]))
    for job in jobs:
        fetch(*job)
    dc[...] = jnp.zeros(dc.shape, F32)
    db[...] = jnp.zeros(db.shape, F32)
    wv[...] = jnp.zeros(wv.shape, F32)
    cross[...] = jnp.zeros(cross.shape, F32)
    for job in jobs:
        arrive(*job)
    g = slice(chunk // per_group * N, chunk // per_group * N + N)
    between[0] = dot_tb(cc[Q : 2 * Q, g], bc[0:Q, g]).astype(BF16)
    between[1] = dot_tb(bc[0:Q, g], cc[Q : 2 * Q, g]).astype(BF16)

    def body(j, lo):
        at = pl.ds(lo, SUB)
        own = pl.ds(pl.multiple_of((yv[0] * chunks + chunk) * cw + lo, SUB), SUB)
        band = pl.ds(pl.multiple_of(chunk * cw + lo, SUB), SUB)
        across_kernel(
            yv, x.at[:, own], rec.at[:, :, at], halo.at[:, band], w.at[:, own], xc.at[:, at],
            dyo.at[:, at], sl.at[:, at], yi.at[:, at], dxi.at[:, at], bc.at[:, g], cc.at[:, g],
            fe, exp2.at[:, band], seg.at[band], rows.at[:, band],
            ent.at[:, at], lea.at[:, at], red.at[:, at], head.at[:, at], gy.at[:, :, at],
            dc, db, wv, ends.at[:, at], cross, between, xs, gs,
        )

    over_subs(cw, body, True)
    mine = pl.ds(pl.multiple_of(yv[0] * Q, Q), Q)
    other = pl.ds(pl.multiple_of((1 - yv[0]) * Q, Q), Q)
    place = pl.ds(pl.multiple_of((yv[0] * chunks + chunk) * cw, cw), cw)
    copies(
        [
            (gy.at[:, other], send), (gy.at[0, mine], y_ref.at[:, place]),
            (gy.at[1, mine], gx_ref.at[:, place]),
        ],
        more,
    )


def across_kernel(
    yv, x_own, rec, halo, w, xc, dyo, sl, yi, dxi, bc, cc, fe, exp2, seg, rows, ent, lea,
    red_ref, head_ref, gy, dc_ref, db_ref, wv_ref, ends_ref, cross_ref, between, xs, gs,
):
    y = yv[0]
    xs[0:8] = halo[...]
    in_order(y, x_own[...], rec[0], xs, 8)
    x = xc[...].astype(F32)
    dy = dyo[...].astype(F32)
    f = dot(fe[0], exp2[...])
    er = dot(fe[1], exp2[...])
    d0, d1, skip = rows[0:1], rows[1:2], rows[3:4]
    top, end = slice(0, Q), slice(Q, 2 * Q)
    wf = x * f
    df = dy * er
    w0 = wf[top].astype(BF16)
    dy1 = df[end].astype(BF16)
    wt = jnp.concatenate([(wf[top] * d1).astype(BF16), wf[end].astype(BF16)], axis=0)
    dyr = jnp.concatenate([df[top].astype(BF16), (df[end] * d0).astype(BF16)], axis=0)
    e0 = ent[...]
    r1 = lea[...]
    ce = dot(cc[...], e0)
    br = dot(bc[...], r1)
    ce1 = d0 * ce[end] + dot(between[0], w0)
    br0 = d1 * br[top] + dot(between[1], dy1)
    over = jnp.concatenate([ce[top], ce1], axis=0) * er
    back = jnp.concatenate([br0, br[end]], axis=0) * f
    dc_ref[...] += dot_tb(dyr, e0)
    db_ref[...] += dot_tb(wt, r1)
    cross_ref[...] += dot_tb(dy1, w0)
    flow = d0 * d1 * jnp.sum(r1.astype(F32) * e0.astype(F32), axis=0, keepdims=True)
    flow0 = flow + d0 * jnp.sum(df[end] * ce[end], axis=0, keepdims=True)
    flow1 = flow + d1 * jnp.sum(wf[top] * br[top], axis=0, keepdims=True)
    yn = yi[...] + over
    dxn = dxi[...] + back
    wv_ref[0] += dot((dy * yn).astype(BF16), seg[...])
    wv_ref[1] += dot((x * dxn).astype(BF16), seg[...])
    xb = x * back
    ends_ref[...] = jnp.concatenate(
        [
            jnp.sum(xb[top], axis=0, keepdims=True) + flow0,
            jnp.sum(xb[end], axis=0, keepdims=True) + flow1,
            jnp.sum(x * dy, axis=0, keepdims=True),
            jnp.zeros((5, SUB), F32),
        ],
        axis=0,
    )
    ds = (dxn + skip * dy) * sl[...].astype(F32)
    gx, dw = conv_back(ds, xs, gs, w, 2 * Q)
    red_ref[...] = dw
    head_ref[...] = ds[0:8]
    gy[0] = (yn + skip * x).astype(BF16)
    gy[1] = gx.astype(BF16)


def finish_group(
    yv, b_own, c_own, b_rec, c_rec, b_halo, c_halo, wb, wc, slope, bc, cc, parts,
    gb_ref, gc_ref, red_ref, head_ref, send_ref, xs, gs, gv,
):
    y = yv[0]
    dc, db, dcb, cross = [sum(r[...] for r in refs[1:]) + refs[0][...] for refs in zip(*parts)]
    dcb = dcb.astype(BF16)
    cross = cross.astype(BF16)
    for b in range(2):
        at = slice(b * Q, b * Q + Q)
        gv[0, at] = db[at] + dot_ta(dcb[b], cc[at])
        gv[1, at] = dc[at] + dot(dcb[b], bc[at])
    gv[0, 0:Q] += dot_ta(cross, cc[Q : 2 * Q])
    gv[1, Q : 2 * Q] += dot(cross, bc[0:Q])
    for i, (own, rec, halo, w, out) in enumerate(
        ((b_own, b_rec, b_halo, wb, gb_ref), (c_own, c_rec, c_halo, wc, gc_ref))
    ):
        cs = slice(i * N, (i + 1) * N)
        xs[0:8] = halo[...]
        in_order(y, own[...], rec[...], xs, 8)
        ds = gv[i] * slope[i]
        gx, dw = conv_back(ds, xs, gs, w, 2 * Q)
        red_ref[:, cs] = dw
        head_ref[:, cs] = ds[0:8]

        @pl.when(y == 0)
        def _():
            out[...] = gx[0:Q].astype(BF16)
            send_ref[:, cs] = gx[Q:].astype(BF16)

        @pl.when(y != 0)
        def _():
            out[...] = gx[Q:].astype(BF16)
            send_ref[:, cs] = gx[0:Q].astype(BF16)


def finish_views(yv, g, b, c, rec, halo, w, slopes, bc, cc, gb, gc, red, head):
    groups = bc.shape[1] // N
    half = halo.shape[1] - 2 * groups * N
    wide = 2 * half
    gs = slice(g * N, (g + 1) * N)
    own = pl.ds(pl.multiple_of((yv[0] * groups + g) * N, N), N)

    def weights(i):
        return pl.ds(pl.multiple_of(wide + (2 * i * groups + yv[0] * groups + g) * N, N), N)

    return (
        b.at[:, own], c.at[:, own], rec.at[:, gs], rec.at[:, (groups + g) * N : (groups + g + 1) * N],
        halo.at[:, half + g * N : half + (g + 1) * N],
        halo.at[:, half + (groups + g) * N : half + (groups + g + 1) * N],
        w.at[:, weights(0)], w.at[:, weights(1)], slopes.at[:, :, gs], bc.at[:, gs], cc.at[:, gs],
    ), (gb, gc, red, head)


def finish_kernel(
    yv, b, c, rec, halo, w, slopes, bc, cc, dc0, db0, dcb0, cross0, dc1, db1, dcb1, cross1,
    red, head, gb, gc, send_ref, xs, gs, gv,
):
    ins, outs = finish_views(yv, 0, b, c, rec, halo, w, slopes, bc, cc, gb, gc, red, head)
    finish_group(yv, *ins, [(dc0, db0, dcb0, cross0), (dc1, db1, dcb1, cross1)], *outs, send_ref, xs, gs, gv)
    for ref in outs[2:]:
        ref[:, 2 * N :] = jnp.zeros((8, ref.shape[1] - 2 * N), F32)


def finish_last_kernel(
    yv, b, c, rec, halo, w, slopes, bc, cc, dc0, db0, dcb0, cross0, dc1, db1, dcb1, cross1, st, par, seg, before, *rest,
):
    chunks = (len(rest) - 11) // 3
    wvs, ends, tops = [rest[i * chunks : (i + 1) * chunks] for i in range(3)]
    rest = rest[3 * chunks :]
    red, head, gb, gc, send_ref, gdt_ref, next_ref, xs, gs, gv, gd = rest
    y = yv[0]
    ins, outs = finish_views(yv, 1, b, c, rec, halo, w, slopes, bc, cc, gb, gc, red, head)
    finish_group(yv, *ins, [(dc0, db0, dcb0, cross0), (dc1, db1, dcb1, cross1)], *outs, send_ref, xs, gs, gv)
    red_ref, head_ref = red, head
    heads = par.shape[1]
    step, raw = st[:, 0:heads], st[:, heads:]
    rate = jnp.exp(par[0:1])
    cw = ends[0].shape[1]
    w_sum = sum(wv[0] for wv in wvs[1:]) + wvs[0][0]
    v_sum = sum(wv[1] for wv in wvs[1:]) + wvs[0][1]
    e_sum = split_dot(ends[0][...], seg[0:cw])
    for i in range(1, chunks):
        e_sum = e_sum + split_dot(ends[i][...], seg[i * cw : (i + 1) * cw])
    tri = jnp.where(triangle(False), 1.0, 0.0).astype(BF16)
    diff = w_sum - v_sum
    dl = jnp.concatenate(
        [exact_dot(tri, diff[0:Q]) + e_sum[0:1], exact_dot(tri, diff[Q:]) + e_sum[1:2]], axis=0
    )
    draw = (v_sum / step - rate * dl) / (1.0 + jnp.exp(-raw))
    red_ref[:, 2 * N :] = jnp.concatenate(
        [
            jnp.concatenate(
                [
                    jnp.sum(dl * (-rate * step), axis=0, keepdims=True),
                    jnp.sum(draw, axis=0, keepdims=True),
                    e_sum[2:3],
                    jnp.zeros((5, heads), F32),
                ],
                axis=0,
            ),
            jnp.zeros((8, red_ref.shape[1] - 2 * N - heads), F32),
        ],
        axis=1,
    )
    head_ref[:, 2 * N :] = jnp.zeros((8, head_ref.shape[1] - 2 * N), F32)
    items = []
    for r in range(3):
        row = slice(r, r + 1)
        items += [v[row] for v in tops]
        items.append(
            jnp.concatenate(
                [
                    before[row, 0:N], head_ref[row, 0:N],
                    before[row, N : 2 * N], head_ref[row, N : 2 * N],
                ],
                axis=1,
            )
        )
    items.append(jnp.zeros((16 - 3 * (chunks + 1), cw), F32))
    next_ref[...] = jnp.concatenate(items, axis=0)
    gd[...] = jnp.concatenate([draw, draw], axis=1).astype(BF16)

    @pl.when(y == 0)
    def _():
        gdt_ref[...] = gd[0:Q]
        send_ref[:, 2 * N :] = gd[Q:]

    @pl.when(y != 0)
    def _():
        gdt_ref[...] = gd[Q:]
        send_ref[:, 2 * N :] = gd[0:Q]


def add_kernel(yv, *refs):
    total = refs[0][...]
    for r in refs[1:-1]:
        total = total + r[...]
    refs[-1][...] = total


def gather_kernel(yv, *refs, side, count):
    out = refs[-1]
    more = refs[2 * count : -1]

    def fill(k):
        at = 0
        for r in refs[k * count : (k + 1) * count]:
            width = r.shape[1]
            total = r[...]
            for m in more:
                total = total + m[:, at : at + width]
            out[:, at : at + width] = total
            at += width

    for core in range(2):

        @pl.when(yv[3] == core)
        def _():
            fill(1 - core if side else core)


def join_kernel(yv, first, second, out):
    out[0] = first[...]
    out[1] = second[...]


def spread(yv, own, got, dst):
    width = own[0].shape[1]
    for k in range(2):

        @pl.when(yv[0] == k)
        def _():
            for g in range(2):
                at = (k * 2 + g) * width
                dst[:, at : at + width] = own[g][...].astype(F32)
                at = ((1 - k) * 2 + g) * width
                dst[:, at : at + width] = got[g].astype(F32)


def rim_kernel(
    yv, next0, next_e, next_o, w, b0, b1, c0, c1, got0, got1, gdt_own, gx,
    gx_ref, gb_ref, gc_ref, gdt_ref, mark, both, full,
):
    mark[...] = jnp.zeros(mark.shape, F32)
    lane = lax.broadcasted_iota(jnp.int32, gdt_own.shape, 1)
    low = lane < gdt_own.shape[1] // 2
    own, got = gdt_own[...].astype(F32), got1[:, 2 * N :].astype(F32)

    @pl.when(yv[0] == 0)
    def _():
        gdt_ref[...] = jnp.where(low, own, got).astype(BF16)

    @pl.when(yv[0] != 0)
    def _():
        gdt_ref[...] = jnp.where(low, got, own).astype(BF16)

    spread(yv, (b0, b1), [r[:, 0:N] for r in (got0, got1)], full.at[0])
    spread(yv, (c0, c1), [r[:, N : 2 * N] for r in (got0, got1)], full.at[1])
    gb_ref[...] = full[0].astype(BF16)
    gc_ref[...] = full[1].astype(BF16)
    rows = slice(Q - 16, Q)
    both[0] = next0[...]

    @pl.when(yv[2] == 0)
    def _():
        both[1] = next_e[...]

    @pl.when(yv[2] != 0)
    def _():
        both[1] = next_o[...]

    step = next0.shape[1]
    blocks = gx.shape[1] // 2 // step
    keep = jnp.where((yv[0] == 0) | (yv[4] == 0), 0.0, 1.0)

    def add(src, dst, lo, half, block, at, width, to):
        h = [keep * both[half, r * (blocks + 1) + block : r * (blocks + 1) + block + 1, at : at + width] for r in range(3)]
        k = w[:, lo : lo + width]
        more = jnp.concatenate(
            [
                jnp.zeros((13, width), F32),
                k[0:1] * h[0],
                k[0:1] * h[1] + k[1:2] * h[0],
                k[0:1] * h[2] + k[1:2] * h[1] + k[2:3] * h[0],
            ],
            axis=0,
        )
        dst[:, to : to + width] = (src[:, to : to + width].astype(F32) + more).astype(BF16)

    for half in range(2):
        for i in range(blocks):
            at = (half * blocks + i) * step
            add(gx, gx_ref, at, half, i, 0, step, at)
        for i, (src, dst) in enumerate(((full.at[0, rows], gb_ref.at[rows]), (full.at[1, rows], gc_ref.at[rows]))):
            to = half * step // 2
            add(src, dst, (2 * blocks + i) * step + to, half, blocks, i * step // 2, step // 2, to)


def sums_kernel(yv, mine, theirs, gw_ref, gb_ref, gh_ref, both, *, wide, heads):
    width = mine.shape[2]

    @pl.when(yv[3] == 0)
    def _():
        both[:, :, 0:width] = mine[...]
        both[:, :, width:] = theirs[...]

    @pl.when(yv[3] != 0)
    def _():
        both[:, :, 0:width] = theirs[...]
        both[:, :, width:] = mine[...]

    step = width - wide // 2

    def fill(order):
        for k in range(2):
            v = both[order[k]]
            for i in range(2):
                to, at = k * wide + i * (wide // 2), i * width + step
                gw_ref[:, to : to + wide // 2] = v[0:4, at : at + wide // 2]
                gb_ref[:, to : to + wide // 2] = v[4:5, at : at + wide // 2]
            for i in range(2):
                for g in range(2):
                    to = 2 * wide + i * 4 * N + (2 * k + g) * N
                    gw_ref[:, to : to + N] = v[0:4, g * width + i * N : g * width + (i + 1) * N]
                    gb_ref[:, to : to + N] = v[4:5, g * width + i * N : g * width + (i + 1) * N]
        at = width + 2 * N
        values = jnp.concatenate(
            [both[order[0]][:, at : at + heads], both[order[1]][:, at : at + heads]], axis=1
        )
        per_dev = gh_ref.shape[1]
        row = lax.broadcasted_iota(jnp.int32, (2 * heads, per_dev), 0)
        col = lax.broadcasted_iota(jnp.int32, (2 * heads, per_dev), 1)
        pick = jnp.where(row == col + yv[5] * per_dev, 1.0, 0.0).astype(BF16)
        hi = values.astype(BF16)
        rest = values - hi.astype(F32)
        mid = rest.astype(BF16)
        low = (rest - mid.astype(F32)).astype(BF16)
        gh_ref[...] = (dot(hi, pick) + dot(mid, pick) + dot(low, pick))[0:3]

    @pl.when(yv[0] == 0)
    def _():
        fill((0, 1))

    @pl.when(yv[0] != 0)
    def _():
        fill((1, 0))


def whole(shape):
    return pl.BlockSpec(shape, lambda *_: (0,) * len(shape))


def shape_of(*dims, dtype=F32):
    return jax.ShapeDtypeStruct(dims, dtype)


def call(kernel, yv, ins, outs, scratch, micros, nbytes, keep=(), after=(), hbm=()):
    count = len(ins)
    extra = len(keep) + len(after)

    def run(yr, *refs):
        kernel(yr, *refs[:count], *refs[count + extra :])

    near = pl.BlockSpec(memory_space=pltpu.MemorySpace.VMEM)
    anywhere = pl.BlockSpec(memory_space=pl.ANY)
    ins = [i if isinstance(i, tuple) else (i, near) for i in ins]
    return pl.pallas_call(
        run,
        out_shape=outs,
        in_specs=[pl.BlockSpec(memory_space=pltpu.MemorySpace.SMEM)]
        + [i[1] for i in ins]
        + [anywhere if k in hbm else near for k in range(len(keep))]
        + [anywhere] * len(after),
        out_specs=[anywhere if k in hbm else near for k in range(len(outs))],
        scratch_shapes=scratch,
        compiler_params=params(),
        cost_estimate=cost(micros, nbytes),
        input_output_aliases={1 + count + k: k for k in range(len(keep))},
    )(yv, *[i[0] for i in ins], *keep, *after)


def per_device(
    ssm_input, b_input, c_input, dt_input, conv_weight, conv_bias, a_log, dt_bias, skip_gain, grad_out
):
    x_rows, b_rows, c_rows = ssm_input[0], b_input[0], c_input[0]
    dt_rows, dy_rows = dt_input[0], grad_out[0]
    devices = lax.axis_size("sp")
    dp_size = lax.axis_size("dp")
    spots = devices // 2
    me = lax.axis_index("sp")
    y = lax.rem(me, 2)
    z = me // 2
    core = lax.rem(lax.axis_index("dp"), 2)
    yv = jnp.stack([y, z, lax.rem(z, 2), core, spots - 1 - z, me]).astype(jnp.int32)
    xw = x_rows.shape[1] // 2
    bw = b_rows.shape[1] // 2
    hl = dt_rows.shape[1] // 2
    chunks = 4
    cw = xw // chunks
    subs = cw // SUB
    groups = bw // N
    per_group = chunks // groups
    two = 2 * Q
    piece = 2 * N + 2 * hl
    base = groups * piece
    bands = base // SUB
    bias = conv_bias[None]

    def pairs(fn, n=devices):
        return [(i, fn(i)) for i in range(n) if fn(i) is not None and 0 <= fn(i) < n]

    swap = pairs(lambda i: i ^ 1)

    def joint(v, fn):
        moves = []
        for d in range(dp_size):
            for i in range(devices):
                to = fn(i)
                if to is None or not 0 <= to < devices:
                    moves.append((d * devices + i, (d ^ 1) * devices + i))
                else:
                    moves.append((d * devices + i, d * devices + to))
        return lax.ppermute(v, ("dp", "sp"), moves)

    def slant(i):
        return i + 1 if i % 2 else i - 1

    def evens(i):
        return i ^ 2

    def odds(i):
        return ((i + 2) ^ 2) - 2 if 2 <= i < devices - 2 else None

    in_hbm = pl.BlockSpec(memory_space=pltpu.MemorySpace.HBM)
    anywhere = pl.BlockSpec(memory_space=pl.ANY)
    msg, rim_out = call(
        pack_small_kernel, yv, [(x_rows, in_hbm), b_rows, c_rows, dt_rows],
        [shape_of(Q, 2 * bw + 2 * hl, dtype=BF16), shape_of(32, 2 * bw, dtype=BF16)],
        [
            pltpu.VMEM((16, 2 * xw), BF16), pltpu.VMEM((16, 2 * bw), BF16),
            pltpu.VMEM((16, 2 * bw), BF16), pltpu.SemaphoreType.DMA((3,)), pltpu.SemaphoreType.DMA((3,)),
        ],
        1, 1 << 20, hbm=(0,),
    )
    rec_bc = lax.ppermute(msg, "sp", swap)
    (rim_out,) = call(
        gate_kernel, yv, [rim_out], [shape_of(32, 2 * bw, dtype=BF16)], [], 1, 1 << 10, after=[rec_bc]
    )
    rim = joint(rim_out, slant)
    rim_e = joint(rim_out, evens)
    rim_o = joint(rim_out, odds)
    rec = []

    def send_chunk(c, after):
        def kernel(*refs):
            pack_kernel(*refs, chunk=c, chunks=chunks)

        (out,) = call(
            kernel, yv, [x_rows, dy_rows], [shape_of(2, Q, cw, dtype=BF16)],
            [pltpu.SemaphoreType.DMA((2,))], 1, 1 << 20, after=after, hbm=(0,),
        )
        rec.append(lax.ppermute(out, "sp", swap))

    send_chunk(0, [msg])

    par = lax.dynamic_slice_in_dim(
        jnp.concatenate([jnp.stack([a_log, dt_bias, skip_gain]), jnp.zeros((5, 2 * hl), F32)], 0),
        y * hl, hl, 1,
    )
    nq = hl // 4
    exp2, seg, halo, bcc, ccc, bct, cct, slopes, fe, rows, qcols, rowt, st = call(
        setup_whole, yv,
        [b_rows, c_rows, dt_rows, rec_bc, rim, rim_e, rim_o, conv_weight, bias, par],
        [
            shape_of(2 * hl, xw, dtype=BF16), shape_of(xw, hl, dtype=BF16), shape_of(8, xw + 2 * bw), shape_of(two, bw, dtype=BF16), shape_of(two, bw, dtype=BF16),
            shape_of(bw, two, dtype=BF16), shape_of(bw, two, dtype=BF16), shape_of(2, two, bw),
            shape_of(2, two, 2 * hl, dtype=BF16), shape_of(8, xw), shape_of(nq, two, 8),
            shape_of(nq, 8, two), shape_of(two, 2 * hl),
        ],
        [
            pltpu.VMEM((two + 8, bw), F32), pltpu.VMEM((two, hl), F32),
            pltpu.VMEM((2 * hl, two), F32), pltpu.VMEM((16, rim.shape[1]), F32),
        ],
        4, 4 << 20,
    )
    send_chunk(1, [rec_bc])
    states = []
    xcs, dyos, sls = [], [], []
    long = pltpu.VMEM((two + 8, SUB), F32)

    def state(c, after):
        nonlocal states
        big = shape_of(chunks, N, cw, dtype=BF16)
        tall = shape_of(two, cw, dtype=BF16)

        def kernel(*refs):
            state_chunk(*refs, chunk=c, per_group=per_group)

        t, u, xc, dyo, sl = call(
            kernel, yv,
            [x_rows, dy_rows, rec[c], halo, conv_weight, bias, bct, cct, fe, exp2, rows],
            [big, big, tall, tall, tall],
            [long, pltpu.VMEM((2, N, cw), BF16), pltpu.SemaphoreType.DMA((2,))], 3, 4 << 20,
            keep=states, after=after, hbm=(0, 1),
        )
        states = [t, u]
        xcs.append(xc)
        dyos.append(dyo)
        sls.append(sl)
        return xc

    yis, dxis, dcbs = [], [], []

    def within(c, after):
        def kernel(*refs):
            within_chunk(*refs, chunk=c, per_group=per_group)

        yi, dxi, dcb = call(
            kernel, yv, [xcs[c], dyos[c], qcols, rowt, bcc, ccc],
            [shape_of(two, cw), shape_of(two, cw), shape_of(2, Q, Q)],
            [pltpu.VMEM((4, Q, Q), F32)], 3, 4 << 20, after=after,
        )
        yis.append(yi)
        dxis.append(dxi)
        dcbs.append(dcb)
        return dcb

    finals = []
    sums = []
    reds, edges = [], []
    got_x = []

    def across(c, ents, leas, after):
        nonlocal finals
        full = shape_of(Q, 2 * xw, dtype=BF16)
        strip = shape_of(8, cw)

        def kernel(*refs):
            across_chunk(*refs, chunk=c, chunks=chunks, per_group=per_group)

        out = call(
            kernel, yv,
            [
                x_rows, rec[c], halo, conv_weight, xcs[c], dyos[c], sls[c], yis[c], dxis[c],
                bcc, ccc, fe, exp2, seg, rows,
            ] + [(v, anywhere) for v in ents + leas],
            [
                full, full, strip, strip, shape_of(2, Q, cw, dtype=BF16), shape_of(two, N),
                shape_of(two, N), shape_of(2, two, hl), shape_of(8, cw), shape_of(Q, Q),
            ],
            [
                long, long, pltpu.VMEM((2, two, cw), BF16), pltpu.VMEM((N, cw), BF16),
                pltpu.VMEM((N, cw), BF16), pltpu.VMEM((2, Q, Q), BF16), pltpu.SemaphoreType.DMA((2 * halves_,)), pltpu.SemaphoreType.DMA((3,)),
            ],
            6, 6 << 20, keep=finals, after=after, hbm=(0, 1),
        )
        finals = list(out[:2])
        reds.append(out[2])
        edges.append(out[3])
        sums.append(out[5:])
        got_x.append(lax.ppermute(out[4], "sp", swap))
        return out[8]

    def unpack(c, after):
        full = shape_of(Q, 2 * xw, dtype=BF16)

        def kernel(*refs):
            unpack_kernel(*refs, chunk=c, chunks=chunks)

        *finals[:2], mark = call(
            kernel, yv, [(got_x[c], anywhere)], [full, full, shape_of(8, 128)],
            [pltpu.SemaphoreType.DMA((2,))], 1, 1 << 20, keep=finals[:2], after=after, hbm=(0, 1),
        )
        return mark

    grads_bc = []
    group_reds, group_edges = [], []

    def finish(g, last, after):
        own = shape_of(Q, N, dtype=BF16)
        strip = shape_of(8, piece)
        ins = [b_rows, c_rows, rec_bc, halo, conv_weight, slopes, bcc, ccc]
        for c in range(g * per_group, (g + 1) * per_group):
            ins += [sums[c][0], sums[c][1], dcbs[c], sums[c][4]]
        outs = [strip, strip, own, own, shape_of(Q, piece if last else 2 * N, dtype=BF16)]
        narrow = pltpu.VMEM((two + 8, N), F32)
        scratch = [narrow, narrow, pltpu.VMEM((2, two, N), F32)]
        if last:
            ins += [st, par, seg, group_edges[0]] + [v[2] for v in sums] + [v[3] for v in sums] + edges
            outs += [shape_of(Q, 2 * hl, dtype=BF16), shape_of(16, cw)]
            scratch.append(pltpu.VMEM((two, 2 * hl), BF16))
        out = call(
            finish_last_kernel if last else finish_kernel, yv, ins, outs, scratch, 3, 4 << 20, after=after
        )
        group_reds.append(out[0])
        group_edges.append(out[1])
        grads_bc.append(out[2:4])
        return lax.ppermute(out[4], "sp", swap), out[4:]

    halves_ = 2
    part = cw // halves_
    zero = jnp.zeros((N, part), BF16)
    ins_e = [[zero] for _ in range(halves_)]
    ins_o = [[zero] for _ in range(halves_)]
    steps = chunks + spots - 2
    state(0, [])
    got_bc = []
    waits = []
    for t in range(steps + 1):
        for i in range(halves_):
            token = []
            if t < steps:
                moving = shape_of(N, part, dtype=BF16)

                def kernel(*refs, step=t, lane=i):
                    hop_kernel(*refs, step=step, part=lane)

                out_e, out_o = call(
                    kernel, yv, [ins_e[i][-1], ins_o[i][-1], states[0], states[1], rows],
                    [moving, moving], [], 1, 3 << 20, after=waits,
                )
                token = [out_e]
                ins_e[i].append(joint(out_e, evens))
                ins_o[i].append(joint(out_o, odds))
            if t == 0 and i == 0:
                send_chunk(2, token)
            waits = []
            if i == 0 and t < chunks - 1:
                waits.append(within(t, token))
            if i == 1 and t + 1 < chunks:
                waits.append(state(t + 1, token))
                if t + 3 < chunks:
                    send_chunk(t + 3, [rec[t + 1]])
            c = t + 1 - spots
            if i == 0 and 0 <= c < chunks:
                if c == chunks - 1:
                    token = []
                ents, leas = [], []
                for k in range(1, spots):
                    for h in range(halves_):
                        ents.append((ins_o if k % 2 == 0 else ins_e)[h][c + k])
                        leas.append((ins_o if (spots - 1 - k) % 2 else ins_e)[h][c + k])
                waits.append(across(c, ents, leas, token))
            if i == 1 and c == 0:
                waits.append(within(chunks - 1, token))
            if i == 1 and c == chunks - 2:
                mark = unpack(0, token)
                got, tok = finish(0, False, token)
                got_bc.append(got)
                waits += [tok[0], mark]
    got, (_, gdt_own, next_rows) = finish(1, True, [])
    got_bc.append(got)

    hw = (base + xw) // 2
    slab = shape_of(8, hw)

    def add(items, after=()):
        (out,) = call(add_kernel, yv, items, [slab], [], 1, 1 << 20, after=after)
        return out

    per_side = chunks // 2
    pieces = []
    for k in range(2):
        pieces += [group_reds[k]] + reds[k * per_side : (k + 1) * per_side]

    def gather(side, more):
        def kernel(*refs):
            gather_kernel(*refs, side=side, count=1 + per_side)

        (out,) = call(kernel, yv, pieces + more, [slab], [], 1, 1 << 20)
        return out

    theirs = gather(True, [])
    mine = gather(False, [lax.ppermute(theirs, "dp", pairs(lambda i: i ^ 1, dp_size))])
    size = 2
    while size < dp_size:
        got = lax.ppermute(mine, "dp", pairs(lambda i: i ^ size, dp_size))
        marks = []
        if size == 2:
            marks = [unpack(1, [mine]), unpack(2, [mine])]
        mine = add([mine, got], marks)
        size *= 2
    size = 2
    while size < devices:
        ways = 4 if size * 4 <= devices else 2
        got = [lax.ppermute(mine, "sp", pairs(lambda i: i ^ (size * k))) for k in range(1, ways)]
        size *= ways
        mine = add([mine] + got)
    unpack(3, [mine])
    y_all, gx_all = finals[:2]
    next0 = joint(next_rows, slant)
    next_e = joint(next_rows, evens)
    next_o = joint(next_rows, odds)
    last = pl.BlockSpec((16, 2 * xw), lambda j, yr: (Q // 16 - 1, 0))
    small = [next0, next_e, next_o, conv_weight] + [grads_bc[g][i] for i in range(2) for g in range(2)]
    small += [got_bc[0], got_bc[1], gdt_own]
    full = shape_of(Q, 2 * bw, dtype=BF16)
    grad_x, grad_b, grad_c, gdt, rim_mark = pl.pallas_call(
        rim_kernel,
        out_shape=[shape_of(Q, 2 * xw, dtype=BF16), full, full, shape_of(Q, 2 * hl, dtype=BF16), shape_of(8, 128)],
        grid_spec=pltpu.PrefetchScalarGridSpec(
            num_scalar_prefetch=1,
            grid=(1,),
            in_specs=[whole(v.shape) for v in small] + [last],
            out_specs=[last, whole(full.shape), whole(full.shape), whole((Q, 2 * hl)), whole((8, 128))],
            scratch_shapes=[pltpu.VMEM((2, 16, cw), F32), pltpu.VMEM((2, Q, 2 * bw), F32)],
        ),
        compiler_params=params(),
        cost_estimate=cost(1, 1 << 20),
        input_output_aliases={1 + len(small): 0},
    )(yv, *small, gx_all)

    got_y = lax.ppermute(mine, "sp", swap)

    (mine,) = call(
        join_kernel, yv, [mine, got_y], [shape_of(2, 8, hw)], [], 1, 1 << 20, after=[rim_mark]
    )
    theirs = lax.ppermute(mine, "dp", pairs(lambda i: i ^ 1, dp_size))
    per_dev = 2 * hl // devices

    def summed(*refs):
        sums_kernel(*refs, wide=xw, heads=hl)

    gw, gbias, gheads = pl.pallas_call(
        lambda yr, a, b, unused, *refs: summed(yr, a, b, *refs),
        out_shape=[
            shape_of(4, bias.shape[1]), shape_of(1, bias.shape[1]), shape_of(3, per_dev),
        ],
        grid_spec=pltpu.PrefetchScalarGridSpec(
            num_scalar_prefetch=1,
            grid=(1,),
            in_specs=[whole(mine.shape), whole(theirs.shape), anywhere],
            out_specs=[
                whole((4, bias.shape[1])), whole((1, bias.shape[1])), whole((3, per_dev)),
            ],
            scratch_shapes=[pltpu.VMEM((2, 8, base + xw), F32)],
        ),
        compiler_params=params(),
        cost_estimate=cost(1, 1 << 20),
    )(yv, mine, theirs, rim_mark)
    return (
        y_all[None], grad_x[None], grad_b[None], grad_c[None], gdt[None], gw, gbias[0], gheads,
    )


def solution(mesh):
    rows = P("dp", "sp", None)
    in_specs = (rows, rows, rows, rows, P(), P(), P(), P(), P(), rows)
    out_specs = (rows, rows, rows, rows, rows, P(), P(), P(None, "sp"))
    return jax.shard_map(
        per_device, mesh=mesh, in_specs=in_specs, out_specs=out_specs, check_vma=False
    )
```

```python
import jax
import jax.numpy as jnp
from jax import lax
from jax.experimental import pallas as pl
from jax.experimental.pallas import tpu as pltpu
from jax.sharding import PartitionSpec as P

N = 256
Q = 128
HEAD = 64
SUB = 256
LOG2E = 1.4426950408889634
F32 = jnp.float32
BF16 = jnp.bfloat16
NEG = -1e30


def params():
    return pltpu.CompilerParams(vmem_limit_bytes=14 * 1024 * 1024)


def cost(micros, nbytes):
    return pl.CostEstimate(flops=int(micros * 1e9), bytes_accessed=nbytes, transcendentals=0)


def dot(a, b):
    return jnp.dot(a, b, preferred_element_type=F32)


def dot_tb(a, b):
    return lax.dot_general(a, b, (((1,), (1,)), ((), ())), preferred_element_type=F32)


def dot_ta(a, b):
    return lax.dot_general(a, b, (((0,), (0,)), ((), ())), preferred_element_type=F32)


def halves(v):
    hi = v.astype(BF16)
    return hi, (v - hi.astype(F32)).astype(BF16)


def split_dot(v, m):
    hi, lo = halves(v)
    return dot(hi, m) + dot(lo, m)


def exact_dot(m, v):
    hi = v.astype(BF16)
    rest = v - hi.astype(F32)
    mid = rest.astype(BF16)
    low = (rest - mid.astype(F32)).astype(BF16)
    return dot(m, hi) + dot(m, mid) + dot(m, low)


def triangle(lower):
    row = lax.broadcasted_iota(jnp.int32, (Q, Q), 0)
    col = lax.broadcasted_iota(jnp.int32, (Q, Q), 1)
    return row >= col if lower else row <= col


def in_order(y, own, rec, dst, first=0):
    rows = own.shape[0]

    @pl.when(y == 0)
    def _():
        dst[first : first + rows] = own.astype(dst.dtype)
        dst[first + rows : first + 2 * rows] = rec.astype(dst.dtype)

    @pl.when(y != 0)
    def _():
        dst[first : first + rows] = rec.astype(dst.dtype)
        dst[first + rows : first + 2 * rows] = own.astype(dst.dtype)


def conv_sum(xs, w, bias, rows):
    total = bias[...]
    for k in range(4):
        total = total + w[k : k + 1] * xs[5 + k : 5 + k + rows]
    return total


def gates(s):
    sig = 0.5 + 0.5 * jnp.tanh(0.5 * s)
    out = s * sig
    return out, sig + out * (1.0 - sig)


def conv_back(ds, xs, gs, w, rows):
    gs[0:rows] = ds
    gs[rows : rows + 8] = jnp.zeros((8, ds.shape[1]), F32)
    dx = w[3:4] * ds
    for k in range(3):
        dx = dx + w[k : k + 1] * gs[3 - k : 3 - k + rows]
    dw = [jnp.sum(ds * xs[5 + k : 5 + k + rows], axis=0, keepdims=True) for k in range(4)]
    dw.append(jnp.sum(ds, axis=0, keepdims=True))
    dw.append(jnp.zeros((3, ds.shape[1]), F32))
    return dx, jnp.concatenate(dw, axis=0)


def copies(pairs, sems):
    moves = [pltpu.make_async_copy(src, dst, sems.at[i]) for i, (src, dst) in enumerate(pairs)]
    for m in moves:
        m.start()
    for m in moves:
        m.wait()


def pack_rim_kernel(yv, x, b, c, out, xt, bt, ct, sems):
    half = x.shape[1] // 2
    width = b.shape[1] // 2
    step = 2 * width
    copies([(src.at[pl.ds(Q - 16, 16)], dst) for src, dst in ((x, xt), (b, bt), (c, ct))], sems)
    x3, b3, c3 = [r[...].astype(F32)[13:16] for r in (xt, bt, ct)]
    blocks = half // step + 1
    for k in range(2):
        items = []
        for r in range(3):
            for i in range(blocks - 1):
                at = k * half + i * step
                items.append(x3[r : r + 1, at : at + step])
            mine = slice(k * width, (k + 1) * width)
            items.append(jnp.concatenate([b3[r : r + 1, mine], c3[r : r + 1, mine]], axis=1))
        items.append(jnp.zeros((16 - 3 * blocks, step), F32))
        out[16 * k : 16 * (k + 1)] = jnp.concatenate(items, axis=0).astype(BF16)


def pack_small_kernel(yv, x, b, c, dt, out, rim, xt, bt, ct, sems, rim_sems):
    width = b.shape[1] // 2
    at = pl.multiple_of((1 - yv[0]) * width, 128)
    moves = [
        pltpu.make_async_copy(src, dst, sems.at[i])
        for i, (src, dst) in enumerate(
            (
                (b.at[:, pl.ds(at, width)], out.at[:, pl.ds(0, width)]),
                (c.at[:, pl.ds(at, width)], out.at[:, pl.ds(width, width)]),
                (dt, out.at[:, pl.ds(2 * width, dt.shape[1])]),
            )
        )
    ]
    for m in moves:
        m.start()
    pack_rim_kernel(yv, x, b, c, rim, xt, bt, ct, rim_sems)
    for m in moves:
        m.wait()


def gate_kernel(yv, src, dst):
    dst[...] = src[...]


def pack_kernel(yv, x, dy, out, sems, *, chunk, chunks):
    width = out.shape[2]
    at = pl.multiple_of(((1 - yv[0]) * chunks + chunk) * width, 128)
    copies([(x.at[:, pl.ds(at, width)], out.at[0]), (dy.at[:, pl.ds(at, width)], out.at[1])], sems)


def unpack_kernel(yv, got, y_ref, gx_ref, mark, sems, *, chunk, chunks):
    width = got.shape[2]
    at = pl.multiple_of(((1 - yv[0]) * chunks + chunk) * width, 128)
    copies([(got.at[0], y_ref.at[:, pl.ds(at, width)]), (got.at[1], gx_ref.at[:, pl.ds(at, width)])], sems)
    mark[...] = jnp.zeros(mark.shape, F32)


def setup_kernel(
    yv, b_own, c_own, dt_own, rec, rim, rim_e, rim_o, wb, wc, bb, bc_, par, exp2, seg_ref,
    halo_ref, bc_ref, cc_ref, bt_ref, ct_ref, ds_ref, fe_ref, rows_ref, cols_ref, rowt_ref, st_ref,
    xs, dts, xs2, rims,
):
    y = yv[0]
    width = b_own.shape[1]
    heads = par.shape[1]
    row = lax.broadcasted_iota(jnp.int32, exp2.shape, 0)
    lane = lax.broadcasted_iota(jnp.int32, exp2.shape, 1)
    exp2[...] = jnp.where(lane // HEAD == lax.rem(row, heads), 1.0, 0.0).astype(BF16)
    row = lax.broadcasted_iota(jnp.int32, seg_ref.shape, 0)
    lane = lax.broadcasted_iota(jnp.int32, seg_ref.shape, 1)
    seg_ref[...] = jnp.where(row // HEAD == lane, 1.0, 0.0).astype(BF16)
    half = halo_ref.shape[1] - 2 * width

    @pl.when(y == 0)
    def _():
        rims[...] = rim[0:16].astype(F32)

    @pl.when((y != 0) & (yv[2] == 0))
    def _():
        rims[...] = rim_o[16:32].astype(F32)

    @pl.when((y != 0) & (yv[2] != 0))
    def _():
        rims[...] = rim_e[16:32].astype(F32)

    blocks = halo_ref.shape[1] // rim.shape[1]
    keep = jnp.where(yv[1] == 0, 0.0, 1.0)
    halo_ref[...] = keep * jnp.concatenate(
        [jnp.zeros((5, halo_ref.shape[1]), F32)]
        + [
            jnp.concatenate([rims[r * blocks + i : r * blocks + i + 1] for i in range(blocks)], axis=1)
            for r in range(3)
        ],
        axis=0,
    )
    for i, (own, w, bias, out, out_t) in enumerate(
        ((b_own, wb, bb, bc_ref, bt_ref), (c_own, wc, bc_, cc_ref, ct_ref))
    ):
        at = i * width
        xs[0:8] = halo_ref[:, half + at : half + at + width]
        in_order(y, own[...], rec[0:Q, at : at + width], xs, 8)
        v, slope = gates(conv_sum(xs, w, bias, 2 * Q))
        out[...] = v.astype(BF16)
        out_t[...] = jnp.transpose(v).astype(BF16)
        ds_ref[i] = slope

    @pl.when(y == 0)
    def _():
        dts[0:Q] = dt_own[:, 0:heads].astype(F32)
        dts[Q : 2 * Q] = rec[0:Q, 2 * width : 2 * width + heads].astype(F32)

    @pl.when(y != 0)
    def _():
        dts[0:Q] = rec[0:Q, 2 * width + heads : 2 * width + 2 * heads].astype(F32)
        dts[Q : 2 * Q] = dt_own[:, heads : 2 * heads].astype(F32)

    raw = dts[...] + par[1:2]
    step = jnp.log1p(jnp.exp(raw))
    logs = -step * jnp.exp(par[0:1])
    tri = jnp.where(triangle(True), 1.0, 0.0).astype(BF16)
    run0 = exact_dot(tri, logs[0:Q])
    run1 = exact_dot(tri, logs[Q:])
    tot0, tot1 = run0[Q - 1 : Q], run1[Q - 1 : Q]
    run = jnp.concatenate([run0, run1], axis=0)
    to_end = jnp.concatenate([jnp.exp(tot0 - run0), jnp.exp(tot1 - run1)], axis=0)
    hi, lo = halves(step * to_end)
    fe_ref[0] = jnp.concatenate([hi, lo], axis=1)
    hi, lo = halves(jnp.exp(run))
    fe_ref[1] = jnp.concatenate([hi, lo], axis=1)
    st_ref[...] = jnp.concatenate([step, raw], axis=1)
    small = jnp.concatenate(
        [jnp.exp(tot0), jnp.exp(tot1), jnp.exp(tot0 + tot1), par[2:3], jnp.zeros((4, heads), F32)],
        axis=0,
    )
    hi, lo = halves(small)
    rows_ref[...] = dot(jnp.concatenate([hi, lo], axis=1), exp2[...])
    r2 = run * LOG2E
    q2 = (run - jnp.log(step)) * LOG2E
    xs2[...] = jnp.transpose(jnp.concatenate([r2, q2], axis=1))
    for j in range(heads // 4):
        cols_ref[j] = jnp.concatenate([r2[:, 4 * j : 4 * j + 4], q2[:, 4 * j : 4 * j + 4]], axis=1)
        rowt_ref[j] = jnp.concatenate(
            [xs2[4 * j : 4 * j + 4], xs2[heads + 4 * j : heads + 4 * j + 4]], axis=0
        )


def state_kernel(
    yv, x_own, dy_own, rec, halo, w, bias, bt, ct, fe, exp2, rows,
    t_ref, u_ref, xc_ref, dyo_ref, sl_ref, xs,
):
    y = yv[0]
    xs[0:8] = halo[...]
    in_order(y, x_own[...], rec[0], xs, 8)
    in_order(y, dy_own[...], rec[1], dyo_ref)
    v, slope = gates(conv_sum(xs, w, bias, 2 * Q))
    xc = v.astype(BF16)
    xc_ref[...] = xc
    sl_ref[...] = slope.astype(BF16)
    top, end = slice(0, Q), slice(Q, 2 * Q)
    d0, d1 = rows[0:1], rows[1:2]
    wf = xc.astype(F32) * dot(fe[0], exp2[...])
    df = dyo_ref[...].astype(F32) * dot(fe[1], exp2[...])
    wt = jnp.concatenate([(wf[top] * d1).astype(BF16), wf[end].astype(BF16)], axis=0)
    dyr = jnp.concatenate([df[top].astype(BF16), (df[end] * d0).astype(BF16)], axis=0)
    t_ref[0] = dot(bt[...], wt).astype(BF16)
    u_ref[0] = dot(ct[...], dyr).astype(BF16)


def setup_whole(yv, b, c, dt, rec, rim, rim_e, rim_o, w, bias, par, *rest):
    width = rec.shape[1] // 2 - dt.shape[1] // 2
    first = w.shape[1] - 4 * width
    own = pl.ds(pl.multiple_of(yv[0] * width, width), width)

    def at(i):
        return pl.ds(pl.multiple_of(first + 2 * i * width + yv[0] * width, width), width)

    setup_kernel(
        yv, b.at[:, own], c.at[:, own], dt, rec, rim, rim_e, rim_o, w.at[:, at(0)], w.at[:, at(1)],
        bias.at[:, at(0)], bias.at[:, at(1)], par, *rest,
    )


def over_subs(width, body, roll):
    if not roll:
        for j in range(width // SUB):
            body(j, j * SUB)
        return

    def step(j, _):
        body(j, pl.multiple_of(j * SUB, SUB))
        return 0

    lax.fori_loop(0, width // SUB, step, 0)


def state_chunk(
    yv, x, dy, rec, halo, w, bias, bt, ct, fe, exp2, rows, t_all, u_all, xc, dyo, sl, xs, tu, sems,
    *, chunk, per_group,
):
    chunks, _, cw = t_all.shape
    g = chunk // per_group * N

    def body(j, lo):
        at = pl.ds(lo, SUB)
        own = pl.ds(pl.multiple_of((yv[0] * chunks + chunk) * cw + lo, SUB), SUB)
        band = pl.ds(pl.multiple_of(chunk * cw + lo, SUB), SUB)
        state_kernel(
            yv, x.at[:, own], dy.at[:, own], rec.at[:, :, at], halo.at[:, band], w.at[:, own],
            bias.at[:, own], bt.at[g : g + N], ct.at[g : g + N], fe, exp2.at[:, band],
            rows.at[:, band], tu.at[0:1, :, at], tu.at[1:2, :, at],
            xc.at[:, at], dyo.at[:, at], sl.at[:, at], xs,
        )

    over_subs(cw, body, True)
    copies([(tu.at[0], t_all.at[chunk]), (tu.at[1], u_all.at[chunk])], sems)


def hop_kernel(yv, in_e, in_o, t, u, rows, out_e, out_o, *, step, part):
    chunks, height, whole_width = t.shape
    width = out_e.shape[1]
    cf = jnp.clip(step - yv[1], 0, chunks - 1)
    cb = jnp.clip(step - yv[4], 0, chunks - 1)
    lanes = slice(part * width, (part + 1) * width)

    def decay(c, spot):
        at = pl.ds(pl.multiple_of(c * whole_width + part * width, width), width)
        return rows[2:3, at] * jnp.where(spot == 0, 0.0, 1.0)

    row_f = decay(cf, yv[1])
    row_b = decay(cb, yv[4])

    def move(src, row, add, c, dst):
        for r in range(0, height, 32):
            at = slice(r, r + 32)
            more = add[c, at, lanes]
            dst[at] = (row * src[at].astype(F32) + more.astype(F32)).astype(BF16)

    @pl.when(yv[2] == 0)
    def _():
        move(in_o, row_f, t, cf, out_e)
        move(in_e, row_b, u, cb, out_o)

    @pl.when(yv[2] != 0)
    def _():
        move(in_e, row_f, t, cf, out_o)
        move(in_o, row_b, u, cb, out_e)


def within_chunk(yv, xc, dyo, cols, rowt, bc, cc, yi, dxi, dcb_ref, cb, *, chunk, per_group):
    cw = xc.shape[1]
    g = slice(chunk // per_group * N, chunk // per_group * N + N)
    dcb_ref[...] = jnp.zeros(dcb_ref.shape, F32)
    for b in range(2):
        at = slice(b * Q, b * Q + Q)
        cb[b] = dot_tb(cc[at, g], bc[at, g])
        cb[2 + b] = dot_tb(bc[at, g], cc[at, g])

    def body(j, lo):
        at = pl.ds(lo, SUB)
        item = pl.ds(chunk * (cw // SUB) + j, 1)
        within_kernel(
            yv, xc.at[:, at], dyo.at[:, at], cols.at[item], rowt.at[item], yi.at[:, at],
            dxi.at[:, at], dcb_ref, cb,
        )

    over_subs(cw, body, False)


def within_kernel(yv, xc, dyo, cols, rowt, yi_ref, dxi_ref, dcb_ref, cb):
    low = triangle(True)
    high = triangle(False)
    lane = lax.broadcasted_iota(jnp.int32, (1, 2 * HEAD), 1)
    first = jnp.where(lane < HEAD, 1.0, 0.0).astype(BF16)
    second = jnp.where(lane < HEAD, 0.0, 1.0).astype(BF16)
    for b in range(2):
        at = slice(b * Q, b * Q + Q)
        dcb = dcb_ref[b]
        for p in range(2):
            ls = slice(p * 2 * HEAD, (p + 1) * 2 * HEAD)
            xp = xc[at, ls]
            dyp = dyo[at, ls]
            xbd = jnp.concatenate([xp * first, xp * second], axis=0)
            dbd = jnp.concatenate([dyp * first, dyp * second], axis=0)
            decay, mix, mixt = [], [], []
            for i in range(2):
                h = 2 * p + i
                ex = cols[0, at, h : h + 1] - rowt[0, 4 + h : 5 + h, at]
                lt = jnp.exp2(jnp.where(low, ex, NEG))
                ext = rowt[0, h : h + 1, at] - cols[0, at, 4 + h : 5 + h]
                ltt = jnp.exp2(jnp.where(high, ext, NEG))
                decay.append(lt)
                mix.append((cb[b] * lt).astype(BF16))
                mixt.append((cb[2 + b] * ltt).astype(BF16))
            yi_ref[at, ls] = dot(jnp.concatenate(mix, axis=1), xbd)
            dxi_ref[at, ls] = dot(jnp.concatenate(mixt, axis=1), dbd)
            dm = dot_tb(dyp, xbd)
            dcb = dcb + dm[:, 0:Q] * decay[0] + dm[:, Q:] * decay[1]
        dcb_ref[b] = dcb


def fetch(spot, choices, dst, sem):
    @pl.when(spot == 0)
    def _():
        dst[...] = jnp.zeros(dst.shape, dst.dtype)

    for k, src in enumerate(choices, 1):

        @pl.when(spot == k)
        def _():
            pltpu.make_async_copy(src, dst, sem).start()


def arrive(spot, choices, dst, sem):
    @pl.when(spot != 0)
    def _():
        pltpu.make_async_copy(choices[0], dst, sem).wait()


def across_chunk(
    yv, x, rec, halo, w, xc, dyo, sl, yi, dxi, bc, cc, fe, exp2, seg, rows, *rest,
    chunk, chunks, per_group,
):
    hops = (len(rest) - 18) // 2
    ents, leas = rest[:hops], rest[hops : 2 * hops]
    (y_ref, gx_ref, red, head, send, dc, db, wv, ends, cross) = rest[2 * hops : -8]
    xs, gs, gy, ent, lea, between, sems, more = rest[-8:]
    cw = xc.shape[1]
    parts = ents[0].shape[1]
    count = cw // parts
    jobs = []
    for i in range(count):
        at = slice(i * parts, (i + 1) * parts)
        jobs.append((yv[1], ents[i::count], ent.at[:, at], sems.at[2 * i]))
        jobs.append((yv[4], leas[i::count], lea.at[:, at], sems.at[2 * i + 1]))
    for job in jobs:
        fetch(*job)
    dc[...] = jnp.zeros(dc.shape, F32)
    db[...] = jnp.zeros(db.shape, F32)
    wv[...] = jnp.zeros(wv.shape, F32)
    cross[...] = jnp.zeros(cross.shape, F32)
    for job in jobs:
        arrive(*job)
    g = slice(chunk // per_group * N, chunk // per_group * N + N)
    between[0] = dot_tb(cc[Q : 2 * Q, g], bc[0:Q, g]).astype(BF16)
    between[1] = dot_tb(bc[0:Q, g], cc[Q : 2 * Q, g]).astype(BF16)

    def body(j, lo):
        at = pl.ds(lo, SUB)
        own = pl.ds(pl.multiple_of((yv[0] * chunks + chunk) * cw + lo, SUB), SUB)
        band = pl.ds(pl.multiple_of(chunk * cw + lo, SUB), SUB)
        across_kernel(
            yv, x.at[:, own], rec.at[:, :, at], halo.at[:, band], w.at[:, own], xc.at[:, at],
            dyo.at[:, at], sl.at[:, at], yi.at[:, at], dxi.at[:, at], bc.at[:, g], cc.at[:, g],
            fe, exp2.at[:, band], seg.at[band], rows.at[:, band],
            ent.at[:, at], lea.at[:, at], red.at[:, at], head.at[:, at], gy.at[:, :, at],
            dc, db, wv, ends.at[:, at], cross, between, xs, gs,
        )

    over_subs(cw, body, True)
    mine = pl.ds(pl.multiple_of(yv[0] * Q, Q), Q)
    other = pl.ds(pl.multiple_of((1 - yv[0]) * Q, Q), Q)
    place = pl.ds(pl.multiple_of((yv[0] * chunks + chunk) * cw, cw), cw)
    copies(
        [
            (gy.at[:, other], send), (gy.at[0, mine], y_ref.at[:, place]),
            (gy.at[1, mine], gx_ref.at[:, place]),
        ],
        more,
    )


def across_kernel(
    yv, x_own, rec, halo, w, xc, dyo, sl, yi, dxi, bc, cc, fe, exp2, seg, rows, ent, lea,
    red_ref, head_ref, gy, dc_ref, db_ref, wv_ref, ends_ref, cross_ref, between, xs, gs,
):
    y = yv[0]
    xs[0:8] = halo[...]
    in_order(y, x_own[...], rec[0], xs, 8)
    x = xc[...].astype(F32)
    dy = dyo[...].astype(F32)
    f = dot(fe[0], exp2[...])
    er = dot(fe[1], exp2[...])
    d0, d1, skip = rows[0:1], rows[1:2], rows[3:4]
    top, end = slice(0, Q), slice(Q, 2 * Q)
    wf = x * f
    df = dy * er
    w0 = wf[top].astype(BF16)
    dy1 = df[end].astype(BF16)
    wt = jnp.concatenate([(wf[top] * d1).astype(BF16), wf[end].astype(BF16)], axis=0)
    dyr = jnp.concatenate([df[top].astype(BF16), (df[end] * d0).astype(BF16)], axis=0)
    e0 = ent[...]
    r1 = lea[...]
    ce = dot(cc[...], e0)
    br = dot(bc[...], r1)
    ce1 = d0 * ce[end] + dot(between[0], w0)
    br0 = d1 * br[top] + dot(between[1], dy1)
    over = jnp.concatenate([ce[top], ce1], axis=0) * er
    back = jnp.concatenate([br0, br[end]], axis=0) * f
    dc_ref[...] += dot_tb(dyr, e0)
    db_ref[...] += dot_tb(wt, r1)
    cross_ref[...] += dot_tb(dy1, w0)
    flow = d0 * d1 * jnp.sum(r1.astype(F32) * e0.astype(F32), axis=0, keepdims=True)
    flow0 = flow + d0 * jnp.sum(df[end] * ce[end], axis=0, keepdims=True)
    flow1 = flow + d1 * jnp.sum(wf[top] * br[top], axis=0, keepdims=True)
    yn = yi[...] + over
    dxn = dxi[...] + back
    wv_ref[0] += dot((dy * yn).astype(BF16), seg[...])
    wv_ref[1] += dot((x * dxn).astype(BF16), seg[...])
    xb = x * back
    ends_ref[...] = jnp.concatenate(
        [
            jnp.sum(xb[top], axis=0, keepdims=True) + flow0,
            jnp.sum(xb[end], axis=0, keepdims=True) + flow1,
            jnp.sum(x * dy, axis=0, keepdims=True),
            jnp.zeros((5, SUB), F32),
        ],
        axis=0,
    )
    ds = (dxn + skip * dy) * sl[...].astype(F32)
    gx, dw = conv_back(ds, xs, gs, w, 2 * Q)
    red_ref[...] = dw
    head_ref[...] = ds[0:8]
    gy[0] = (yn + skip * x).astype(BF16)
    gy[1] = gx.astype(BF16)


def finish_group(
    yv, b_own, c_own, b_rec, c_rec, b_halo, c_halo, wb, wc, slope, bc, cc, parts,
    gb_ref, gc_ref, red_ref, head_ref, send_ref, xs, gs, gv,
):
    y = yv[0]
    dc, db, dcb, cross = [sum(r[...] for r in refs[1:]) + refs[0][...] for refs in zip(*parts)]
    dcb = dcb.astype(BF16)
    cross = cross.astype(BF16)
    for b in range(2):
        at = slice(b * Q, b * Q + Q)
        gv[0, at] = db[at] + dot_ta(dcb[b], cc[at])
        gv[1, at] = dc[at] + dot(dcb[b], bc[at])
    gv[0, 0:Q] += dot_ta(cross, cc[Q : 2 * Q])
    gv[1, Q : 2 * Q] += dot(cross, bc[0:Q])
    for i, (own, rec, halo, w, out) in enumerate(
        ((b_own, b_rec, b_halo, wb, gb_ref), (c_own, c_rec, c_halo, wc, gc_ref))
    ):
        cs = slice(i * N, (i + 1) * N)
        xs[0:8] = halo[...]
        in_order(y, own[...], rec[...], xs, 8)
        ds = gv[i] * slope[i]
        gx, dw = conv_back(ds, xs, gs, w, 2 * Q)
        red_ref[:, cs] = dw
        head_ref[:, cs] = ds[0:8]

        @pl.when(y == 0)
        def _():
            out[...] = gx[0:Q].astype(BF16)
            send_ref[:, cs] = gx[Q:].astype(BF16)

        @pl.when(y != 0)
        def _():
            out[...] = gx[Q:].astype(BF16)
            send_ref[:, cs] = gx[0:Q].astype(BF16)


def finish_views(yv, g, b, c, rec, halo, w, slopes, bc, cc, gb, gc, red, head):
    groups = bc.shape[1] // N
    half = halo.shape[1] - 2 * groups * N
    wide = 2 * half
    gs = slice(g * N, (g + 1) * N)
    own = pl.ds(pl.multiple_of((yv[0] * groups + g) * N, N), N)

    def weights(i):
        return pl.ds(pl.multiple_of(wide + (2 * i * groups + yv[0] * groups + g) * N, N), N)

    return (
        b.at[:, own], c.at[:, own], rec.at[:, gs], rec.at[:, (groups + g) * N : (groups + g + 1) * N],
        halo.at[:, half + g * N : half + (g + 1) * N],
        halo.at[:, half + (groups + g) * N : half + (groups + g + 1) * N],
        w.at[:, weights(0)], w.at[:, weights(1)], slopes.at[:, :, gs], bc.at[:, gs], cc.at[:, gs],
    ), (gb, gc, red, head)


def finish_kernel(
    yv, b, c, rec, halo, w, slopes, bc, cc, dc0, db0, dcb0, cross0, dc1, db1, dcb1, cross1,
    red, head, gb, gc, send_ref, xs, gs, gv,
):
    ins, outs = finish_views(yv, 0, b, c, rec, halo, w, slopes, bc, cc, gb, gc, red, head)
    finish_group(yv, *ins, [(dc0, db0, dcb0, cross0), (dc1, db1, dcb1, cross1)], *outs, send_ref, xs, gs, gv)
    for ref in outs[2:]:
        ref[:, 2 * N :] = jnp.zeros((8, ref.shape[1] - 2 * N), F32)


def finish_last_kernel(
    yv, b, c, rec, halo, w, slopes, bc, cc, dc0, db0, dcb0, cross0, dc1, db1, dcb1, cross1, st, par, seg, before, *rest,
):
    chunks = (len(rest) - 11) // 3
    wvs, ends, tops = [rest[i * chunks : (i + 1) * chunks] for i in range(3)]
    rest = rest[3 * chunks :]
    red, head, gb, gc, send_ref, gdt_ref, next_ref, xs, gs, gv, gd = rest
    y = yv[0]
    ins, outs = finish_views(yv, 1, b, c, rec, halo, w, slopes, bc, cc, gb, gc, red, head)
    finish_group(yv, *ins, [(dc0, db0, dcb0, cross0), (dc1, db1, dcb1, cross1)], *outs, send_ref, xs, gs, gv)
    red_ref, head_ref = red, head
    heads = par.shape[1]
    step, raw = st[:, 0:heads], st[:, heads:]
    rate = jnp.exp(par[0:1])
    cw = ends[0].shape[1]
    w_sum = sum(wv[0] for wv in wvs[1:]) + wvs[0][0]
    v_sum = sum(wv[1] for wv in wvs[1:]) + wvs[0][1]
    e_sum = split_dot(ends[0][...], seg[0:cw])
    for i in range(1, chunks):
        e_sum = e_sum + split_dot(ends[i][...], seg[i * cw : (i + 1) * cw])
    tri = jnp.where(triangle(False), 1.0, 0.0).astype(BF16)
    diff = w_sum - v_sum
    dl = jnp.concatenate(
        [exact_dot(tri, diff[0:Q]) + e_sum[0:1], exact_dot(tri, diff[Q:]) + e_sum[1:2]], axis=0
    )
    draw = (v_sum / step - rate * dl) / (1.0 + jnp.exp(-raw))
    red_ref[:, 2 * N :] = jnp.concatenate(
        [
            jnp.concatenate(
                [
                    jnp.sum(dl * (-rate * step), axis=0, keepdims=True),
                    jnp.sum(draw, axis=0, keepdims=True),
                    e_sum[2:3],
                    jnp.zeros((5, heads), F32),
                ],
                axis=0,
            ),
            jnp.zeros((8, red_ref.shape[1] - 2 * N - heads), F32),
        ],
        axis=1,
    )
    head_ref[:, 2 * N :] = jnp.zeros((8, head_ref.shape[1] - 2 * N), F32)
    items = []
    for r in range(3):
        row = slice(r, r + 1)
        items += [v[row] for v in tops]
        items.append(
            jnp.concatenate(
                [
                    before[row, 0:N], head_ref[row, 0:N],
                    before[row, N : 2 * N], head_ref[row, N : 2 * N],
                ],
                axis=1,
            )
        )
    items.append(jnp.zeros((16 - 3 * (chunks + 1), cw), F32))
    next_ref[...] = jnp.concatenate(items, axis=0)
    gd[...] = jnp.concatenate([draw, draw], axis=1).astype(BF16)

    @pl.when(y == 0)
    def _():
        gdt_ref[...] = gd[0:Q]
        send_ref[:, 2 * N :] = gd[Q:]

    @pl.when(y != 0)
    def _():
        gdt_ref[...] = gd[Q:]
        send_ref[:, 2 * N :] = gd[0:Q]


def add_kernel(yv, *refs):
    total = refs[0][...]
    for r in refs[1:-1]:
        total = total + r[...]
    refs[-1][...] = total


def gather_kernel(yv, *refs, side, count):
    out = refs[-1]
    more = refs[2 * count : -1]

    def fill(k):
        at = 0
        for r in refs[k * count : (k + 1) * count]:
            width = r.shape[1]
            total = r[...]
            for m in more:
                total = total + m[:, at : at + width]
            out[:, at : at + width] = total
            at += width

    for core in range(2):

        @pl.when(yv[3] == core)
        def _():
            fill(1 - core if side else core)


def join_kernel(yv, first, second, out):
    out[0] = first[...]
    out[1] = second[...]


def spread(yv, own, got, dst):
    width = own[0].shape[1]
    for k in range(2):

        @pl.when(yv[0] == k)
        def _():
            for g in range(2):
                at = (k * 2 + g) * width
                dst[:, at : at + width] = own[g][...].astype(F32)
                at = ((1 - k) * 2 + g) * width
                dst[:, at : at + width] = got[g].astype(F32)


def rim_kernel(
    yv, next0, next_e, next_o, w, b0, b1, c0, c1, got0, got1, gdt_own, gx,
    gx_ref, gb_ref, gc_ref, gdt_ref, mark, both, full,
):
    mark[...] = jnp.zeros(mark.shape, F32)
    lane = lax.broadcasted_iota(jnp.int32, gdt_own.shape, 1)
    low = lane < gdt_own.shape[1] // 2
    own, got = gdt_own[...].astype(F32), got1[:, 2 * N :].astype(F32)

    @pl.when(yv[0] == 0)
    def _():
        gdt_ref[...] = jnp.where(low, own, got).astype(BF16)

    @pl.when(yv[0] != 0)
    def _():
        gdt_ref[...] = jnp.where(low, got, own).astype(BF16)

    spread(yv, (b0, b1), [r[:, 0:N] for r in (got0, got1)], full.at[0])
    spread(yv, (c0, c1), [r[:, N : 2 * N] for r in (got0, got1)], full.at[1])
    gb_ref[...] = full[0].astype(BF16)
    gc_ref[...] = full[1].astype(BF16)
    rows = slice(Q - 16, Q)
    both[0] = next0[...]

    @pl.when(yv[2] == 0)
    def _():
        both[1] = next_e[...]

    @pl.when(yv[2] != 0)
    def _():
        both[1] = next_o[...]

    step = next0.shape[1]
    blocks = gx.shape[1] // 2 // step
    keep = jnp.where((yv[0] == 0) | (yv[4] == 0), 0.0, 1.0)

    def add(src, dst, lo, half, block, at, width, to):
        h = [keep * both[half, r * (blocks + 1) + block : r * (blocks + 1) + block + 1, at : at + width] for r in range(3)]
        k = w[:, lo : lo + width]
        more = jnp.concatenate(
            [
                jnp.zeros((13, width), F32),
                k[0:1] * h[0],
                k[0:1] * h[1] + k[1:2] * h[0],
                k[0:1] * h[2] + k[1:2] * h[1] + k[2:3] * h[0],
            ],
            axis=0,
        )
        dst[:, to : to + width] = (src[:, to : to + width].astype(F32) + more).astype(BF16)

    for half in range(2):
        for i in range(blocks):
            at = (half * blocks + i) * step
            add(gx, gx_ref, at, half, i, 0, step, at)
        for i, (src, dst) in enumerate(((full.at[0, rows], gb_ref.at[rows]), (full.at[1, rows], gc_ref.at[rows]))):
            to = half * step // 2
            add(src, dst, (2 * blocks + i) * step + to, half, blocks, i * step // 2, step // 2, to)


def sums_kernel(yv, mine, theirs, gw_ref, gb_ref, gh_ref, both, *, wide, heads):
    width = mine.shape[2]

    @pl.when(yv[3] == 0)
    def _():
        both[:, :, 0:width] = mine[...]
        both[:, :, width:] = theirs[...]

    @pl.when(yv[3] != 0)
    def _():
        both[:, :, 0:width] = theirs[...]
        both[:, :, width:] = mine[...]

    step = width - wide // 2

    def fill(order):
        for k in range(2):
            v = both[order[k]]
            for i in range(2):
                to, at = k * wide + i * (wide // 2), i * width + step
                gw_ref[:, to : to + wide // 2] = v[0:4, at : at + wide // 2]
                gb_ref[:, to : to + wide // 2] = v[4:5, at : at + wide // 2]
            for i in range(2):
                for g in range(2):
                    to = 2 * wide + i * 4 * N + (2 * k + g) * N
                    gw_ref[:, to : to + N] = v[0:4, g * width + i * N : g * width + (i + 1) * N]
                    gb_ref[:, to : to + N] = v[4:5, g * width + i * N : g * width + (i + 1) * N]
        at = width + 2 * N
        values = jnp.concatenate(
            [both[order[0]][:, at : at + heads], both[order[1]][:, at : at + heads]], axis=1
        )
        per_dev = gh_ref.shape[1]
        row = lax.broadcasted_iota(jnp.int32, (2 * heads, per_dev), 0)
        col = lax.broadcasted_iota(jnp.int32, (2 * heads, per_dev), 1)
        pick = jnp.where(row == col + yv[5] * per_dev, 1.0, 0.0).astype(BF16)
        hi = values.astype(BF16)
        rest = values - hi.astype(F32)
        mid = rest.astype(BF16)
        low = (rest - mid.astype(F32)).astype(BF16)
        gh_ref[...] = (dot(hi, pick) + dot(mid, pick) + dot(low, pick))[0:3]

    @pl.when(yv[0] == 0)
    def _():
        fill((0, 1))

    @pl.when(yv[0] != 0)
    def _():
        fill((1, 0))


def whole(shape):
    return pl.BlockSpec(shape, lambda *_: (0,) * len(shape))


def shape_of(*dims, dtype=F32):
    return jax.ShapeDtypeStruct(dims, dtype)


def call(kernel, yv, ins, outs, scratch, micros, nbytes, keep=(), after=(), hbm=()):
    count = len(ins)
    extra = len(keep) + len(after)

    def run(yr, *refs):
        kernel(yr, *refs[:count], *refs[count + extra :])

    near = pl.BlockSpec(memory_space=pltpu.MemorySpace.VMEM)
    anywhere = pl.BlockSpec(memory_space=pl.ANY)
    ins = [i if isinstance(i, tuple) else (i, near) for i in ins]
    return pl.pallas_call(
        run,
        out_shape=outs,
        in_specs=[pl.BlockSpec(memory_space=pltpu.MemorySpace.SMEM)]
        + [i[1] for i in ins]
        + [anywhere if k in hbm else near for k in range(len(keep))]
        + [anywhere] * len(after),
        out_specs=[anywhere if k in hbm else near for k in range(len(outs))],
        scratch_shapes=scratch,
        compiler_params=params(),
        cost_estimate=cost(micros, nbytes),
        input_output_aliases={1 + count + k: k for k in range(len(keep))},
    )(yv, *[i[0] for i in ins], *keep, *after)


def per_device(
    ssm_input, b_input, c_input, dt_input, conv_weight, conv_bias, a_log, dt_bias, skip_gain, grad_out
):
    x_rows, b_rows, c_rows = ssm_input[0], b_input[0], c_input[0]
    dt_rows, dy_rows = dt_input[0], grad_out[0]
    devices = lax.axis_size("sp")
    dp_size = lax.axis_size("dp")
    spots = devices // 2
    me = lax.axis_index("sp")
    y = lax.rem(me, 2)
    z = me // 2
    core = lax.rem(lax.axis_index("dp"), 2)
    yv = jnp.stack([y, z, lax.rem(z, 2), core, spots - 1 - z, me]).astype(jnp.int32)
    xw = x_rows.shape[1] // 2
    bw = b_rows.shape[1] // 2
    hl = dt_rows.shape[1] // 2
    chunks = 4
    cw = xw // chunks
    subs = cw // SUB
    groups = bw // N
    per_group = chunks // groups
    two = 2 * Q
    piece = 2 * N + 2 * hl
    base = groups * piece
    bands = base // SUB
    bias = conv_bias[None]

    def pairs(fn, n=devices):
        return [(i, fn(i)) for i in range(n) if fn(i) is not None and 0 <= fn(i) < n]

    swap = pairs(lambda i: i ^ 1)

    def joint(v, fn):
        moves = []
        for d in range(dp_size):
            for i in range(devices):
                to = fn(i)
                if to is None or not 0 <= to < devices:
                    moves.append((d * devices + i, (d ^ 1) * devices + i))
                else:
                    moves.append((d * devices + i, d * devices + to))
        return lax.ppermute(v, ("dp", "sp"), moves)

    def slant(i):
        return i + 1 if i % 2 else i - 1

    def evens(i):
        return i ^ 2

    def odds(i):
        return ((i + 2) ^ 2) - 2 if 2 <= i < devices - 2 else None

    in_hbm = pl.BlockSpec(memory_space=pltpu.MemorySpace.HBM)
    anywhere = pl.BlockSpec(memory_space=pl.ANY)
    msg, rim_out = call(
        pack_small_kernel, yv, [(x_rows, in_hbm), b_rows, c_rows, dt_rows],
        [shape_of(Q, 2 * bw + 2 * hl, dtype=BF16), shape_of(32, 2 * bw, dtype=BF16)],
        [
            pltpu.VMEM((16, 2 * xw), BF16), pltpu.VMEM((16, 2 * bw), BF16),
            pltpu.VMEM((16, 2 * bw), BF16), pltpu.SemaphoreType.DMA((3,)), pltpu.SemaphoreType.DMA((3,)),
        ],
        1, 1 << 20, hbm=(0,),
    )
    rec_bc = lax.ppermute(msg, "sp", swap)
    (rim_out,) = call(
        gate_kernel, yv, [rim_out], [shape_of(32, 2 * bw, dtype=BF16)], [], 1, 1 << 10, after=[rec_bc]
    )
    rim = joint(rim_out, slant)
    rim_e = joint(rim_out, evens)
    rim_o = joint(rim_out, odds)
    rec = []

    def send_chunk(c, after):
        def kernel(*refs):
            pack_kernel(*refs, chunk=c, chunks=chunks)

        (out,) = call(
            kernel, yv, [x_rows, dy_rows], [shape_of(2, Q, cw, dtype=BF16)],
            [pltpu.SemaphoreType.DMA((2,))], 1, 1 << 20, after=after, hbm=(0,),
        )
        rec.append(lax.ppermute(out, "sp", swap))

    send_chunk(0, [msg])

    par = lax.dynamic_slice_in_dim(
        jnp.concatenate([jnp.stack([a_log, dt_bias, skip_gain]), jnp.zeros((5, 2 * hl), F32)], 0),
        y * hl, hl, 1,
    )
    nq = hl // 4
    exp2, seg, halo, bcc, ccc, bct, cct, slopes, fe, rows, qcols, rowt, st = call(
        setup_whole, yv,
        [b_rows, c_rows, dt_rows, rec_bc, rim, rim_e, rim_o, conv_weight, bias, par],
        [
            shape_of(2 * hl, xw, dtype=BF16), shape_of(xw, hl, dtype=BF16), shape_of(8, xw + 2 * bw), shape_of(two, bw, dtype=BF16), shape_of(two, bw, dtype=BF16),
            shape_of(bw, two, dtype=BF16), shape_of(bw, two, dtype=BF16), shape_of(2, two, bw),
            shape_of(2, two, 2 * hl, dtype=BF16), shape_of(8, xw), shape_of(nq, two, 8),
            shape_of(nq, 8, two), shape_of(two, 2 * hl),
        ],
        [
            pltpu.VMEM((two + 8, bw), F32), pltpu.VMEM((two, hl), F32),
            pltpu.VMEM((2 * hl, two), F32), pltpu.VMEM((16, rim.shape[1]), F32),
        ],
        4, 4 << 20,
    )
    send_chunk(1, [rec_bc])
    states = []
    xcs, dyos, sls = [], [], []
    long = pltpu.VMEM((two + 8, SUB), F32)

    def state(c, after):
        nonlocal states
        big = shape_of(chunks, N, cw, dtype=BF16)
        tall = shape_of(two, cw, dtype=BF16)

        def kernel(*refs):
            state_chunk(*refs, chunk=c, per_group=per_group)

        t, u, xc, dyo, sl = call(
            kernel, yv,
            [x_rows, dy_rows, rec[c], halo, conv_weight, bias, bct, cct, fe, exp2, rows],
            [big, big, tall, tall, tall],
            [long, pltpu.VMEM((2, N, cw), BF16), pltpu.SemaphoreType.DMA((2,))], 3, 4 << 20,
            keep=states, after=after, hbm=(0, 1),
        )
        states = [t, u]
        xcs.append(xc)
        dyos.append(dyo)
        sls.append(sl)
        return xc

    yis, dxis, dcbs = [], [], []

    def within(c, after):
        def kernel(*refs):
            within_chunk(*refs, chunk=c, per_group=per_group)

        yi, dxi, dcb = call(
            kernel, yv, [xcs[c], dyos[c], qcols, rowt, bcc, ccc],
            [shape_of(two, cw), shape_of(two, cw), shape_of(2, Q, Q)],
            [pltpu.VMEM((4, Q, Q), F32)], 3, 4 << 20, after=after,
        )
        yis.append(yi)
        dxis.append(dxi)
        dcbs.append(dcb)
        return dcb

    finals = []
    sums = []
    reds, edges = [], []
    got_x = []

    def across(c, ents, leas, after):
        nonlocal finals
        full = shape_of(Q, 2 * xw, dtype=BF16)
        strip = shape_of(8, cw)

        def kernel(*refs):
            across_chunk(*refs, chunk=c, chunks=chunks, per_group=per_group)

        out = call(
            kernel, yv,
            [
                x_rows, rec[c], halo, conv_weight, xcs[c], dyos[c], sls[c], yis[c], dxis[c],
                bcc, ccc, fe, exp2, seg, rows,
            ] + [(v, anywhere) for v in ents + leas],
            [
                full, full, strip, strip, shape_of(2, Q, cw, dtype=BF16), shape_of(two, N),
                shape_of(two, N), shape_of(2, two, hl), shape_of(8, cw), shape_of(Q, Q),
            ],
            [
                long, long, pltpu.VMEM((2, two, cw), BF16), pltpu.VMEM((N, cw), BF16),
                pltpu.VMEM((N, cw), BF16), pltpu.VMEM((2, Q, Q), BF16), pltpu.SemaphoreType.DMA((2 * halves_,)), pltpu.SemaphoreType.DMA((3,)),
            ],
            6, 6 << 20, keep=finals, after=after, hbm=(0, 1),
        )
        finals = list(out[:2])
        reds.append(out[2])
        edges.append(out[3])
        sums.append(out[5:])
        got_x.append(lax.ppermute(out[4], "sp", swap))
        return out[8]

    def unpack(c, after):
        full = shape_of(Q, 2 * xw, dtype=BF16)

        def kernel(*refs):
            unpack_kernel(*refs, chunk=c, chunks=chunks)

        *finals[:2], mark = call(
            kernel, yv, [(got_x[c], anywhere)], [full, full, shape_of(8, 128)],
            [pltpu.SemaphoreType.DMA((2,))], 1, 1 << 20, keep=finals[:2], after=after, hbm=(0, 1),
        )
        return mark

    grads_bc = []
    group_reds, group_edges = [], []

    def finish(g, last, after):
        own = shape_of(Q, N, dtype=BF16)
        strip = shape_of(8, piece)
        ins = [b_rows, c_rows, rec_bc, halo, conv_weight, slopes, bcc, ccc]
        for c in range(g * per_group, (g + 1) * per_group):
            ins += [sums[c][0], sums[c][1], dcbs[c], sums[c][4]]
        outs = [strip, strip, own, own, shape_of(Q, piece if last else 2 * N, dtype=BF16)]
        narrow = pltpu.VMEM((two + 8, N), F32)
        scratch = [narrow, narrow, pltpu.VMEM((2, two, N), F32)]
        if last:
            ins += [st, par, seg, group_edges[0]] + [v[2] for v in sums] + [v[3] for v in sums] + edges
            outs += [shape_of(Q, 2 * hl, dtype=BF16), shape_of(16, cw)]
            scratch.append(pltpu.VMEM((two, 2 * hl), BF16))
        out = call(
            finish_last_kernel if last else finish_kernel, yv, ins, outs, scratch, 3, 4 << 20, after=after
        )
        group_reds.append(out[0])
        group_edges.append(out[1])
        grads_bc.append(out[2:4])
        return lax.ppermute(out[4], "sp", swap), out[4:]

    halves_ = 2
    part = cw // halves_
    zero = jnp.zeros((N, part), BF16)
    ins_e = [[zero] for _ in range(halves_)]
    ins_o = [[zero] for _ in range(halves_)]
    steps = chunks + spots - 2
    state(0, [])
    got_bc = []
    waits = []
    for t in range(steps + 1):
        for i in range(halves_):
            token = []
            if t < steps:
                moving = shape_of(N, part, dtype=BF16)

                def kernel(*refs, step=t, lane=i):
                    hop_kernel(*refs, step=step, part=lane)

                out_e, out_o = call(
                    kernel, yv, [ins_e[i][-1], ins_o[i][-1], states[0], states[1], rows],
                    [moving, moving], [], 1, 3 << 20, after=waits,
                )
                token = [out_e]
                ins_e[i].append(joint(out_e, evens))
                ins_o[i].append(joint(out_o, odds))
            if t == 0 and i == 0:
                send_chunk(2, token)
            waits = []
            if i == 0 and t < chunks - 1:
                waits.append(within(t, token))
            if i == 1 and t + 1 < chunks:
                waits.append(state(t + 1, token))
                if t + 3 < chunks:
                    send_chunk(t + 3, [rec[t + 1]])
            c = t + 1 - spots
            if i == 0 and 0 <= c < chunks:
                if c == chunks - 1:
                    token = []
                ents, leas = [], []
                for k in range(1, spots):
                    for h in range(halves_):
                        ents.append((ins_o if k % 2 == 0 else ins_e)[h][c + k])
                        leas.append((ins_o if (spots - 1 - k) % 2 else ins_e)[h][c + k])
                waits.append(across(c, ents, leas, token))
            if i == 1 and c == 0:
                waits.append(within(chunks - 1, token))
            if i == 1 and c == chunks - 2:
                mark = unpack(0, token)
                got, tok = finish(0, False, token)
                got_bc.append(got)
                waits += [tok[0], mark]
    got, (_, gdt_own, next_rows) = finish(1, True, [])
    got_bc.append(got)

    hw = (base + xw) // 2
    slab = shape_of(8, hw)

    def add(items, after=()):
        (out,) = call(add_kernel, yv, items, [slab], [], 1, 1 << 20, after=after)
        return out

    per_side = chunks // 2
    pieces = []
    for k in range(2):
        pieces += [group_reds[k]] + reds[k * per_side : (k + 1) * per_side]

    def gather(side, more):
        def kernel(*refs):
            gather_kernel(*refs, side=side, count=1 + per_side)

        (out,) = call(kernel, yv, pieces + more, [slab], [], 1, 1 << 20)
        return out

    theirs = gather(True, [])
    mine = gather(False, [lax.ppermute(theirs, "dp", pairs(lambda i: i ^ 1, dp_size))])
    size = 2
    while size < dp_size:
        got = lax.ppermute(mine, "dp", pairs(lambda i: i ^ size, dp_size))
        marks = []
        if size == 2:
            marks = [unpack(1, [mine]), unpack(2, [mine])]
        mine = add([mine, got], marks)
        size *= 2
    size = 2
    while size < devices:
        ways = 4 if size * 4 <= devices else 2
        got = [lax.ppermute(mine, "sp", pairs(lambda i: i ^ (size * k))) for k in range(1, ways)]
        size *= ways
        mine = add([mine] + got)
    unpack(3, [mine])
    y_all, gx_all = finals[:2]
    next0 = joint(next_rows, slant)
    next_e = joint(next_rows, evens)
    next_o = joint(next_rows, odds)
    last = pl.BlockSpec((16, 2 * xw), lambda j, yr: (Q // 16 - 1, 0))
    small = [next0, next_e, next_o, conv_weight] + [grads_bc[g][i] for i in range(2) for g in range(2)]
    small += [got_bc[0], got_bc[1], gdt_own]
    full = shape_of(Q, 2 * bw, dtype=BF16)
    grad_x, grad_b, grad_c, gdt, rim_mark = pl.pallas_call(
        rim_kernel,
        out_shape=[shape_of(Q, 2 * xw, dtype=BF16), full, full, shape_of(Q, 2 * hl, dtype=BF16), shape_of(8, 128)],
        grid_spec=pltpu.PrefetchScalarGridSpec(
            num_scalar_prefetch=1,
            grid=(1,),
            in_specs=[whole(v.shape) for v in small] + [last],
            out_specs=[last, whole(full.shape), whole(full.shape), whole((Q, 2 * hl)), whole((8, 128))],
            scratch_shapes=[pltpu.VMEM((2, 16, cw), F32), pltpu.VMEM((2, Q, 2 * bw), F32)],
        ),
        compiler_params=params(),
        cost_estimate=cost(1, 1 << 20),
        input_output_aliases={1 + len(small): 0},
    )(yv, *small, gx_all)

    got_y = lax.ppermute(mine, "sp", swap)

    (mine,) = call(
        join_kernel, yv, [mine, got_y], [shape_of(2, 8, hw)], [], 1, 1 << 20, after=[rim_mark]
    )
    theirs = lax.ppermute(mine, "dp", pairs(lambda i: i ^ 1, dp_size))
    per_dev = 2 * hl // devices

    def summed(*refs):
        sums_kernel(*refs, wide=xw, heads=hl)

    gw, gbias, gheads = pl.pallas_call(
        lambda yr, a, b, unused, *refs: summed(yr, a, b, *refs),
        out_shape=[
            shape_of(4, bias.shape[1]), shape_of(1, bias.shape[1]), shape_of(3, per_dev),
        ],
        grid_spec=pltpu.PrefetchScalarGridSpec(
            num_scalar_prefetch=1,
            grid=(1,),
            in_specs=[whole(mine.shape), whole(theirs.shape), anywhere],
            out_specs=[
                whole((4, bias.shape[1])), whole((1, bias.shape[1])), whole((3, per_dev)),
            ],
            scratch_shapes=[pltpu.VMEM((2, 8, base + xw), F32)],
        ),
        compiler_params=params(),
        cost_estimate=cost(1, 1 << 20),
    )(yv, mine, theirs, rim_mark)
    return (
        y_all[None], grad_x[None], grad_b[None], grad_c[None], gdt[None], gw, gbias[0], gheads,
    )


def solution(mesh):
    rows = P("dp", "sp", None)
    in_specs = (rows, rows, rows, rows, P(), P(), P(), P(), P(), rows)
    out_specs = (rows, rows, rows, rows, rows, P(), P(), P(None, "sp"))
    return jax.shard_map(
        per_device, mesh=mesh, in_specs=in_specs, out_specs=out_specs, check_vma=False
    )
```
